32 devices in a mesh: dp: 8 (over y, x, core), tensor: 4 (over z).
Axes of the slice: x: 2, y: 2, z: 4, core: 2. Of those that a mesh axis runs over, the one named last changes fastest.
Arguments:
- clips: bfloat16 [16, 1568, 1024], P('dp', 'tensor'), may hold values from -6 to 6
- w_qkv: bfloat16 [3, 1024, 1024], P(None, 'dp', 'tensor'), may hold values from -0.1875 to 0.1875
- w_out: bfloat16 [1024, 1024], P('tensor', 'dp'), may hold values from -1.25 to 1.25
- w_up: bfloat16 [1024, 4096], P('dp', 'tensor'), may hold values from -0.1875 to 0.1875
- w_down: bfloat16 [4096, 1024], P('tensor', 'dp'), may hold values from -0.09375 to 0.09375
- norm_gain: bfloat16 [2, 1024], P(None, 'dp'), may hold values from 0.5 to 1.5
- shifts: bfloat16 [4, 1024], P(None, 'dp'), may hold values from -3 to 3
- bias_qv: bfloat16 [2, 1024], P(None, ('tensor', 'dp')), may hold values from -3 to 3
- up_bias: bfloat16 [4096], P(('tensor', 'dp')), may hold values from -3 to 3
- teacher: bfloat16 [16, 1568, 1024], P('dp', 'tensor'), may hold values from -6 to 6
Outputs:
- out: bfloat16 [16, 1568, 1024], P('dp', 'tensor')
- grad_in: bfloat16 [16, 1568, 1024], P('dp', 'tensor')
- grad_qkv: float32 [3, 1024, 1024], P(None, 'dp', 'tensor')
- grad_out: float32 [1024, 1024], P('tensor', 'dp')
- grad_up: float32 [1024, 4096], P('dp', 'tensor')
- grad_down: float32 [4096, 1024], P('tensor', 'dp')
- grad_gain: float32 [2, 1024], P(None, ('dp', 'tensor'))
- grad_shift: float32 [4, 1024], P(None, ('dp', 'tensor'))
- grad_bias_qv: float32 [2, 1024], P(None, ('tensor', 'dp'))
- grad_up_bias: float32 [4096], P(('tensor', 'dp'))
The draws below stay inside these ranges and needn't reach their ends.
All inputs are finite; a program needn't handle non-finite values.
Results may differ from the reference program's by a relative error of at most 0.005.
The reference program's roundings to bfloat16 on the way count: a program that leaves them out, or rounds other values in their place, can miss the bound.
Values may be sent and summed in bfloat16 or wider, within the bound.
No kernel may reach another device: no remote copies, remote signals or barrier semaphores. Data moves between devices by JAX's collectives and lax.ppermute only.
A program may use at most 320 MiB of HBM per device.

```python
import jax
import jax.numpy as jnp
from jax import lax

D = 1024
HEADS = 16
HEAD_DIM = 64
FF = 4096
SEQ = 1568
CLIPS = 16


def levels(stream_key, dims, shards, least, largest):
    def one(dim, parts):
        draws = jax.random.uniform(jax.random.fold_in(jax.random.fold_in(stream_key, 6), dim), (parts,), jnp.float32, least / len(shards), largest / len(shards))
        return jnp.repeat(jnp.exp(draws), dims[dim] // parts).reshape((-1,) + (1,) * (len(dims) - dim - 1))

    level = one(*shards[0])
    for cut in shards[1:]:
        level = level * one(*cut)
    return level


def normal_values(stream_key, extent, scale, bound, split=(), held_as=jnp.bfloat16):
    drawn = scale * jax.random.normal(stream_key, extent, jnp.float32)
    if split:
        drawn = drawn * levels(stream_key, extent, split, -0.22, 0.18)
    return jnp.clip(drawn, -bound, bound).astype(held_as)


def setup_inputs(seed: int = 0) -> dict:
    splits = jax.random.split(jax.random.key(seed), 11)
    return {
        "clips": normal_values(splits[0], (CLIPS, SEQ, D), 1.0, 6.0, ((0, 8), (1, 4))),
        "w_qkv": normal_values(splits[1], (3, D, D), D ** -0.5, 0.1875, ((1, 8), (2, 4))),
        "w_out": normal_values(splits[2], (D, D), (D // 40) ** -0.5, 1.25, ((0, 4), (1, 8))),
        "w_up": normal_values(splits[3], (D, FF), D ** -0.5, 0.1875, ((0, 8), (1, 4))),
        "w_down": normal_values(splits[4], (FF, D), FF ** -0.5, 0.09375, ((0, 4), (1, 8))),
        "norm_gain": jnp.clip(1.0 + 0.1 * jax.random.normal(splits[5], (2, D), jnp.float32), 0.5, 1.5).astype(jnp.bfloat16),
        "shifts": normal_values(splits[6], (4, D), 0.5, 3.0, ((1, 8),)),
        "bias_qv": normal_values(splits[7], (2, D), 0.5, 3.0, ((1, 32),)),
        "up_bias": normal_values(splits[8], (FF,), 0.5, 3.0, ((0, 32),)),
        "teacher": normal_values(splits[9], (CLIPS, SEQ, D), 1.0, 6.0, ((0, 8), (1, 4))),
    }


EPS = 1e-05
HIGH = lax.Precision.HIGHEST

@jax.custom_vjp
def low(v):
    return lax.optimization_barrier(v.astype(jnp.bfloat16)).astype(jnp.float32)

@jax.custom_vjp
def low_back(v):
    return v

def low_keep(v):
    return (low(v), None)

def low_pass(kept, grad):
    return (grad,)

def back_keep(v):
    return (v, None)

def back_low(kept, grad):
    return (low(grad),)
low.defvjp(low_keep, low_pass)
low_back.defvjp(back_keep, back_low)

def layer_norm(value, gain, shift):
    mean = lax.optimization_barrier(jnp.mean(value, -1, keepdims=True))
    centred = value - mean
    spread = lax.optimization_barrier(jnp.mean(centred * centred, -1, keepdims=True))
    return centred * lax.rsqrt(spread + EPS) * gain + shift

def product(left, right):
    return jnp.dot(left, right, precision=HIGH)

def head_attend(query, keys, values):
    scores = low_back(jnp.dot(query, keys.T, precision=HIGH) * HEAD_DIM ** (-0.5))
    top = lax.optimization_barrier(jnp.max(scores, -1, keepdims=True))
    expd = jnp.exp(scores - top)
    prob = expd / lax.optimization_barrier(jnp.sum(expd, -1, keepdims=True))
    return jnp.dot(low(prob), values, precision=HIGH)

def split_heads(value):
    return value.reshape(value.shape[0], HEADS, HEAD_DIM).transpose(1, 0, 2)

def forward(inputs, w_qkv, w_out, w_up, w_down, norm_gain, shifts, bias_qv, up_bias):
    length = inputs.shape[0]
    first = low(layer_norm(inputs, norm_gain[0], shifts[0]))
    query = low(low_back(product(first, w_qkv[0]) + bias_qv[0]))
    keys = low(low_back(product(first, w_qkv[1])))
    values = low(low_back(product(first, w_qkv[2]) + bias_qv[1]))
    attended = lax.map(jax.checkpoint(lambda item: head_attend(item[0], item[1], item[2])), (split_heads(query), split_heads(keys), split_heads(values)))
    mixed = low(low_back(attended.transpose(1, 0, 2).reshape(length, HEADS * HEAD_DIM)))
    hidden = inputs + low_back(product(mixed, w_out)) + shifts[2]
    second = low(layer_norm(hidden, norm_gain[1], shifts[1]))
    pre = low_back(product(second, w_up) + up_bias)
    active = low(jax.nn.gelu(pre, approximate=False))
    return hidden + low_back(product(active, w_down)) + shifts[3]

def reference(clips, w_qkv, w_out, w_up, w_down, norm_gain, shifts, bias_qv, up_bias, teacher):
    params = tuple((p.astype(jnp.float32) for p in (w_qkv, w_out, w_up, w_down, norm_gain, shifts, bias_qv, up_bias)))

    def per_clip(acc, item):
        state, target = item

        def loss_of(value, *weights):
            result = forward(value, *weights)
            diff = result - target
            return (0.5 * jnp.sum(diff * diff), result)
        loss, back, result = jax.vjp(loss_of, state, *params, has_aux=True)
        grads = back(jnp.ones_like(loss))
        acc = tuple((a + g for a, g in zip(acc, grads[1:])))
        return (acc, (result.astype(jnp.bfloat16), grads[0].astype(jnp.bfloat16)))
    init = tuple((jnp.zeros_like(p) for p in params))
    acc, (outs, grad_in) = lax.scan(per_clip, init, (clips.astype(jnp.float32), teacher.astype(jnp.float32)))
    return (outs, grad_in, acc[0], acc[1], acc[2], acc[3], acc[4], acc[5], acc[6], acc[7])
```

```python
import functools

import jax
import jax.numpy as jnp
from jax import lax
from jax.experimental import pallas as pl
from jax.experimental.pallas import tpu as pltpu
from jax.sharding import Mesh, PartitionSpec as P

HEAD_DIM = 64


EPS = 1e-05


def layer_norm(value, gain, shift):
    mean = jnp.mean(value, -1, keepdims=True)
    centred = value - mean
    spread = jnp.mean(centred * centred, -1, keepdims=True)
    return centred * lax.rsqrt(spread + EPS) * gain + shift


def exact_gelu(value):
    return jax.nn.gelu(value, approximate=False)


def attend_clip(query, keys, values, scale):
    scores = jnp.einsum("qhe,khe->hqk", query, keys, preferred_element_type=jnp.float32) * scale
    top = jnp.max(scores, -1, keepdims=True)
    expd = jnp.exp(scores - top)
    total = jnp.sum(expd, -1, keepdims=True)
    prob = (expd / total).astype(jnp.bfloat16)
    mixed = jnp.einsum("hqk,khe->qhe", prob, values, preferred_element_type=jnp.float32)
    return (mixed.astype(jnp.bfloat16), (top + jnp.log(total))[..., 0])


def attend_back(query, keys, values, d_mixed, logsum, scale):
    scores = jnp.einsum("qhe,khe->hqk", query, keys, preferred_element_type=jnp.float32) * scale
    prob = jnp.exp(scores - logsum[:, :, None])
    d_prob = jnp.einsum("qhe,khe->hqk", d_mixed, values, preferred_element_type=jnp.float32)
    delta = jnp.sum(d_prob * prob, -1, keepdims=True)
    d_scores = (prob * (d_prob - delta)).astype(jnp.bfloat16)
    d_values = jnp.einsum(
        "hqk,qhe->khe", prob.astype(jnp.bfloat16), d_mixed, preferred_element_type=jnp.float32
    )
    d_query = jnp.einsum("hqk,khe->qhe", d_scores, keys, preferred_element_type=jnp.float32) * scale
    d_keys = jnp.einsum("hqk,qhe->khe", d_scores, query, preferred_element_type=jnp.float32) * scale
    return jnp.stack([d_query, d_keys, d_values]).astype(jnp.bfloat16)


def local(clips, w_qkv, w_out, w_up, w_down, norm_gain, shifts, bias_qv, up_bias, teacher):
    wq, wo, wu, wd, gains, shift_all, bias_pair, up_shift = (
        lax.all_gather(w_qkv, "dp", axis=1, tiled=True),
        lax.all_gather(w_out, "dp", axis=1, tiled=True),
        lax.all_gather(w_up, "dp", axis=0, tiled=True),
        lax.all_gather(w_down, "dp", axis=1, tiled=True),
        lax.all_gather(norm_gain, "dp", axis=1, tiled=True),
        lax.all_gather(shifts, "dp", axis=1, tiled=True),
        lax.all_gather(bias_qv, "dp", axis=1, tiled=True),
        lax.all_gather(up_bias, "dp", axis=0, tiled=True),
    )
    gains = gains.astype(jnp.float32)
    shift_all = shift_all.astype(jnp.float32)
    bias_pair = bias_pair.astype(jnp.float32)
    up_shift = up_shift.astype(jnp.float32)
    width = wq.shape[2]
    heads_here = width // HEAD_DIM
    scale = HEAD_DIM ** (-0.5)
    inputs = jnp.swapaxes(clips, 0, 1).astype(jnp.float32)
    first = layer_norm(inputs, gains[0], shift_all[0]).astype(jnp.bfloat16)
    whole_first = lax.all_gather(first, "tensor", axis=0, tiled=True)
    seq = whole_first.shape[0]
    count = whole_first.shape[1]
    projected = jnp.einsum("scd,kde->ksce", whole_first, wq, preferred_element_type=jnp.float32)
    qkv_bias = jnp.stack([bias_pair[0], jnp.zeros_like(bias_pair[0]), bias_pair[1]])
    qkv = (projected + qkv_bias[:, None, None, :]).astype(jnp.bfloat16)

    def heads(value):
        return jnp.swapaxes(value, 0, 1).reshape(count, seq, heads_here, HEAD_DIM)

    query_h, keys_h, values_h = (heads(qkv[0]), heads(qkv[1]), heads(qkv[2]))
    attended, logsum = lax.map(
        lambda item: attend_clip(item[0], item[1], item[2], scale), (query_h, keys_h, values_h)
    )
    mixed = jnp.swapaxes(attended.reshape(count, seq, width), 0, 1)
    piece = mixed
    attn = lax.psum_scatter(
        jnp.einsum("scd,de->sce", piece, wo, preferred_element_type=jnp.float32),
        "tensor",
        scatter_dimension=0,
        tiled=True,
    )
    hidden = inputs + attn + shift_all[2]
    second = layer_norm(hidden, gains[1], shift_all[1]).astype(jnp.bfloat16)
    whole_second = lax.all_gather(second, "tensor", axis=0, tiled=True)
    pre = jnp.einsum("scd,df->scf", whole_second, wu, preferred_element_type=jnp.float32) + up_shift
    active = exact_gelu(pre).astype(jnp.bfloat16)
    piece = active
    ffn = lax.psum_scatter(
        jnp.einsum("scf,fe->sce", piece, wd, preferred_element_type=jnp.float32),
        "tensor",
        scatter_dimension=0,
        tiled=True,
    )
    output = hidden + ffn + shift_all[3]
    d_out = output - jnp.swapaxes(teacher, 0, 1).astype(jnp.float32)
    whole_d_ffn = lax.all_gather(d_out.astype(jnp.bfloat16), "tensor", axis=0, tiled=True)
    d_active = jnp.einsum("sce,fe->scf", whole_d_ffn, wd, preferred_element_type=jnp.float32)
    grad_down = jnp.einsum("scf,sce->fe", active, whole_d_ffn, preferred_element_type=jnp.float32)
    gelu_value, gelu_back = jax.vjp(exact_gelu, pre)
    d_pre = gelu_back(d_active)[0].astype(jnp.bfloat16)
    grad_up_shift = jnp.sum(d_pre.astype(jnp.float32), (0, 1))
    grad_up = jnp.einsum("scd,scf->df", whole_second, d_pre, preferred_element_type=jnp.float32)
    piece = d_pre
    d_second = lax.psum_scatter(
        jnp.einsum("scf,df->scd", piece, wu, preferred_element_type=jnp.float32),
        "tensor",
        scatter_dimension=0,
        tiled=True,
    )
    norm_value, second_back = jax.vjp(layer_norm, hidden, gains[1], shift_all[1])
    d_hidden_norm, grad_gain_two, grad_shift_two = second_back(d_second)
    d_hidden = d_out + d_hidden_norm
    whole_d_attn = lax.all_gather(d_hidden.astype(jnp.bfloat16), "tensor", axis=0, tiled=True)
    d_mixed = jnp.einsum(
        "sce,de->scd", whole_d_attn, wo, preferred_element_type=jnp.float32
    ).astype(jnp.bfloat16)
    grad_out = jnp.einsum("scd,sce->de", mixed, whole_d_attn, preferred_element_type=jnp.float32)
    d_heads = jnp.swapaxes(d_mixed, 0, 1).reshape(count, seq, heads_here, HEAD_DIM)
    d_stacked = lax.map(
        lambda item: attend_back(item[0], item[1], item[2], item[3], item[4], scale),
        (query_h, keys_h, values_h, d_heads, logsum),
    )
    d_qkv = jnp.transpose(d_stacked.reshape(count, 3, seq, width), (1, 2, 0, 3))
    bias_sums = jnp.sum(d_qkv.astype(jnp.float32), (1, 2))
    grad_pair = jnp.stack([bias_sums[0], bias_sums[2]])
    grad_qkv = jnp.einsum("scd,ksce->kde", whole_first, d_qkv, preferred_element_type=jnp.float32)
    piece = d_qkv
    d_first = lax.psum_scatter(
        jnp.einsum("ksce,kde->scd", piece, wq, preferred_element_type=jnp.float32),
        "tensor",
        scatter_dimension=0,
        tiled=True,
    )
    first_value, first_back = jax.vjp(layer_norm, inputs, gains[0], shift_all[0])
    d_in_norm, grad_gain_one, grad_shift_one = first_back(d_first)
    d_inputs = d_hidden + d_in_norm
    sums = (
        lax.psum_scatter(grad_qkv, "dp", scatter_dimension=1, tiled=True),
        lax.psum_scatter(grad_out, "dp", scatter_dimension=1, tiled=True),
        lax.psum_scatter(grad_up, "dp", scatter_dimension=0, tiled=True),
        lax.psum_scatter(grad_down, "dp", scatter_dimension=1, tiled=True),
        lax.psum_scatter(grad_pair, "dp", scatter_dimension=1, tiled=True),
        lax.psum_scatter(grad_up_shift, "dp", scatter_dimension=0, tiled=True),
    )
    grad_gain = jnp.stack([grad_gain_one, grad_gain_two])
    grad_shift = jnp.stack(
        [grad_shift_one, grad_shift_two, jnp.sum(d_hidden, (0, 1)), jnp.sum(d_out, (0, 1))]
    )
    norm_sums = (
        lax.psum_scatter(grad_gain, ("dp", "tensor"), scatter_dimension=1, tiled=True),
        lax.psum_scatter(grad_shift, ("dp", "tensor"), scatter_dimension=1, tiled=True),
    )
    result = jnp.swapaxes(output, 0, 1).astype(jnp.bfloat16)
    grad_in = jnp.swapaxes(d_inputs, 0, 1).astype(jnp.bfloat16)
    return (
        result,
        grad_in,
        sums[0],
        sums[1],
        sums[2],
        sums[3],
        norm_sums[0],
        norm_sums[1],
        sums[4],
        sums[5],
    )


BF = jnp.bfloat16
F32 = jnp.float32
LOG2E = 1.4426950408889634
VMEM_LIMIT = 56 * 2**20
ROW_NN = (((1,), (0,)), ((), ()))
ROW_NT = (((1,), (1,)), ((), ()))
ROW_TN = (((0,), (0,)), ((), ()))


def dot(left, right, dims=ROW_NN):
    return lax.dot_general(left, right, dims, preferred_element_type=F32)


def three_parts(value):
    high = value.astype(BF)
    rest = value - high.astype(F32)
    middle = rest.astype(BF)
    return high, middle, (rest - middle.astype(F32)).astype(BF)


def query_blocks(seq, step):
    blocks = []
    start = 0
    while start < seq:
        used = min(step, seq - start)
        blocks.append((start, -(-used // 128) * 128, used))
        start += used
    return blocks


def pad_columns(value, width):
    extra = width - value.shape[1]
    if extra == 0:
        return value
    return jnp.concatenate([value, jnp.zeros((value.shape[0], extra), value.dtype)], 1)


def attend_kernel(seq, padded, step, q_ref, k_ref, v_ref, o_ref, wide_ref, lse_ref, key_s, query_s, value_s):
    key = k_ref[0]
    key_s[...] = jnp.concatenate([key, key, key, jnp.zeros((HEAD_DIM, seq), BF)], 0).T
    parts = three_parts(pad_columns(q_ref[0].astype(F32) * (LOG2E * HEAD_DIM**-0.5), padded))
    query_s[...] = jnp.concatenate([*parts, jnp.zeros((HEAD_DIM, padded), BF)], 0)
    value_s[0:HEAD_DIM] = v_ref[0]
    value_s[HEAD_DIM : HEAD_DIM + 16] = jnp.ones((16, seq), BF)
    for start, width, used in query_blocks(seq, step):
        scores = dot(key_s[...], query_s[:, start : start + width])
        top = jnp.max(scores, 0, keepdims=True)
        prob = jnp.exp2(scores - top).astype(BF)
        mixed = dot(value_s[...], prob)
        total = mixed[HEAD_DIM : HEAD_DIM + 1]
        result = (mixed[0:HEAD_DIM] * (1.0 / total))[:, :used]
        wide_ref[0, :, start : start + used] = result
        o_ref[0, :, start : start + used] = result.astype(BF)
        lse_ref[0, :, start : start + used] = (top + jnp.log2(total))[:, :used]


def attend(query, keys, values, step):
    heads, _, seq = query.shape
    padded = -(-seq // 128) * 128
    spec = lambda rows: pl.BlockSpec((1, rows, seq), lambda h: (h, 0, 0))
    return pl.pallas_call(
        functools.partial(attend_kernel, seq, padded, step),
        grid=(heads,),
        in_specs=[spec(HEAD_DIM)] * 3,
        out_specs=[spec(HEAD_DIM), spec(HEAD_DIM), spec(1)],
        out_shape=[
            jax.ShapeDtypeStruct((heads, HEAD_DIM, seq), BF),
            jax.ShapeDtypeStruct((heads, HEAD_DIM, seq), F32),
            jax.ShapeDtypeStruct((heads, 1, seq), F32),
        ],
        scratch_shapes=[
            pltpu.VMEM((seq, 4 * HEAD_DIM), BF),
            pltpu.VMEM((4 * HEAD_DIM, padded), BF),
            pltpu.VMEM((HEAD_DIM + 16, seq), BF),
        ],
        compiler_params=pltpu.CompilerParams(vmem_limit_bytes=VMEM_LIMIT),
        cost_estimate=pl.CostEstimate(
            flops=4 * heads * seq * seq * 256, bytes_accessed=12 * heads * seq * HEAD_DIM, transcendentals=heads * seq * seq
        ),
        name="attend",
    )(query, keys, values)


def attend_back_kernel(seq, padded, step, q_ref, k_ref, v_ref, d_ref, lse_ref, delta_ref, out_ref, key_s, query_s, value_s, dmix_s):
    key = k_ref[0]
    ones = jnp.ones((16, seq), BF)
    key_s[...] = jnp.concatenate([key, key, key, ones, jnp.zeros((48, seq), BF)], 0).T
    value_s[...] = jnp.concatenate([v_ref[0], ones, jnp.zeros((48, seq), BF)], 0).T
    query = pad_columns(q_ref[0], padded).astype(F32)
    blank = jnp.zeros((13, padded), BF)
    tail = jnp.zeros((48, padded), BF)
    lse = jnp.concatenate([*three_parts(pad_columns(-lse_ref[0], padded)), blank], 0)
    delta = jnp.concatenate([*three_parts(pad_columns(-delta_ref[0], padded)), blank], 0)
    query_s[...] = jnp.concatenate([*three_parts(query * (LOG2E * HEAD_DIM**-0.5)), lse, tail], 0)
    dmix_s[...] = jnp.concatenate([pad_columns(d_ref[0], padded), delta, tail], 0)
    scaled = (query * HEAD_DIM**-0.5).astype(BF)
    d_keys = jnp.zeros((HEAD_DIM, seq), F32)
    d_values = jnp.zeros((HEAD_DIM, seq), F32)
    for start, width, used in query_blocks(seq, step):
        prob = jnp.exp2(dot(key_s[...], query_s[:, start : start + width]))
        d_scores = (prob * dot(value_s[...], dmix_s[:, start : start + width])).astype(BF)
        d_values = d_values + dot(dmix_s[0:HEAD_DIM, start : start + width], prob.astype(BF), ROW_NT)
        d_keys = d_keys + dot(scaled[:, start : start + width], d_scores, ROW_NT)
        d_query = dot(key, d_scores) * HEAD_DIM**-0.5
        out_ref[0, 0, :, start : start + used] = d_query[:, :used].astype(BF)
    out_ref[1, 0] = d_keys.astype(BF)
    out_ref[2, 0] = d_values.astype(BF)


def attend_backward(query, keys, values, d_mixed, lse, delta, step):
    heads, _, seq = query.shape
    padded = -(-seq // 128) * 128
    spec = lambda rows: pl.BlockSpec((1, rows, seq), lambda h: (h, 0, 0))
    return pl.pallas_call(
        functools.partial(attend_back_kernel, seq, padded, step),
        grid=(heads,),
        in_specs=[spec(HEAD_DIM)] * 4 + [spec(1)] * 2,
        out_specs=pl.BlockSpec((3, 1, HEAD_DIM, seq), lambda h: (0, h, 0, 0)),
        out_shape=jax.ShapeDtypeStruct((3, heads, HEAD_DIM, seq), BF),
        scratch_shapes=[
            pltpu.VMEM((seq, 4 * HEAD_DIM), BF),
            pltpu.VMEM((4 * HEAD_DIM, padded), BF),
            pltpu.VMEM((seq, 2 * HEAD_DIM), BF),
            pltpu.VMEM((2 * HEAD_DIM, padded), BF),
        ],
        compiler_params=pltpu.CompilerParams(vmem_limit_bytes=VMEM_LIMIT),
        cost_estimate=pl.CostEstimate(
            flops=10 * heads * seq * seq * 256, bytes_accessed=14 * heads * seq * HEAD_DIM, transcendentals=heads * seq * seq
        ),
        name="attend_backward",
    )(query, keys, values, d_mixed, lse, delta)


def gelu_pair(value):
    cdf = 0.5 * (1.0 + lax.erf(value * 0.7071067811865476))
    slope = cdf + value * (jnp.exp(-0.5 * value * value) * 0.3989422804014327)
    return value * cdf, slope


def ffn_kernel(x_ref, w_ref, b_ref, out_ref, g_ref, slope_ref):
    width = x_ref.shape[1]
    units = w_ref.shape[4]
    pre = dot(x_ref[...], w_ref[:, 0, 0].reshape(width, units)) + b_ref[0]
    active, slope = gelu_pair(pre)
    active = active.astype(BF)
    g_ref[...] = active
    slope_ref[...] = slope
    part = dot(active, w_ref[:, 0, 1].reshape(width, units), ROW_NT)

    @pl.when(pl.program_id(0) == 0)
    def _():
        out_ref[...] = part

    @pl.when(pl.program_id(0) > 0)
    def _():
        out_ref[...] += part


def ffn_forward(x, weights, bias):
    rows, width = x.shape
    owners, blocks, _, part, units = weights.shape
    whole = pl.BlockSpec((rows, width), lambda t: (0, 0))
    column = pl.BlockSpec((rows, units), lambda t: (0, t))
    return pl.pallas_call(
        ffn_kernel,
        grid=(blocks,),
        in_specs=[
            whole,
            pl.BlockSpec((owners, 1, 2, part, units), lambda t: (0, t, 0, 0, 0)),
            pl.BlockSpec((1, 1, units), lambda t: (t, 0, 0)),
        ],
        out_specs=[whole, column, column],
        out_shape=[
            jax.ShapeDtypeStruct((rows, width), F32),
            jax.ShapeDtypeStruct((rows, blocks * units), BF),
            jax.ShapeDtypeStruct((rows, blocks * units), F32),
        ],
        compiler_params=pltpu.CompilerParams(vmem_limit_bytes=VMEM_LIMIT),
        cost_estimate=pl.CostEstimate(
            flops=4 * rows * width * blocks * units, bytes_accessed=2 * weights.size + 10 * rows * blocks * units, transcendentals=rows * blocks * units
        ),
        name="ffn",
    )(x, weights, bias)


def ffn_back_kernel(d_ref, w_ref, slope_ref, out_ref, dpre_ref, sum_ref):
    width = d_ref.shape[1]
    units = w_ref.shape[4]
    d_active = dot(d_ref[...], w_ref[:, 0, 1].reshape(width, units))
    d_pre = (d_active * slope_ref[...]).astype(BF)
    dpre_ref[...] = d_pre
    sum_ref[0] = jnp.sum(d_pre.astype(F32), 0, keepdims=True)
    part = dot(d_pre, w_ref[:, 0, 0].reshape(width, units), ROW_NT)

    @pl.when(pl.program_id(0) == 0)
    def _():
        out_ref[...] = part

    @pl.when(pl.program_id(0) > 0)
    def _():
        out_ref[...] += part


def ffn_backward(d_out, weights, slope):
    rows, width = d_out.shape
    owners, blocks, _, part, units = weights.shape
    whole = pl.BlockSpec((rows, width), lambda t: (0, 0))
    column = pl.BlockSpec((rows, units), lambda t: (0, t))
    return pl.pallas_call(
        ffn_back_kernel,
        grid=(blocks,),
        in_specs=[
            whole,
            pl.BlockSpec((owners, 1, 2, part, units), lambda t: (0, t, 0, 0, 0)),
            column,
        ],
        out_specs=[whole, column, pl.BlockSpec((1, 1, units), lambda t: (t, 0, 0))],
        out_shape=[
            jax.ShapeDtypeStruct((rows, width), F32),
            jax.ShapeDtypeStruct((rows, blocks * units), BF),
            jax.ShapeDtypeStruct((blocks, 1, units), F32),
        ],
        compiler_params=pltpu.CompilerParams(vmem_limit_bytes=VMEM_LIMIT),
        cost_estimate=pl.CostEstimate(
            flops=4 * rows * width * blocks * units, bytes_accessed=2 * weights.size + 6 * rows * blocks * units, transcendentals=0
        ),
        name="ffn_backward",
    )(d_out, weights, slope)


def ffn_grad_kernel(xa_ref, xb_ref, da_ref, db_ref, pa_ref, pb_ref, ga_ref, gb_ref, up_ref, down_ref, x_s, d_s):
    half = xa_ref.shape[0]

    @pl.when(pl.program_id(0) == 0)
    def _():
        x_s[...] = jnp.concatenate([xa_ref[...], xb_ref[...]], 0).T
        d_s[...] = jnp.concatenate([da_ref[...], db_ref[...]], 0).T

    d_pre = jnp.concatenate([pa_ref[...], pb_ref[...]], 0)
    up_ref[...] = dot(x_s[...], d_pre).astype(BF).reshape(up_ref.shape)
    active = jnp.concatenate([ga_ref[...], gb_ref[...]], 0)
    down_ref[...] = dot(d_s[...], active).astype(BF).reshape(down_ref.shape)


def ffn_grads(xa, xb, da, db, pa, pb, ga, gb, blocks):
    rows, width = xa.shape
    units = pa.shape[1] // blocks
    whole = pl.BlockSpec((rows, width), lambda t: (0, 0))
    column = pl.BlockSpec((rows, units), lambda t: (0, t))
    shape = (2, 2, blocks, width // 4, units)
    out = pl.BlockSpec((2, 2, 1, width // 4, units), lambda t: (0, 0, t, 0, 0))
    return pl.pallas_call(
        ffn_grad_kernel,
        grid=(blocks,),
        in_specs=[whole] * 4 + [column] * 4,
        out_specs=[out, out],
        out_shape=[jax.ShapeDtypeStruct(shape, BF)] * 2,
        scratch_shapes=[pltpu.VMEM((width, 2 * rows), BF)] * 2,
        compiler_params=pltpu.CompilerParams(vmem_limit_bytes=VMEM_LIMIT),
        cost_estimate=pl.CostEstimate(
            flops=8 * rows * width * blocks * units, bytes_accessed=8 * rows * width + 8 * rows * blocks * units + 4 * width * blocks * units, transcendentals=0
        ),
        name="ffn_grads",
    )(xa, xb, da, db, pa, pb, ga, gb)


def swap(value, axis):
    return lax.ppermute(value, axis, [(0, 1), (1, 0)])


def ordered(bit, mine, other, axis):
    return jnp.concatenate([jnp.where(bit == 0, mine, other), jnp.where(bit == 0, other, mine)], axis)


def chain_gather(value, place, size):
    up = [(i, i + 1) for i in range(size - 1)]
    down = [(i + 1, i) for i in range(size - 1)]
    below, above = [value], [value]
    for _ in range(size - 1):
        below.append(lax.ppermute(below[-1], "t", up))
        above.append(lax.ppermute(above[-1], "t", down))
    row = jnp.stack(below[:0:-1] + [value] + above[1:])
    return lax.dynamic_slice_in_dim(row, size - 1 - place, size, 0)


def chain_scatter(value, place, size):
    up = [(i, i + 1) for i in range(size - 1)]
    down = [(i + 1, i) for i in range(size - 1)]
    blank = jnp.zeros_like(value[0])
    row = jnp.concatenate([jnp.stack([blank] * (size - 1)), value, jnp.stack([blank] * (size - 1))])
    at = lambda away: lax.dynamic_index_in_dim(row, size - 1 + place + away, 0, keepdims=False)
    rising, falling = None, None
    for away in range(size - 1, 0, -1):
        lift, drop = at(away), at(-away)
        if rising is not None:
            lift = (lift.astype(F32) + rising.astype(F32)).astype(BF)
            drop = (drop.astype(F32) + falling.astype(F32)).astype(BF)
        rising = lax.ppermute(lift, "t", up)
        falling = lax.ppermute(drop, "t", down)
    return at(0).astype(F32) + rising.astype(F32) + falling.astype(F32)


def halve(value, bit, axis, name):
    mine = lax.dynamic_index_in_dim(value, bit, axis, keepdims=False)
    other = lax.dynamic_index_in_dim(value, 1 - bit, axis, keepdims=False)
    return (mine.astype(F32) + swap(other, name).astype(F32)).astype(BF)


def moments(value):
    mean = jnp.mean(value, -1, keepdims=True)
    centred = value - mean
    scale = lax.rsqrt(jnp.mean(centred * centred, -1, keepdims=True) + EPS)
    return centred, scale


def norm_back(d_value, centred, scale, gain):
    unit = centred * scale
    d_unit = d_value * gain
    grad_in = scale * (d_unit - jnp.mean(d_unit, -1, keepdims=True) - unit * jnp.mean(d_unit * unit, -1, keepdims=True))
    return grad_in, jnp.sum(d_value * unit, 0), jnp.sum(d_value, 0)


def clip_local(clips, w_qkv, w_out, w_up, w_down, norm_gain, shifts, bias_qv, up_bias, teacher):
    y, x, c, t = (lax.axis_index(name) for name in ("y", "x", "c", "t"))
    every = ("y", "x", "c", "t")
    steps = 4
    width = clips.shape[2]
    odd = t % 2

    first_way, second_way = [], []
    for column in range(4):
        for core in range(2):
            for place in range(4):
                source = (column * 2 + core) * 4 + place
                to = (column * 2 + place // 2) * 4 + 2 * core
                first_way.append((source, to + place % 2))
                second_way.append((source, to + 1 - place % 2))
    back = lambda way: [(b, a) for a, b in way]

    def to_chip(value):
        pick = lambda i: lax.dynamic_index_in_dim(value, i, 0, keepdims=False)
        return jnp.concatenate([lax.ppermute(pick(odd), every, first_way), lax.ppermute(pick(1 - odd), every, second_way)])

    def from_chip(value):
        near = lax.ppermute(value[: value.shape[0] // 2], every, back(first_way))
        far = lax.ppermute(value[value.shape[0] // 2 :], every, back(second_way))
        return jnp.stack([jnp.where(odd == 0, near, far), jnp.where(odd == 0, far, near)])

    vectors = jnp.concatenate([norm_gain, shifts, jnp.zeros((2, norm_gain.shape[1]), BF)])
    for bit, name in ((c, "c"), (x, "x"), (y, "y")):
        vectors = ordered(bit, vectors, swap(vectors, name), 1)
    vectors = vectors.astype(F32)
    gains, shift_all = vectors[0:2], vectors[2:6]

    inputs = to_chip(clips)

    dims = w_qkv.shape[1]
    cols = w_out.shape[0] // 2
    attn = jnp.concatenate([jnp.swapaxes(w_qkv, 1, 2), w_out[None]]).reshape(4, 2, cols, dims)
    mine = lax.dynamic_index_in_dim(attn, c, 1, keepdims=False)
    other = lax.dynamic_index_in_dim(attn, 1 - c, 1, keepdims=False)
    mine_attn = mine.reshape(4 * cols, dims)
    other_attn = other.reshape(4 * cols, dims)
    units = w_up.shape[1] // 2
    ff = jnp.stack([w_up, w_down.T]).reshape(2, dims, 2, units)
    mine_ff = lax.dynamic_index_in_dim(ff, c, 2, keepdims=False)
    other_ff = swap(lax.dynamic_index_in_dim(ff, 1 - c, 2, keepdims=False), "c")
    ff_piece = ordered(c, mine_ff, other_ff, 1)
    attn_piece = ordered(c, mine_attn, swap(other_attn, "c"), 1)
    small = jnp.concatenate([bias_qv.reshape(-1), up_bias, jnp.zeros((2 * dims - bias_qv.size - up_bias.size,), BF)])[None]
    small_other = swap(small, "c")
    attn_piece = jnp.concatenate([attn_piece, ordered(c, small, small_other, 0), jnp.zeros((14, 2 * dims), BF)])
    attn_rows = chain_gather(attn_piece, t, steps)
    split = 2 * cols
    part_a, part_b = attn_rows[:, :split], attn_rows[:, split:]
    part_a = ordered(y, part_a, swap(part_a, "y"), 2)
    part_b = ordered(x, part_b, swap(part_b, "x"), 2)
    other_a = swap(part_a, "x")
    other_b = swap(part_b, "y")
    piece = 2 * dims
    part_a = jnp.concatenate(
        [ordered(x, part_a[..., i * piece : (i + 1) * piece], other_a[..., i * piece : (i + 1) * piece], 2) for i in range(2)], 2
    )
    part_b = ordered(y, part_b, other_b, 2)
    arrange = lambda value: jnp.swapaxes(value.reshape(steps, 2, cols, width), 0, 1).reshape(2, steps * cols, width)
    w_qk = arrange(part_a)
    w_vo = arrange(part_b[:, : 2 * cols])
    w_in = jnp.concatenate([w_qk, w_vo[:1]]).reshape(3 * steps * cols, width)
    w_back = w_vo[1]
    biases = part_b[:, 2 * cols : 2 * cols + 2].reshape(steps, 2, 4, piece).astype(F32)
    biases = lax.dynamic_slice_in_dim(jnp.transpose(biases, (0, 2, 1, 3)).reshape(steps, 8, piece), 4 * c, 4, 1)
    lane = bias_qv.shape[1]
    bias_pair = jnp.transpose(biases[..., : 2 * lane].reshape(steps, 4, 2, lane), (2, 0, 1, 3)).reshape(2, steps * cols)
    up_shift = biases[..., 2 * lane : 2 * lane + up_bias.size].reshape(steps, 1, units)

    ff_all = lax.all_gather(ff_piece, ("y", "x", "t"), axis=0, tiled=False).reshape(4, steps, 2, 2 * dims, units)

    inputs = inputs.astype(F32)
    centred_one, scale_one = moments(inputs)
    first = (centred_one * scale_one * gains[0] + shift_all[0]).astype(BF)
    whole_first = jnp.concatenate([first, swap(first, "c")])
    half = first.shape[0]
    seq = 2 * half
    bias_in = jnp.concatenate([bias_pair[0], jnp.zeros_like(bias_pair[0]), bias_pair[1]])
    qkv = (dot(w_in, whole_first, ROW_NT) + bias_in[:, None]).astype(BF)
    heads = steps * cols // HEAD_DIM
    query, keys, values = qkv.reshape(3, heads, HEAD_DIM, seq)
    mixed, mixed_wide, lse = attend(query, keys, values, 1664)
    flat = mixed.reshape(heads * HEAD_DIM, seq)
    attn_other = dot(flat[:, half:], w_back, ROW_TN)
    attn_mine = dot(flat[:, :half], w_back, ROW_TN)
    hidden = inputs + (attn_mine + swap(attn_other, "c")) + shift_all[2]

    centred_two, scale_two = moments(hidden)
    second = (centred_two * scale_two * gains[1] + shift_all[1]).astype(BF)
    second_other = swap(second, "c")
    out_mine, act_mine, slope_mine = ffn_forward(second, ff_all, up_shift)
    out_other, act_other, slope_other = ffn_forward(second_other, ff_all, up_shift)
    output = hidden + (out_mine + swap(out_other, "c")) + shift_all[3]
    d_out = output - to_chip(teacher).astype(F32)
    result = from_chip(output.astype(BF))
    d_ffn = d_out.astype(BF)
    d_ffn_other = swap(d_ffn, "c")
    d_second, d_pre, sum_mine = ffn_backward(d_ffn, ff_all, slope_mine)
    d_second_other, d_pre_other, sum_other = ffn_backward(d_ffn_other, ff_all, slope_other)
    up_sum = (sum_mine + sum_other).reshape(steps, units)
    d_second = d_second + swap(d_second_other, "c")
    grad_up, grad_down = ffn_grads(second, second_other, d_ffn, d_ffn_other, d_pre, d_pre_other, act_mine, act_other, steps)
    grad_up = halve(halve(grad_up, x, 1, "x"), y, 0, "y")
    grad_down = halve(halve(grad_down, y, 0, "y"), x, 0, "x")
    grad_ff = chain_scatter(jnp.stack([grad_up, grad_down], 1), t, steps).reshape(2, 2, dims, units)
    mine = lax.dynamic_index_in_dim(grad_ff, c, 1, keepdims=False)
    other = swap(lax.dynamic_index_in_dim(grad_ff, 1 - c, 1, keepdims=False), "c")
    grad_ff = ordered(c, mine, other, 2)

    d_norm, grad_gain_two, grad_shift_two = norm_back(d_second, centred_two, scale_two, gains[1])
    d_hidden = d_out + d_norm
    d_attn = d_hidden.astype(BF)
    d_attn = jnp.concatenate([d_attn, swap(d_attn, "c")])

    d_mixed = dot(w_back, d_attn, ROW_NT).astype(BF)
    grad_out = dot(flat, d_attn)
    d_heads = d_mixed.reshape(heads, HEAD_DIM, seq)
    delta = jnp.sum(d_heads.astype(F32) * mixed_wide, 1, keepdims=True)
    d_qkv = attend_backward(query, keys, values, d_heads, lse, delta, 256)
    d_flat = d_qkv.reshape(3 * heads * HEAD_DIM, seq)
    d_first_other = dot(d_flat[:, half:], w_in, ROW_TN)
    d_first = dot(d_flat[:, :half], w_in, ROW_TN) + swap(d_first_other, "c")
    grad_in = dot(d_flat, whole_first)
    bias_sums = jnp.sum(d_qkv.astype(F32), 3).reshape(3, steps * cols)
    d_norm, grad_gain_one, grad_shift_one = norm_back(d_first, centred_one, scale_one, gains[0])
    d_inputs = from_chip((d_hidden + d_norm).astype(BF))

    grad_attn = jnp.concatenate([grad_in, grad_out]).astype(BF).reshape(4, steps, cols, 2, 2, piece)
    grad_a = halve(halve(grad_attn[:2], x, 4, "x"), y, 3, "y")
    grad_b = halve(halve(grad_attn[2:], y, 3, "y"), x, 3, "x")
    grad_attn = jnp.swapaxes(jnp.concatenate([grad_a, grad_b]), 0, 1)
    grad_attn = chain_scatter(grad_attn, t, steps).reshape(4, cols, 2, dims)
    mine = lax.dynamic_index_in_dim(grad_attn, c, 2, keepdims=False)
    other = swap(lax.dynamic_index_in_dim(grad_attn, 1 - c, 2, keepdims=False), "c")
    grad_attn = ordered(c, mine, other, 1)

    normed = jnp.stack([grad_gain_one, grad_gain_two, grad_shift_one, grad_shift_two, jnp.sum(d_hidden, 0), jnp.sum(d_out, 0)])
    rows = jnp.swapaxes(normed.reshape(6, 32, width // 32), 0, 1).reshape(32, 6 * (width // 32))
    pair = jnp.transpose(jnp.stack([bias_sums[0], bias_sums[2]]).reshape(2, steps, 4, lane), (2, 1, 0, 3))
    ups = jnp.transpose(up_sum.reshape(steps, 4, up_bias.size), (1, 0, 2))
    mine = jnp.concatenate([pair.reshape(16, 2 * lane), ups.reshape(16, up_bias.size)], 1)
    here = jnp.where((jnp.arange(2) == c)[:, None, None], mine[None], 0.0).reshape(32, mine.shape[1])
    sums = lax.psum_scatter(jnp.concatenate([rows, here], 1), every, scatter_dimension=0, tiled=True)[0]
    thin = width // 32
    vector_sums = sums[: 6 * thin].reshape(6, thin)
    return (
        result,
        d_inputs,
        jnp.swapaxes(grad_attn[:3], 1, 2),
        grad_attn[3],
        grad_ff[0],
        grad_ff[1].T,
        vector_sums[:2],
        vector_sums[2:],
        sums[6 * thin : 6 * thin + 2 * lane].reshape(2, lane),
        sums[6 * thin + 2 * lane :],
    )


def clip_per_chip(mesh):
    fine = Mesh(mesh.devices.reshape(2, 2, 2, 4), ("y", "x", "c", "t"))
    dp = ("y", "x", "c")
    in_specs = (
        P(dp, "t", None),
        P(None, dp, "t"),
        P("t", dp),
        P(dp, "t"),
        P("t", dp),
        P(None, dp),
        P(None, dp),
        P(None, ("t",) + dp),
        P(("t",) + dp),
        P(dp, "t", None),
    )
    out_specs = in_specs[:1] * 2 + in_specs[1:5] + (
        P(None, dp + ("t",)),
        P(None, dp + ("t",)),
        P(None, ("t",) + dp),
        P(("t",) + dp),
    )
    return jax.shard_map(clip_local, mesh=fine, in_specs=in_specs, out_specs=out_specs, check_vma=False)


def solution(mesh):
    if dict(mesh.shape) == {"dp": 8, "tensor": 4}:
        return clip_per_chip(mesh)
    in_specs = (
        P("dp", "tensor", None),
        P(None, "dp", "tensor"),
        P("tensor", "dp"),
        P("dp", "tensor"),
        P("tensor", "dp"),
        P(None, "dp"),
        P(None, "dp"),
        P(None, ("tensor", "dp")),
        P(("tensor", "dp")),
        P("dp", "tensor", None),
    )
    out_specs = (
        P("dp", "tensor", None),
        P("dp", "tensor", None),
        P(None, "dp", "tensor"),
        P("tensor", "dp"),
        P("dp", "tensor"),
        P("tensor", "dp"),
        P(None, ("dp", "tensor")),
        P(None, ("dp", "tensor")),
        P(None, ("tensor", "dp")),
        P(("tensor", "dp")),
    )
    return jax.shard_map(local, mesh=mesh, in_specs=in_specs, out_specs=out_specs, check_vma=False)
```

```python
import functools

import jax
import jax.numpy as jnp
from jax import lax
from jax.experimental import pallas as pl
from jax.experimental.pallas import tpu as pltpu
from jax.sharding import Mesh, PartitionSpec as P

HEAD_DIM = 64


EPS = 1e-05


def layer_norm(value, gain, shift):
    mean = jnp.mean(value, -1, keepdims=True)
    centred = value - mean
    spread = jnp.mean(centred * centred, -1, keepdims=True)
    return centred * lax.rsqrt(spread + EPS) * gain + shift


def exact_gelu(value):
    return jax.nn.gelu(value, approximate=False)


def attend_clip(query, keys, values, scale):
    scores = jnp.einsum("qhe,khe->hqk", query, keys, preferred_element_type=jnp.float32) * scale
    top = jnp.max(scores, -1, keepdims=True)
    expd = jnp.exp(scores - top)
    total = jnp.sum(expd, -1, keepdims=True)
    prob = (expd / total).astype(jnp.bfloat16)
    mixed = jnp.einsum("hqk,khe->qhe", prob, values, preferred_element_type=jnp.float32)
    return (mixed.astype(jnp.bfloat16), (top + jnp.log(total))[..., 0])


def attend_back(query, keys, values, d_mixed, logsum, scale):
    scores = jnp.einsum("qhe,khe->hqk", query, keys, preferred_element_type=jnp.float32) * scale
    prob = jnp.exp(scores - logsum[:, :, None])
    d_prob = jnp.einsum("qhe,khe->hqk", d_mixed, values, preferred_element_type=jnp.float32)
    delta = jnp.sum(d_prob * prob, -1, keepdims=True)
    d_scores = (prob * (d_prob - delta)).astype(jnp.bfloat16)
    d_values = jnp.einsum(
        "hqk,qhe->khe", prob.astype(jnp.bfloat16), d_mixed, preferred_element_type=jnp.float32
    )
    d_query = jnp.einsum("hqk,khe->qhe", d_scores, keys, preferred_element_type=jnp.float32) * scale
    d_keys = jnp.einsum("hqk,qhe->khe", d_scores, query, preferred_element_type=jnp.float32) * scale
    return jnp.stack([d_query, d_keys, d_values]).astype(jnp.bfloat16)


def local(clips, w_qkv, w_out, w_up, w_down, norm_gain, shifts, bias_qv, up_bias, teacher):
    wq, wo, wu, wd, gains, shift_all, bias_pair, up_shift = (
        lax.all_gather(w_qkv, "dp", axis=1, tiled=True),
        lax.all_gather(w_out, "dp", axis=1, tiled=True),
        lax.all_gather(w_up, "dp", axis=0, tiled=True),
        lax.all_gather(w_down, "dp", axis=1, tiled=True),
        lax.all_gather(norm_gain, "dp", axis=1, tiled=True),
        lax.all_gather(shifts, "dp", axis=1, tiled=True),
        lax.all_gather(bias_qv, "dp", axis=1, tiled=True),
        lax.all_gather(up_bias, "dp", axis=0, tiled=True),
    )
    gains = gains.astype(jnp.float32)
    shift_all = shift_all.astype(jnp.float32)
    bias_pair = bias_pair.astype(jnp.float32)
    up_shift = up_shift.astype(jnp.float32)
    width = wq.shape[2]
    heads_here = width // HEAD_DIM
    scale = HEAD_DIM ** (-0.5)
    inputs = jnp.swapaxes(clips, 0, 1).astype(jnp.float32)
    first = layer_norm(inputs, gains[0], shift_all[0]).astype(jnp.bfloat16)
    whole_first = lax.all_gather(first, "tensor", axis=0, tiled=True)
    seq = whole_first.shape[0]
    count = whole_first.shape[1]
    projected = jnp.einsum("scd,kde->ksce", whole_first, wq, preferred_element_type=jnp.float32)
    qkv_bias = jnp.stack([bias_pair[0], jnp.zeros_like(bias_pair[0]), bias_pair[1]])
    qkv = (projected + qkv_bias[:, None, None, :]).astype(jnp.bfloat16)

    def heads(value):
        return jnp.swapaxes(value, 0, 1).reshape(count, seq, heads_here, HEAD_DIM)

    query_h, keys_h, values_h = (heads(qkv[0]), heads(qkv[1]), heads(qkv[2]))
    attended, logsum = lax.map(
        lambda item: attend_clip(item[0], item[1], item[2], scale), (query_h, keys_h, values_h)
    )
    mixed = jnp.swapaxes(attended.reshape(count, seq, width), 0, 1)
    piece = mixed
    attn = lax.psum_scatter(
        jnp.einsum("scd,de->sce", piece, wo, preferred_element_type=jnp.float32),
        "tensor",
        scatter_dimension=0,
        tiled=True,
    )
    hidden = inputs + attn + shift_all[2]
    second = layer_norm(hidden, gains[1], shift_all[1]).astype(jnp.bfloat16)
    whole_second = lax.all_gather(second, "tensor", axis=0, tiled=True)
    pre = jnp.einsum("scd,df->scf", whole_second, wu, preferred_element_type=jnp.float32) + up_shift
    active = exact_gelu(pre).astype(jnp.bfloat16)
    piece = active
    ffn = lax.psum_scatter(
        jnp.einsum("scf,fe->sce", piece, wd, preferred_element_type=jnp.float32),
        "tensor",
        scatter_dimension=0,
        tiled=True,
    )
    output = hidden + ffn + shift_all[3]
    d_out = output - jnp.swapaxes(teacher, 0, 1).astype(jnp.float32)
    whole_d_ffn = lax.all_gather(d_out.astype(jnp.bfloat16), "tensor", axis=0, tiled=True)
    d_active = jnp.einsum("sce,fe->scf", whole_d_ffn, wd, preferred_element_type=jnp.float32)
    grad_down = jnp.einsum("scf,sce->fe", active, whole_d_ffn, preferred_element_type=jnp.float32)
    gelu_value, gelu_back = jax.vjp(exact_gelu, pre)
    d_pre = gelu_back(d_active)[0].astype(jnp.bfloat16)
    grad_up_shift = jnp.sum(d_pre.astype(jnp.float32), (0, 1))
    grad_up = jnp.einsum("scd,scf->df", whole_second, d_pre, preferred_element_type=jnp.float32)
    piece = d_pre
    d_second = lax.psum_scatter(
        jnp.einsum("scf,df->scd", piece, wu, preferred_element_type=jnp.float32),
        "tensor",
        scatter_dimension=0,
        tiled=True,
    )
    norm_value, second_back = jax.vjp(layer_norm, hidden, gains[1], shift_all[1])
    d_hidden_norm, grad_gain_two, grad_shift_two = second_back(d_second)
    d_hidden = d_out + d_hidden_norm
    whole_d_attn = lax.all_gather(d_hidden.astype(jnp.bfloat16), "tensor", axis=0, tiled=True)
    d_mixed = jnp.einsum(
        "sce,de->scd", whole_d_attn, wo, preferred_element_type=jnp.float32
    ).astype(jnp.bfloat16)
    grad_out = jnp.einsum("scd,sce->de", mixed, whole_d_attn, preferred_element_type=jnp.float32)
    d_heads = jnp.swapaxes(d_mixed, 0, 1).reshape(count, seq, heads_here, HEAD_DIM)
    d_stacked = lax.map(
        lambda item: attend_back(item[0], item[1], item[2], item[3], item[4], scale),
        (query_h, keys_h, values_h, d_heads, logsum),
    )
    d_qkv = jnp.transpose(d_stacked.reshape(count, 3, seq, width), (1, 2, 0, 3))
    bias_sums = jnp.sum(d_qkv.astype(jnp.float32), (1, 2))
    grad_pair = jnp.stack([bias_sums[0], bias_sums[2]])
    grad_qkv = jnp.einsum("scd,ksce->kde", whole_first, d_qkv, preferred_element_type=jnp.float32)
    piece = d_qkv
    d_first = lax.psum_scatter(
        jnp.einsum("ksce,kde->scd", piece, wq, preferred_element_type=jnp.float32),
        "tensor",
        scatter_dimension=0,
        tiled=True,
    )
    first_value, first_back = jax.vjp(layer_norm, inputs, gains[0], shift_all[0])
    d_in_norm, grad_gain_one, grad_shift_one = first_back(d_first)
    d_inputs = d_hidden + d_in_norm
    sums = (
        lax.psum_scatter(grad_qkv, "dp", scatter_dimension=1, tiled=True),
        lax.psum_scatter(grad_out, "dp", scatter_dimension=1, tiled=True),
        lax.psum_scatter(grad_up, "dp", scatter_dimension=0, tiled=True),
        lax.psum_scatter(grad_down, "dp", scatter_dimension=1, tiled=True),
        lax.psum_scatter(grad_pair, "dp", scatter_dimension=1, tiled=True),
        lax.psum_scatter(grad_up_shift, "dp", scatter_dimension=0, tiled=True),
    )
    grad_gain = jnp.stack([grad_gain_one, grad_gain_two])
    grad_shift = jnp.stack(
        [grad_shift_one, grad_shift_two, jnp.sum(d_hidden, (0, 1)), jnp.sum(d_out, (0, 1))]
    )
    norm_sums = (
        lax.psum_scatter(grad_gain, ("dp", "tensor"), scatter_dimension=1, tiled=True),
        lax.psum_scatter(grad_shift, ("dp", "tensor"), scatter_dimension=1, tiled=True),
    )
    result = jnp.swapaxes(output, 0, 1).astype(jnp.bfloat16)
    grad_in = jnp.swapaxes(d_inputs, 0, 1).astype(jnp.bfloat16)
    return (
        result,
        grad_in,
        sums[0],
        sums[1],
        sums[2],
        sums[3],
        norm_sums[0],
        norm_sums[1],
        sums[4],
        sums[5],
    )


BF = jnp.bfloat16
F32 = jnp.float32
LOG2E = 1.4426950408889634
VMEM_LIMIT = 56 * 2**20
ROW_NN = (((1,), (0,)), ((), ()))
ROW_NT = (((1,), (1,)), ((), ()))
PAIR = 2


def dot(left, right, dims=ROW_NN):
    return lax.dot_general(left, right, dims, preferred_element_type=F32)


def call(body, grid, in_specs, out_specs, out_shape, args, scratch=(), name=None):
    return pl.pallas_call(
        body,
        grid=grid,
        in_specs=in_specs,
        out_specs=out_specs,
        out_shape=out_shape,
        scratch_shapes=list(scratch),
        compiler_params=pltpu.CompilerParams(vmem_limit_bytes=VMEM_LIMIT),
        cost_estimate=pl.CostEstimate(flops=1000, bytes_accessed=1000, transcendentals=0),
        name=name,
    )(*args)


def shaped(shape, dtype=BF):
    return jax.ShapeDtypeStruct(shape, dtype)


def three_parts(value):
    high = value.astype(BF)
    rest = value - high.astype(F32)
    middle = rest.astype(BF)
    return high, middle, (rest - middle.astype(F32)).astype(BF)


def query_blocks(seq, step):
    blocks = []
    start = 0
    while start < seq:
        used = min(step, seq - start)
        blocks.append((start, -(-used // 128) * 128, used))
        start += used
    return blocks


def pad_columns(value, width):
    extra = width - value.shape[1]
    if extra == 0:
        return value
    return jnp.concatenate([value, jnp.zeros((value.shape[0], extra), value.dtype)], 1)


def place_block(place_ref, step):
    return lax.rem(place_ref[0] + step, 4)


def row_blocks(ref, place, start, stop):
    return jnp.concatenate([ref[owner, place, start:stop] for owner in range(ref.shape[0])], 1)


def key_blocks(ref, place, which):
    return jnp.concatenate([ref[owner, place, which] for owner in range(ref.shape[0])], 1)


def project_kernel(place_ref, xa_ref, xb_ref, qk_ref, v_ref, b_ref, out_ref, t_ref, x_s):
    half = xa_ref.shape[0]
    group = pl.program_id(0)

    @pl.when(group == 0)
    def _():
        x_s[0:half] = xa_ref[...]
        x_s[half:] = xb_ref[...]
        t_ref[...] = x_s[...].T

    cols = v_ref.shape[2]
    places = [place_block(place_ref, PAIR * group + p) for p in range(PAIR)]
    for i in range(3):
        pick = (lambda place: row_blocks(v_ref, place, 0, cols)) if i == 2 else (lambda place: key_blocks(qk_ref, place, i))
        weights = jnp.concatenate([pick(place) for place in places], 0)
        value = dot(weights, x_s[...], ROW_NT) + b_ref[0, i]
        out_ref[0, i] = value.astype(BF).reshape(out_ref.shape[2:])


SCALAR = pl.BlockSpec(memory_space=pltpu.SMEM)


def project(place, xa, xb, w_qk, w_vo, bias):
    half, width = xa.shape
    owners, places, _, cols, part = w_qk.shape
    groups = places // PAIR
    heads = PAIR * cols // HEAD_DIM
    whole = pl.BlockSpec((half, width), lambda g: (0, 0))
    return call(
        project_kernel,
        (groups,),
        [
            SCALAR,
            whole,
            whole,
            pl.BlockSpec((owners, places, 2, cols, part), lambda g: (0, 0, 0, 0, 0)),
            pl.BlockSpec((owners, places, cols, part), lambda g: (0, 0, 0, 0)),
            pl.BlockSpec((1, 3, PAIR * cols, 1), lambda g: (g, 0, 0, 0)),
        ],
        [
            pl.BlockSpec((1, 3, heads, HEAD_DIM, 2 * half), lambda g: (g, 0, 0, 0, 0)),
            pl.BlockSpec((width, 2 * half), lambda g: (0, 0)),
        ],
        [shaped((groups, 3, heads, HEAD_DIM, 2 * half)), shaped((width, 2 * half))],
        (place, xa, xb, w_qk, w_vo, bias),
        [pltpu.VMEM((2 * half, width), BF)],
        name="project",
    )


def attend_kernel(seq, padded, step, q_ref, k_ref, v_ref, o_ref, row_ref, wide_ref, lse_ref, key_s, query_s, value_s, hold_s):
    key = k_ref[0, 0, 0]
    key_s[...] = jnp.concatenate([key, key, key, jnp.zeros((HEAD_DIM, seq), BF)], 0).T
    parts = three_parts(pad_columns(q_ref[0, 0, 0].astype(F32) * (LOG2E * HEAD_DIM**-0.5), padded))
    query_s[...] = jnp.concatenate([*parts, jnp.zeros((HEAD_DIM, padded), BF)], 0)
    value_s[0:HEAD_DIM] = v_ref[0, 0, 0]
    value_s[HEAD_DIM : HEAD_DIM + 16] = jnp.ones((16, seq), BF)
    for start, width, used in query_blocks(seq, step):
        scores = dot(key_s[...], query_s[:, start : start + width])
        top = jnp.max(scores, 0, keepdims=True)
        prob = jnp.exp2(scores - top).astype(BF)
        mixed = dot(value_s[...], prob)
        total = mixed[HEAD_DIM : HEAD_DIM + 1]
        result = (mixed[0:HEAD_DIM] * (1.0 / total))[:, :used]
        wide_ref[0, :, start : start + used] = result
        o_ref[0, :, start : start + used] = result.astype(BF)
        lse_ref[0, :, start : start + used] = (top + jnp.log2(total))[:, :used]
    odd = pl.program_id(0) % 2
    hold_s[pl.ds(pl.multiple_of(odd * HEAD_DIM, HEAD_DIM), HEAD_DIM)] = o_ref[0]

    @pl.when(odd == 1)
    def _():
        row_ref[...] = hold_s[...].T


def attend(qkv, group, step):
    _, _, heads, _, seq = qkv.shape
    padded = -(-seq // 128) * 128
    part = lambda i: pl.BlockSpec((1, 1, 1, HEAD_DIM, seq), lambda h: (group, i, h, 0, 0))
    spec = lambda rows: pl.BlockSpec((1, rows, seq), lambda h: (h, 0, 0))
    return call(
        functools.partial(attend_kernel, seq, padded, step),
        (heads,),
        [part(0), part(1), part(2)],
        [spec(HEAD_DIM), pl.BlockSpec((seq, 2 * HEAD_DIM), lambda h: (0, h // 2)), spec(HEAD_DIM), spec(1)],
        [
            shaped((heads, HEAD_DIM, seq)),
            shaped((seq, heads * HEAD_DIM)),
            shaped((heads, HEAD_DIM, seq), F32),
            shaped((heads, 1, seq), F32),
        ],
        (qkv, qkv, qkv),
        [
            pltpu.VMEM((seq, 4 * HEAD_DIM), BF),
            pltpu.VMEM((4 * HEAD_DIM, padded), BF),
            pltpu.VMEM((HEAD_DIM + 16, seq), BF),
            pltpu.VMEM((2 * HEAD_DIM, seq), BF),
        ],
        name="attend",
    )


def attend_back_kernel(
    seq, padded, step, q_ref, k_ref, v_ref, d_ref, lse_ref, delta_ref, out_ref, sum_ref, key_s, query_s, value_s, dmix_s, hold_s
):
    key = k_ref[0, 0, 0]
    ones = jnp.ones((16, seq), BF)
    key_s[...] = jnp.concatenate([key, key, key, ones, jnp.zeros((48, seq), BF)], 0).T
    value_s[...] = jnp.concatenate([v_ref[0, 0, 0], ones, jnp.zeros((48, seq), BF)], 0).T
    query = pad_columns(q_ref[0, 0, 0], padded).astype(F32)
    blank = jnp.zeros((13, padded), BF)
    tail = jnp.zeros((48, padded), BF)
    lse = jnp.concatenate([*three_parts(pad_columns(-lse_ref[0], padded)), blank], 0)
    delta = jnp.concatenate([*three_parts(pad_columns(-delta_ref[0], padded)), blank], 0)
    query_s[...] = jnp.concatenate([*three_parts(query * (LOG2E * HEAD_DIM**-0.5)), lse, tail], 0)
    dmix_s[...] = jnp.concatenate([pad_columns(d_ref[0], padded), delta, tail], 0)
    scaled = (query * HEAD_DIM**-0.5).astype(BF)
    odd = pl.program_id(0) % 2
    here = pl.ds(pl.multiple_of(odd * HEAD_DIM, HEAD_DIM), HEAD_DIM)
    d_keys = jnp.zeros((HEAD_DIM, seq), F32)
    d_values = jnp.zeros((HEAD_DIM, seq), F32)
    for start, width, used in query_blocks(seq, step):
        prob = jnp.exp2(dot(key_s[...], query_s[:, start : start + width]))
        d_scores = (prob * dot(value_s[...], dmix_s[:, start : start + width])).astype(BF)
        d_values = d_values + dot(dmix_s[0:HEAD_DIM, start : start + width], prob.astype(BF), ROW_NT)
        d_keys = d_keys + dot(scaled[:, start : start + width], d_scores, ROW_NT)
        d_query = dot(key, d_scores) * HEAD_DIM**-0.5
        hold_s[0, here, start : start + used] = d_query[:, :used].astype(BF)
    hold_s[1, here] = d_keys.astype(BF)
    hold_s[2, here] = d_values.astype(BF)

    @pl.when(odd == 1)
    def _():
        for i in range(3):
            turned = hold_s[i].T
            out_ref[i] = turned
            sum_ref[i] = jnp.sum(turned.astype(F32), 0, keepdims=True)


def attend_backward(qkv, d_mixed, lse, delta, group, first, count, step):
    _, _, inner, _, seq = qkv.shape
    padded = -(-seq // 128) * 128
    part = lambda i: pl.BlockSpec((1, 1, 1, HEAD_DIM, seq), lambda h: (group, i, first + h, 0, 0))
    spec = lambda rows: pl.BlockSpec((1, rows, seq), lambda h: (group * inner + first + h, 0, 0))
    return call(
        functools.partial(attend_back_kernel, seq, padded, step),
        (count,),
        [part(0), part(1), part(2), spec(HEAD_DIM), pl.BlockSpec((1, 1, seq), lambda h: (first + h, 0, 0)), spec(1)],
        [
            pl.BlockSpec((3, seq, 2 * HEAD_DIM), lambda h: (0, 0, h // 2)),
            pl.BlockSpec((3, 1, 2 * HEAD_DIM), lambda h: (0, 0, h // 2)),
        ],
        [shaped((3, seq, count * HEAD_DIM)), shaped((3, 1, count * HEAD_DIM), F32)],
        (qkv, qkv, qkv, d_mixed, lse, delta),
        [
            pltpu.VMEM((seq, 4 * HEAD_DIM), BF),
            pltpu.VMEM((4 * HEAD_DIM, padded), BF),
            pltpu.VMEM((seq, 2 * HEAD_DIM), BF),
            pltpu.VMEM((2 * HEAD_DIM, padded), BF),
            pltpu.VMEM((3, 2 * HEAD_DIM, seq), BF),
        ],
        name="attend_backward",
    )


def mix_kernel(place_ref, oa_ref, ob_ref, w_ref, out_ref):
    places, cols = w_ref.shape[1:3]
    weights = [row_blocks(w_ref, place_block(place_ref, j), 0, cols) for j in range(places)]
    out_ref[...] = dot(jnp.concatenate([oa_ref[...], ob_ref[...]], 1), jnp.concatenate(weights, 0))


def mix(place, rows, weights, which):
    seq, wide = rows[0].shape
    owners, places, _, part = weights.shape
    cols = PAIR * wide // places
    half = seq // 2
    return call(
        mix_kernel,
        (2,),
        [
            SCALAR,
            pl.BlockSpec((half, wide), lambda n: (which, 0)),
            pl.BlockSpec((half, wide), lambda n: (which, 0)),
            pl.BlockSpec((owners // 2, places, cols, part), lambda n: (n, 0, 1, 0)),
        ],
        pl.BlockSpec((half, owners * part // 2), lambda n: (0, n)),
        shaped((half, owners * part), F32),
        (place, *rows, weights),
        name="mix",
    )


def mix_back_kernel(place_ref, da_ref, db_ref, w_ref, oa_ref, ob_ref, wa_ref, wb_ref, d_ref, delta_ref, *refs):
    *grad_refs, d_s = refs
    half, width = da_ref.shape
    cols = w_ref.shape[2]
    heads = oa_ref.shape[0]
    group = pl.program_id(0)

    @pl.when(group == 0)
    def _():
        d_s[0:half] = da_ref[...]
        d_s[half:] = db_ref[...]

    places = [place_block(place_ref, PAIR * group + p) for p in range(PAIR)]
    weights = jnp.concatenate([row_blocks(w_ref, place, 0, cols) for place in places], 0)
    d_heads = dot(weights, d_s[...], ROW_NT).astype(BF).reshape(oa_ref.shape)
    d_ref[...] = d_heads
    for which, o_ref, wide_ref in ((0, oa_ref, wa_ref), (1, ob_ref, wb_ref)):

        @pl.when(group == which)
        def _():
            delta_ref[...] = jnp.sum(d_heads.astype(F32) * wide_ref[...], 1, keepdims=True)
            grad = dot(o_ref[...].reshape(heads * HEAD_DIM, 2 * half), d_s[...]).astype(BF).T
            for p in range(PAIR):
                grad_refs[p][:, :, 0] = grad[:, p * cols : (p + 1) * cols].reshape(2, 2, width // 4, cols)


def mix_back(place, da, db, weights, mixed, wide):
    half, width = da.shape
    owners, places, _, part = weights.shape
    heads, _, seq = mixed[0].shape
    groups = places // PAIR
    cols = heads * HEAD_DIM // PAIR
    whole = pl.BlockSpec((half, width), lambda g: (0, 0))
    fixed = pl.BlockSpec((heads, HEAD_DIM, seq), lambda g: (0, 0, 0))
    spec = lambda rows: pl.BlockSpec((heads, rows, seq), lambda g: (g, 0, 0))
    grad = pl.BlockSpec((2, 2, 1, width // 4, cols), lambda g: (0, 0, g, 0, 0))
    return call(
        mix_back_kernel,
        (groups,),
        [SCALAR, whole, whole, pl.BlockSpec((owners, places, cols, part), lambda g: (0, 0, 1, 0))] + [fixed] * 4,
        [spec(HEAD_DIM), spec(1), grad, grad],
        [shaped((groups * heads, HEAD_DIM, seq)), shaped((groups * heads, 1, seq), F32)]
        + [shaped((2, 2, groups, width // 4, cols))] * PAIR,
        (place, da, db, weights, *mixed, *wide),
        [pltpu.VMEM((seq, width), BF)],
        name="mix_back",
    )


def project_grad_kernel(t_ref, da_ref, db_ref, *grad_refs):
    width = t_ref.shape[0]
    cols = da_ref.shape[2]
    grad = dot(t_ref[...], jnp.concatenate([da_ref[0], db_ref[0]], 1)).astype(BF)
    for p, grad_ref in enumerate(grad_refs):
        grad_ref[:, :, 0] = grad[:, p * cols : (p + 1) * cols].reshape(2, 2, width // 4, cols)


def project_grads(turned, da, db):
    width, seq = turned.shape
    cols = da.shape[2]
    piece = pl.BlockSpec((1, seq, cols), lambda i: (i, 0, 0))
    grad = pl.BlockSpec((2, 2, 1, width // 4, cols), lambda i: (0, 0, i, 0, 0))
    return call(
        project_grad_kernel,
        (3,),
        [pl.BlockSpec((width, seq), lambda i: (0, 0)), piece, piece],
        [grad, grad],
        [shaped((2, 2, 3, width // 4, cols))] * 2,
        (turned, da, db),
        name="project_grads",
    )


def project_back_kernel(place_ref, a_ref, b_ref, c_ref, d_ref, qk_ref, v_ref, out_ref):
    total = None
    for first, refs in ((0, (a_ref, b_ref)), (PAIR, (c_ref, d_ref))):
        places = [place_block(place_ref, first + p) for p in range(PAIR)]
        left = [ref[i] for i in range(3) for ref in refs]
        right = [qk_ref[0, place, i] for i in range(2) for place in places] + [v_ref[0, place] for place in places]
        part = dot(jnp.concatenate(left, 1), jnp.concatenate(right, 0))
        total = part if total is None else total + part
    out_ref[...] = total


def project_back(place, pieces, w_qk, w_vo, which):
    seq = pieces[0].shape[1]
    owners, places, _, cols, part = w_qk.shape
    half = seq // 2
    return call(
        project_back_kernel,
        (owners,),
        [SCALAR]
        + [pl.BlockSpec((3, half, cols), lambda n: (0, which, 0)) for piece in pieces]
        + [
            pl.BlockSpec((1, places, 2, cols, part), lambda n: (n, 0, 0, 0, 0)),
            pl.BlockSpec((1, places, cols, part), lambda n: (n, 0, 0, 0)),
        ],
        pl.BlockSpec((half, part), lambda n: (0, n)),
        shaped((half, owners * part), F32),
        (place, *pieces, w_qk, w_vo),
        name="project_back",
    )


def gelu_pair(value):
    cdf = 0.5 * (1.0 + lax.erf(value * 0.7071067811865476))
    return value * cdf, cdf + value * (jnp.exp(-0.5 * value * value) * 0.3989422804014327)


def all_blocks(ref):
    return jnp.concatenate([ref[0, t] for t in range(ref.shape[1])], 1)


def ffn_kernel(x_ref, first_ref, last_ref, b_ref, out_ref, g_ref, slope_ref, hold_s):
    blocks = hold_s.shape[0]
    step = pl.program_id(0)

    @pl.when(step < blocks)
    def _():
        pre = dot(x_ref[...], first_ref[...].reshape(x_ref.shape[1], -1)) + b_ref[0]
        active, slope = gelu_pair(pre)
        active = active.astype(BF)
        hold_s[step] = active
        g_ref[...] = active
        slope_ref[...] = slope.astype(BF)

    @pl.when(step >= blocks)
    def _():
        left = jnp.concatenate([hold_s[t] for t in range(blocks)], 1)
        out_ref[...] = dot(left, all_blocks(last_ref), ROW_NT)


def ffn_specs(rows, weights):
    owners, blocks, part, units = weights.shape
    early = lambda s: jnp.minimum(s, blocks - 1)
    late = lambda s: jnp.maximum(s - blocks, 0)
    return (
        pl.BlockSpec((rows, owners * part), lambda s: (0, 0)),
        pl.BlockSpec((owners, 1, part, units), lambda s: (0, early(s), 0, 0)),
        pl.BlockSpec((1, blocks, part, units), lambda s: (late(s), 0, 0, 0)),
        pl.BlockSpec((rows, units), lambda s: (0, early(s))),
        pl.BlockSpec((1, 1, units), lambda s: (early(s), 0, 0)),
        pl.BlockSpec((rows, part), lambda s: (0, late(s))),
    )


def ffn_forward(x, up, down, bias):
    rows, width = x.shape
    owners, blocks, _, units = up.shape
    whole, early, late, column, thin, out = ffn_specs(rows, up)
    return call(
        ffn_kernel,
        (blocks + owners,),
        [whole, early, late, thin],
        [out, column, column],
        [shaped((rows, width), F32), shaped((rows, blocks * units)), shaped((rows, blocks * units))],
        (x, up, down, bias),
        [pltpu.VMEM((blocks, rows, units), BF)],
        name="ffn",
    )


def ffn_back_kernel(d_ref, first_ref, last_ref, slope_ref, out_ref, dpre_ref, sum_ref, hold_s):
    blocks = hold_s.shape[0]
    step = pl.program_id(0)

    @pl.when(step < blocks)
    def _():
        d_pre = (dot(d_ref[...], first_ref[...].reshape(d_ref.shape[1], -1)) * slope_ref[...].astype(F32)).astype(BF)
        hold_s[step] = d_pre
        dpre_ref[...] = d_pre
        sum_ref[0] = jnp.sum(d_pre.astype(F32), 0, keepdims=True)

    @pl.when(step >= blocks)
    def _():
        left = jnp.concatenate([hold_s[t] for t in range(blocks)], 1)
        out_ref[...] = dot(left, all_blocks(last_ref), ROW_NT)


def ffn_backward(d_out, up, down, slope):
    rows, width = d_out.shape
    owners, blocks, _, units = up.shape
    whole, early, late, column, thin, out = ffn_specs(rows, up)
    return call(
        ffn_back_kernel,
        (blocks + owners,),
        [whole, early, late, column],
        [out, column, thin],
        [shaped((rows, width), F32), shaped((rows, blocks * units)), shaped((blocks, 1, units), F32)],
        (d_out, down, up, slope),
        [pltpu.VMEM((blocks, rows, units), BF)],
        name="ffn_backward",
    )


def ffn_grad_kernel(xa_ref, xb_ref, ca_ref, cb_ref, first_ref, last_ref, x_s):
    half = xa_ref.shape[0]

    @pl.when(pl.program_id(0) == 0)
    def _():
        x_s[...] = jnp.concatenate([xa_ref[...], xb_ref[...]], 0).T

    column = jnp.concatenate([ca_ref[...], cb_ref[...]], 0)
    grad = dot(x_s[...], column).astype(BF).reshape(first_ref.shape)

    @pl.when(pl.program_id(0) < PAIR)
    def _():
        first_ref[...] = grad

    @pl.when(pl.program_id(0) >= PAIR)
    def _():
        last_ref[...] = grad


def ffn_grad(xa, xb, ca, cb, blocks):
    rows, width = xa.shape
    units = ca.shape[1] // blocks
    whole = pl.BlockSpec((rows, width), lambda t: (0, 0))
    column = pl.BlockSpec((rows, units), lambda t: (0, t))
    return call(
        ffn_grad_kernel,
        (blocks,),
        [whole, whole, column, column],
        [
            pl.BlockSpec((2, 2, 1, width // 4, units), lambda t: (0, 0, jnp.minimum(t, PAIR - 1), 0, 0)),
            pl.BlockSpec((2, 2, 1, width // 4, units), lambda t: (0, 0, jnp.maximum(t - PAIR, 0), 0, 0)),
        ],
        [shaped((2, 2, PAIR, width // 4, units))] * 2,
        (xa, xb, ca, cb),
        [pltpu.VMEM((width, 2 * rows), BF)],
        name="ffn_grad",
    )


def swap(value, axis):
    return lax.ppermute(value, axis, [(0, 1), (1, 0)])


def after(value, *others):
    return lax.optimization_barrier((value, *others))[0]


def together(*values):
    return lax.optimization_barrier(values)


def ordered(bit, mine, other, axis):
    return jnp.concatenate([jnp.where(bit == 0, mine, other), jnp.where(bit == 0, other, mine)], axis)


def chosen(value, bit, axis):
    return lax.dynamic_index_in_dim(value, bit, axis, keepdims=False)


def added(mine, other):
    return (mine.astype(F32) + other.astype(F32)).astype(BF)


def moments(value):
    mean = jnp.mean(value, -1, keepdims=True)
    centred = value - mean
    scale = lax.rsqrt(jnp.mean(centred * centred, -1, keepdims=True) + EPS)
    return centred, scale


def norm_back(d_value, centred, scale, gain):
    unit = centred * scale
    d_unit = d_value * gain
    grad_in = scale * (d_unit - jnp.mean(d_unit, -1, keepdims=True) - unit * jnp.mean(d_unit * unit, -1, keepdims=True))
    return grad_in, jnp.sum(d_value * unit, 0), jnp.sum(d_value, 0)


def clip_local(clips, w_qkv, w_out, w_up, w_down, norm_gain, shifts, bias_qv, up_bias, teacher):
    y, x, c, t = (lax.axis_index(name) for name in ("y", "x", "c", "t"))
    every = ("y", "x", "c", "t")
    steps = 4
    width = clips.shape[2]
    odd = t % 2

    first_way, second_way = [], []
    for column in range(4):
        for core in range(2):
            for place in range(4):
                source = (column * 2 + core) * 4 + place
                to = (column * 2 + place // 2) * 4 + 2 * core
                first_way.append((source, to + place % 2))
                second_way.append((source, to + 1 - place % 2))
    first_way = [(a, b) for a, b in first_way if a != b]
    back = lambda way: [(b, a) for a, b in way]
    stays = t // 2 == c

    def to_chip(value):
        return lax.ppermute(chosen(value, odd, 0), every, first_way), lax.ppermute(chosen(value, 1 - odd, 0), every, second_way)

    def from_chip(value):
        half = value.shape[0] // 2
        return lax.ppermute(value[:half], every, back(first_way)), lax.ppermute(value[half:], every, back(second_way))

    rings = [[(i, (i + away) % steps) for i in range(steps)] for away in range(steps)]

    def ring_gather(value):
        return tuple(lax.ppermute(value, "t", rings[-j % steps]) for j in range(1, steps))

    def ring_scatter(blocks):
        return tuple(lax.ppermute(blocks[j], "t", rings[j]) for j in range(1, steps))

    def placed(value, axis):
        return lax.dynamic_slice_in_dim(jnp.concatenate([value, value], axis), steps - t, steps, axis)

    def relative(value, axis):
        return lax.dynamic_slice_in_dim(jnp.concatenate([value, value], axis), t, steps, axis)

    def on_chip(value, near, far):
        return jnp.concatenate([jnp.where(stays, chosen(value, odd, 0), near), far])

    def as_clips(value, near, far):
        near = jnp.where(stays, value[: value.shape[0] // 2], near)
        return jnp.stack([jnp.where(odd == 0, near, far), jnp.where(odd == 0, far, near)])

    def piece_of(values, *places):
        parts = []
        for value in values:
            for bit, axis in places:
                value = chosen(value, bit, axis)
            parts.append(value)
        return parts[0] if len(parts) == 1 else jnp.concatenate(parts, parts[0].ndim - 3)

    def scatter_start(one, two):
        return swap(piece_of(one, (1 - x, 1)), "x"), swap(piece_of(two, (1 - y, 0)), "y")

    def sums_of(one, two, parts, row, column):
        first = piece_of(one, (x, 1), (row, 0)).astype(F32) + chosen(parts[0], row, 0).astype(F32)
        return first, piece_of(two, (y, 0), (column, 0)).astype(F32) + chosen(parts[1], column, 0).astype(F32)

    def scatter_middle(one, two, parts):
        first, second = sums_of(one, two, parts, 1 - y, 1 - x)
        return swap(first.astype(BF), "y"), swap(second.astype(BF), "x")

    def scatter_end(one, two, parts, ends):
        first, second = sums_of(one, two, parts, y, x)
        return (first + ends[0].astype(F32)).astype(BF), (second + ends[1].astype(F32)).astype(BF)

    dims = w_qkv.shape[1]
    cols = w_out.shape[0] // 2
    lane = bias_qv.shape[1]
    units = w_up.shape[1] // 2
    attn = jnp.concatenate([jnp.swapaxes(w_qkv, 1, 2), w_out[None]]).reshape(4, 2, cols, dims)
    small = jnp.concatenate([bias_qv.reshape(-1), up_bias, jnp.zeros((16 * dims - bias_qv.size - up_bias.size,), BF)])
    small = small.reshape(16, dims)
    mine, other = chosen(attn, c, 1).reshape(4 * cols, dims), chosen(attn, 1 - c, 1).reshape(4 * cols, dims)
    other = swap(jnp.concatenate([other, small]), "c")
    attn_piece = ordered(c, jnp.concatenate([mine, small]), other, 1)
    qk_piece, vo_piece = attn_piece[: 2 * cols], attn_piece[2 * cols :]
    ff = jnp.stack([w_up, w_down.T]).reshape(2, dims, 2, units)
    ff_piece = ordered(c, chosen(ff, c, 2), swap(chosen(ff, 1 - c, 2), "c"), 1)

    vectors = jnp.concatenate([norm_gain, shifts, jnp.zeros((2, norm_gain.shape[1]), BF)])
    for bit, name in ((c, "c"), (x, "x"), (y, "y")):
        vectors = ordered(bit, vectors, swap(vectors, name), 1)
    vectors = vectors.astype(F32)
    gains, shift_all = vectors[0:2], vectors[2:6]

    near, far = to_chip(clips)
    whole = ("y", "x", "t")
    w_vo = lax.all_gather(vo_piece, whole, axis=0, tiled=False).reshape(4, steps, 2 * cols + 16, 2 * dims)
    qk_rows = together(*ring_gather(qk_piece))
    qk_rows = placed(jnp.stack([qk_piece, *qk_rows]), 0)
    qk_a, qk_b = qk_rows[:, :cols], qk_rows[:, cols:]
    swapped, near = together((swap(qk_a, "y"), swap(qk_b, "x")), near)
    qk_a, qk_b = ordered(y, qk_a[None], swapped[0][None], 0), ordered(x, qk_b[None], swapped[1][None], 0)
    swapped, far = together((swap(qk_a, "x"), swap(qk_b, "y")), far)
    qk_a = ordered(x, qk_a[:, None], swapped[0][:, None], 1).reshape(4, steps, cols, 2 * dims)
    qk_b = ordered(y, qk_b[None], swapped[1][None], 0).reshape(4, steps, cols, 2 * dims)
    w_qk = jnp.stack([qk_a, qk_b], 2)
    up_piece, down_piece = ff_piece
    up_piece, far = together(up_piece, far)
    up_rows = ring_gather(up_piece)
    down_piece, w_vo = together(down_piece, w_vo)
    down_all = lax.all_gather(down_piece, whole, axis=0, tiled=False).reshape(4, steps, 2 * dims, units)
    place = t.reshape(1)

    rows = w_vo[:, :, 2 * cols :].reshape(4, steps, 16, 2, dims)
    rows = jnp.transpose(rows, (1, 0, 3, 2, 4)).reshape(steps, 8, 16 * dims).astype(F32)
    rows = lax.dynamic_slice_in_dim(rows, 4 * c, 4, 1)
    bias_pair = jnp.transpose(rows[..., : 2 * lane].reshape(steps, 4, 2, lane), (2, 0, 1, 3)).reshape(2, steps, cols)
    bias_pair = relative(bias_pair, 1).reshape(2, 2, 2 * cols)
    up_shift = rows[..., 2 * lane : 2 * lane + up_bias.size].reshape(steps, 1, units)

    inputs = on_chip(clips, near, far).astype(F32)
    centred_one, scale_one = moments(inputs)
    first = (centred_one * scale_one * gains[0] + shift_all[0]).astype(BF)
    first_other = swap(first, "c")
    bias_in = jnp.stack([bias_pair[0], jnp.zeros_like(bias_pair[0]), bias_pair[1]], 1)
    qkv, turned = project(place, first, first_other, w_qk, w_vo, bias_in[..., None])
    mixed_a, rows_a, wide_a, lse_a = attend(qkv, 0, 1664)
    up_rows, rows_a = together(up_rows, rows_a)
    up_rows = placed(jnp.stack([up_piece, *up_rows]), 0)
    up_a, up_b = up_rows[:PAIR], up_rows[PAIR:]
    swapped = swap(up_a, "y"), swap(up_b, "x")
    mixed_b, rows_b, wide_b, lse_b = attend(after(qkv, rows_a), 1, 1664)
    swapped, rows_b = together(swapped, rows_b)
    up_a, up_b = ordered(y, up_a[None], swapped[0][None], 0), ordered(x, up_b[None], swapped[1][None], 0)
    swapped = swap(up_a, "x"), swap(up_b, "y")
    rows = (rows_a, rows_b)
    attn_other = mix(place, rows, w_vo, 1)
    down_all, attn_other = together(down_all, attn_other)
    attn_mine = mix(place, (after(rows_a, attn_other), rows_b), w_vo, 0)
    hidden = inputs + (attn_mine + swap(attn_other, "c")) + shift_all[2]

    centred_two, scale_two = moments(hidden)
    second = (centred_two * scale_two * gains[1] + shift_all[1]).astype(BF)
    second_other = swap(second, "c")
    swapped, second = together(swapped, second)
    up_a = ordered(x, up_a[:, None], swapped[0][:, None], 1).reshape(4, PAIR, 2 * dims, units)
    up_b = ordered(y, up_b[None], swapped[1][None], 0).reshape(4, PAIR, 2 * dims, units)
    up_all = jnp.concatenate([up_a, up_b], 1)
    near, far = to_chip(after(teacher, second))
    out_mine, act_mine, slope_mine = ffn_forward(second, up_all, down_all, up_shift)
    out_mine, near = together(out_mine, near)
    out_other, act_other, slope_other = ffn_forward(after(second_other, near), up_all, down_all, up_shift)
    out_other, far = together(out_other, far)
    output = hidden + (out_mine + swap(out_other, "c")) + shift_all[3]
    d_out = output - on_chip(teacher, near, far).astype(F32)
    d_ffn = d_out.astype(BF)
    d_ffn_other = swap(d_ffn, "c")
    d_second, d_pre, sum_mine = ffn_backward(d_ffn, up_all, down_all, slope_mine)
    d_ffn_other, d_pre = together(d_ffn_other, d_pre)
    d_second_other, d_pre_other, sum_other = ffn_backward(d_ffn_other, up_all, down_all, slope_other)
    d_second_swapped = swap(d_second_other, "c")
    up_sum = (sum_mine + sum_other).reshape(steps, units)

    grad_down = ffn_grad(after(d_ffn, d_pre_other), d_ffn_other, act_mine, act_other, steps)
    grad_down = [grad_down[0]], [grad_down[1]]
    down = scatter_start(*grad_down)
    result, grad_down = together(output.astype(BF), grad_down)
    out_near, out_far = from_chip(result)
    d_second_swapped, grad_down = together(d_second_swapped, grad_down)
    d_second = d_second + d_second_swapped
    d_norm, grad_gain_two, grad_shift_two = norm_back(d_second, centred_two, scale_two, gains[1])
    d_hidden = d_out + d_norm
    d_attn = d_hidden.astype(BF)
    d_attn_other = swap(d_attn, "c")
    grad_up = ffn_grad(after(second, d_attn), second_other, d_pre, d_pre_other, steps)
    grad_up = [grad_up[0]], [grad_up[1]]
    up = scatter_start(*grad_up)
    d_attn_other, grad_up = together(d_attn_other, grad_up)

    d_heads, delta, *grad_o = mix_back(place, d_attn, d_attn_other, w_vo, (mixed_a, mixed_b), (wide_a, wide_b))
    down, delta = together(down, delta)
    down_ends = scatter_middle(*grad_down, down)
    back_a, sum_a = attend_backward(qkv, d_heads, lse_b, delta, 1, 0, 2, 256)
    up, out_near, back_a = together(up, out_near, back_a)
    up_ends = scatter_middle(*grad_up, up)
    back_b, sum_b = attend_backward(qkv, after(d_heads, back_a), lse_b, delta, 1, 2, 2, 256)
    up_ends, down_ends, out_far, back_b = together(up_ends, down_ends, out_far, back_b)
    ups, downs = scatter_end(*grad_up, up, up_ends), scatter_end(*grad_down, down, down_ends)
    grad_ff = jnp.concatenate([jnp.stack(pair, 1) for pair in zip(ups, downs)]).reshape(steps * 4 * dims, units)
    ff_total = lax.psum_scatter(grad_ff, "t", scatter_dimension=0, tiled=True)
    grad_one = [[grad, grad_o[p]] for p, grad in enumerate(project_grads(turned, back_a, back_b))]
    one = scatter_start(*grad_one)
    delta, grad_ff, grad_one = together(delta, grad_ff, grad_one)
    back_c, sum_c = attend_backward(qkv, after(d_heads, back_b), lse_a, delta, 0, 2, 2, 256)
    one, back_c = together(one, back_c)
    one_ends = scatter_middle(*grad_one, one)
    back_d, sum_d = attend_backward(qkv, after(d_heads, back_c), lse_a, delta, 0, 0, 2, 256)
    one_ends, back_d = together(one_ends, back_d)
    grad_two = project_grads(turned, back_d, back_c)
    grad_two = [grad_two[0]], [grad_two[1]]
    two = scatter_start(*grad_two)
    pieces = (back_d, back_c, back_a, back_b)
    d_first_other = project_back(place, pieces, w_qk, after(w_vo, grad_two), 1)
    d_first_swapped = swap(d_first_other, "c")
    one = scatter_end(*grad_one, one, one_ends)
    early = [lax.ppermute(jnp.concatenate([one[p][:3], one[p][4:]]), "t", rings[PAIR + p]) for p in range(PAIR)]
    two, d_first_other = together(two, d_first_other)
    two_ends = scatter_middle(*grad_two, two)
    d_first = project_back(place, pieces, w_qk, after(w_vo, d_first_other), 0)
    ff_total, early, d_first = together(ff_total, early, d_first)
    d_first_swapped, d_first = together(d_first_swapped, d_first)
    d_first = d_first + d_first_swapped
    d_norm, grad_gain_one, grad_shift_one = norm_back(d_first, centred_one, scale_one, gains[0])
    d_inputs = (d_hidden + d_norm).astype(BF)
    grad_near, grad_far = from_chip(d_inputs)
    two_ends, d_inputs = together(two_ends, d_inputs)
    two = scatter_end(*grad_two, two, two_ends)
    late = lax.ppermute(jnp.concatenate([two[1], one[1][3:4]]), "t", rings[1])
    late, grad_near, out_near, out_far = together(late, grad_near, out_near, out_far)

    grad_ff = ff_total.astype(F32).reshape(2, 2, dims, units)
    grad_ff = ordered(c, chosen(grad_ff, c, 1), swap(chosen(grad_ff, 1 - c, 1), "c"), 2)
    grad_attn = jnp.concatenate([two[0], one[0][3:4]]).astype(F32)
    grad_attn = sum((part.astype(F32) for part in (*early, late)), grad_attn).reshape(4, 2, dims, cols)
    grad_attn = ordered(c, chosen(grad_attn, c, 1), swap(chosen(grad_attn, 1 - c, 1), "c"), 2)

    normed = jnp.stack([grad_gain_one, grad_gain_two, grad_shift_one, grad_shift_two, jnp.sum(d_hidden, 0), jnp.sum(d_out, 0)])
    thin = width // 32
    rows = jnp.swapaxes(normed.reshape(6, 32, thin), 0, 1).reshape(32, 6 * thin)
    sums = jnp.concatenate([sum_d, sum_c, sum_a, sum_b], 2)
    pair = placed(jnp.stack([sums[0], sums[2]]).reshape(2, steps, 4, lane), 1)
    pair = jnp.transpose(pair, (2, 1, 0, 3))
    ups = jnp.transpose(up_sum.reshape(steps, 4, up_bias.size), (1, 0, 2))
    mine = jnp.concatenate([pair.reshape(16, 2 * lane), ups.reshape(16, up_bias.size)], 1)
    here = jnp.where((jnp.arange(2) == c)[:, None, None], mine[None], 0.0).reshape(32, mine.shape[1])
    sums = after(jnp.concatenate([rows, here], 1), grad_near)
    for bit, name in ((y, "y"), (x, "x"), (c, "c")):
        sums = sums.reshape(2, sums.shape[0] // 2, sums.shape[1])
        sums = chosen(sums, bit, 0) + swap(chosen(sums, 1 - bit, 0), name)
    total = chosen(sums, t, 0)
    for away in range(1, steps):
        total = total + lax.ppermute(chosen(sums, (t + away) % steps, 0), "t", rings[away])
    vector_sums = total[: 6 * thin].reshape(6, thin)
    return (
        as_clips(result, out_near, out_far),
        as_clips(d_inputs, grad_near, grad_far),
        grad_attn[:3],
        grad_attn[3].T,
        grad_ff[0],
        grad_ff[1].T,
        vector_sums[:2],
        vector_sums[2:],
        total[6 * thin : 6 * thin + 2 * lane].reshape(2, lane),
        total[6 * thin + 2 * lane :],
    )


def clip_per_chip(mesh):
    fine = Mesh(mesh.devices.reshape(2, 2, 2, 4), ("y", "x", "c", "t"))
    dp = ("y", "x", "c")
    in_specs = (
        P(dp, "t", None),
        P(None, dp, "t"),
        P("t", dp),
        P(dp, "t"),
        P("t", dp),
        P(None, dp),
        P(None, dp),
        P(None, ("t",) + dp),
        P(("t",) + dp),
        P(dp, "t", None),
    )
    out_specs = in_specs[:1] * 2 + in_specs[1:5] + (
        P(None, dp + ("t",)),
        P(None, dp + ("t",)),
        P(None, ("t",) + dp),
        P(("t",) + dp),
    )
    return jax.shard_map(clip_local, mesh=fine, in_specs=in_specs, out_specs=out_specs, check_vma=False)


def solution(mesh):
    if dict(mesh.shape) == {"dp": 8, "tensor": 4}:
        return clip_per_chip(mesh)
    in_specs = (
        P("dp", "tensor", None),
        P(None, "dp", "tensor"),
        P("tensor", "dp"),
        P("dp", "tensor"),
        P("tensor", "dp"),
        P(None, "dp"),
        P(None, "dp"),
        P(None, ("tensor", "dp")),
        P(("tensor", "dp")),
        P("dp", "tensor", None),
    )
    out_specs = (
        P("dp", "tensor", None),
        P("dp", "tensor", None),
        P(None, "dp", "tensor"),
        P("tensor", "dp"),
        P("dp", "tensor"),
        P("tensor", "dp"),
        P(None, ("dp", "tensor")),
        P(None, ("dp", "tensor")),
        P(None, ("tensor", "dp")),
        P(("tensor", "dp")),
    )
    return jax.shard_map(local, mesh=mesh, in_specs=in_specs, out_specs=out_specs, check_vma=False)
```

```python
import functools

import jax
import jax.numpy as jnp
from jax import lax
from jax.experimental import pallas as pl
from jax.experimental.pallas import tpu as pltpu
from jax.sharding import Mesh, PartitionSpec as P

HEAD_DIM = 64


EPS = 1e-05


def layer_norm(value, gain, shift):
    mean = jnp.mean(value, -1, keepdims=True)
    centred = value - mean
    spread = jnp.mean(centred * centred, -1, keepdims=True)
    return centred * lax.rsqrt(spread + EPS) * gain + shift


def exact_gelu(value):
    return jax.nn.gelu(value, approximate=False)


def attend_clip(query, keys, values, scale):
    scores = jnp.einsum("qhe,khe->hqk", query, keys, preferred_element_type=jnp.float32) * scale
    top = jnp.max(scores, -1, keepdims=True)
    expd = jnp.exp(scores - top)
    total = jnp.sum(expd, -1, keepdims=True)
    prob = (expd / total).astype(jnp.bfloat16)
    mixed = jnp.einsum("hqk,khe->qhe", prob, values, preferred_element_type=jnp.float32)
    return (mixed.astype(jnp.bfloat16), (top + jnp.log(total))[..., 0])


def attend_back(query, keys, values, d_mixed, logsum, scale):
    scores = jnp.einsum("qhe,khe->hqk", query, keys, preferred_element_type=jnp.float32) * scale
    prob = jnp.exp(scores - logsum[:, :, None])
    d_prob = jnp.einsum("qhe,khe->hqk", d_mixed, values, preferred_element_type=jnp.float32)
    delta = jnp.sum(d_prob * prob, -1, keepdims=True)
    d_scores = (prob * (d_prob - delta)).astype(jnp.bfloat16)
    d_values = jnp.einsum(
        "hqk,qhe->khe", prob.astype(jnp.bfloat16), d_mixed, preferred_element_type=jnp.float32
    )
    d_query = jnp.einsum("hqk,khe->qhe", d_scores, keys, preferred_element_type=jnp.float32) * scale
    d_keys = jnp.einsum("hqk,qhe->khe", d_scores, query, preferred_element_type=jnp.float32) * scale
    return jnp.stack([d_query, d_keys, d_values]).astype(jnp.bfloat16)


def local(clips, w_qkv, w_out, w_up, w_down, norm_gain, shifts, bias_qv, up_bias, teacher):
    wq, wo, wu, wd, gains, shift_all, bias_pair, up_shift = (
        lax.all_gather(w_qkv, "dp", axis=1, tiled=True),
        lax.all_gather(w_out, "dp", axis=1, tiled=True),
        lax.all_gather(w_up, "dp", axis=0, tiled=True),
        lax.all_gather(w_down, "dp", axis=1, tiled=True),
        lax.all_gather(norm_gain, "dp", axis=1, tiled=True),
        lax.all_gather(shifts, "dp", axis=1, tiled=True),
        lax.all_gather(bias_qv, "dp", axis=1, tiled=True),
        lax.all_gather(up_bias, "dp", axis=0, tiled=True),
    )
    gains = gains.astype(jnp.float32)
    shift_all = shift_all.astype(jnp.float32)
    bias_pair = bias_pair.astype(jnp.float32)
    up_shift = up_shift.astype(jnp.float32)
    width = wq.shape[2]
    heads_here = width // HEAD_DIM
    scale = HEAD_DIM ** (-0.5)
    inputs = jnp.swapaxes(clips, 0, 1).astype(jnp.float32)
    first = layer_norm(inputs, gains[0], shift_all[0]).astype(jnp.bfloat16)
    whole_first = lax.all_gather(first, "tensor", axis=0, tiled=True)
    seq = whole_first.shape[0]
    count = whole_first.shape[1]
    projected = jnp.einsum("scd,kde->ksce", whole_first, wq, preferred_element_type=jnp.float32)
    qkv_bias = jnp.stack([bias_pair[0], jnp.zeros_like(bias_pair[0]), bias_pair[1]])
    qkv = (projected + qkv_bias[:, None, None, :]).astype(jnp.bfloat16)

    def heads(value):
        return jnp.swapaxes(value, 0, 1).reshape(count, seq, heads_here, HEAD_DIM)

    query_h, keys_h, values_h = (heads(qkv[0]), heads(qkv[1]), heads(qkv[2]))
    attended, logsum = lax.map(
        lambda item: attend_clip(item[0], item[1], item[2], scale), (query_h, keys_h, values_h)
    )
    mixed = jnp.swapaxes(attended.reshape(count, seq, width), 0, 1)
    piece = mixed
    attn = lax.psum_scatter(
        jnp.einsum("scd,de->sce", piece, wo, preferred_element_type=jnp.float32),
        "tensor",
        scatter_dimension=0,
        tiled=True,
    )
    hidden = inputs + attn + shift_all[2]
    second = layer_norm(hidden, gains[1], shift_all[1]).astype(jnp.bfloat16)
    whole_second = lax.all_gather(second, "tensor", axis=0, tiled=True)
    pre = jnp.einsum("scd,df->scf", whole_second, wu, preferred_element_type=jnp.float32) + up_shift
    active = exact_gelu(pre).astype(jnp.bfloat16)
    piece = active
    ffn = lax.psum_scatter(
        jnp.einsum("scf,fe->sce", piece, wd, preferred_element_type=jnp.float32),
        "tensor",
        scatter_dimension=0,
        tiled=True,
    )
    output = hidden + ffn + shift_all[3]
    d_out = output - jnp.swapaxes(teacher, 0, 1).astype(jnp.float32)
    whole_d_ffn = lax.all_gather(d_out.astype(jnp.bfloat16), "tensor", axis=0, tiled=True)
    d_active = jnp.einsum("sce,fe->scf", whole_d_ffn, wd, preferred_element_type=jnp.float32)
    grad_down = jnp.einsum("scf,sce->fe", active, whole_d_ffn, preferred_element_type=jnp.float32)
    gelu_value, gelu_back = jax.vjp(exact_gelu, pre)
    d_pre = gelu_back(d_active)[0].astype(jnp.bfloat16)
    grad_up_shift = jnp.sum(d_pre.astype(jnp.float32), (0, 1))
    grad_up = jnp.einsum("scd,scf->df", whole_second, d_pre, preferred_element_type=jnp.float32)
    piece = d_pre
    d_second = lax.psum_scatter(
        jnp.einsum("scf,df->scd", piece, wu, preferred_element_type=jnp.float32),
        "tensor",
        scatter_dimension=0,
        tiled=True,
    )
    norm_value, second_back = jax.vjp(layer_norm, hidden, gains[1], shift_all[1])
    d_hidden_norm, grad_gain_two, grad_shift_two = second_back(d_second)
    d_hidden = d_out + d_hidden_norm
    whole_d_attn = lax.all_gather(d_hidden.astype(jnp.bfloat16), "tensor", axis=0, tiled=True)
    d_mixed = jnp.einsum(
        "sce,de->scd", whole_d_attn, wo, preferred_element_type=jnp.float32
    ).astype(jnp.bfloat16)
    grad_out = jnp.einsum("scd,sce->de", mixed, whole_d_attn, preferred_element_type=jnp.float32)
    d_heads = jnp.swapaxes(d_mixed, 0, 1).reshape(count, seq, heads_here, HEAD_DIM)
    d_stacked = lax.map(
        lambda item: attend_back(item[0], item[1], item[2], item[3], item[4], scale),
        (query_h, keys_h, values_h, d_heads, logsum),
    )
    d_qkv = jnp.transpose(d_stacked.reshape(count, 3, seq, width), (1, 2, 0, 3))
    bias_sums = jnp.sum(d_qkv.astype(jnp.float32), (1, 2))
    grad_pair = jnp.stack([bias_sums[0], bias_sums[2]])
    grad_qkv = jnp.einsum("scd,ksce->kde", whole_first, d_qkv, preferred_element_type=jnp.float32)
    piece = d_qkv
    d_first = lax.psum_scatter(
        jnp.einsum("ksce,kde->scd", piece, wq, preferred_element_type=jnp.float32),
        "tensor",
        scatter_dimension=0,
        tiled=True,
    )
    first_value, first_back = jax.vjp(layer_norm, inputs, gains[0], shift_all[0])
    d_in_norm, grad_gain_one, grad_shift_one = first_back(d_first)
    d_inputs = d_hidden + d_in_norm
    sums = (
        lax.psum_scatter(grad_qkv, "dp", scatter_dimension=1, tiled=True),
        lax.psum_scatter(grad_out, "dp", scatter_dimension=1, tiled=True),
        lax.psum_scatter(grad_up, "dp", scatter_dimension=0, tiled=True),
        lax.psum_scatter(grad_down, "dp", scatter_dimension=1, tiled=True),
        lax.psum_scatter(grad_pair, "dp", scatter_dimension=1, tiled=True),
        lax.psum_scatter(grad_up_shift, "dp", scatter_dimension=0, tiled=True),
    )
    grad_gain = jnp.stack([grad_gain_one, grad_gain_two])
    grad_shift = jnp.stack(
        [grad_shift_one, grad_shift_two, jnp.sum(d_hidden, (0, 1)), jnp.sum(d_out, (0, 1))]
    )
    norm_sums = (
        lax.psum_scatter(grad_gain, ("dp", "tensor"), scatter_dimension=1, tiled=True),
        lax.psum_scatter(grad_shift, ("dp", "tensor"), scatter_dimension=1, tiled=True),
    )
    result = jnp.swapaxes(output, 0, 1).astype(jnp.bfloat16)
    grad_in = jnp.swapaxes(d_inputs, 0, 1).astype(jnp.bfloat16)
    return (
        result,
        grad_in,
        sums[0],
        sums[1],
        sums[2],
        sums[3],
        norm_sums[0],
        norm_sums[1],
        sums[4],
        sums[5],
    )


BF = jnp.bfloat16
F32 = jnp.float32
LOG2E = 1.4426950408889634
VMEM_LIMIT = 56 * 2**20
ROW_NN = (((1,), (0,)), ((), ()))
ROW_NT = (((1,), (1,)), ((), ()))
PAIR = 2


def dot(left, right, dims=ROW_NN):
    return lax.dot_general(left, right, dims, preferred_element_type=F32)


def call(body, grid, in_specs, out_specs, out_shape, args, scratch=(), name=None, prefetch=0):
    return pl.pallas_call(
        body,
        grid_spec=pltpu.PrefetchScalarGridSpec(
            num_scalar_prefetch=prefetch, grid=grid, in_specs=in_specs, out_specs=out_specs, scratch_shapes=list(scratch)
        ),
        out_shape=out_shape,
        compiler_params=pltpu.CompilerParams(vmem_limit_bytes=VMEM_LIMIT),
        cost_estimate=pl.CostEstimate(flops=1000, bytes_accessed=1000, transcendentals=0),
        name=name,
    )(*args)


def shaped(shape, dtype=BF):
    return jax.ShapeDtypeStruct(shape, dtype)


def three_parts(value):
    high = value.astype(BF)
    rest = value - high.astype(F32)
    middle = rest.astype(BF)
    return high, middle, (rest - middle.astype(F32)).astype(BF)


def query_blocks(seq, step):
    blocks = []
    start = 0
    while start < seq:
        used = min(step, seq - start)
        blocks.append((start, -(-used // 128) * 128, used))
        start += used
    return blocks


def pad_columns(value, width):
    extra = width - value.shape[1]
    if extra == 0:
        return value
    return jnp.concatenate([value, jnp.zeros((value.shape[0], extra), value.dtype)], 1)


def row_blocks(ref, place, start, stop):
    return jnp.concatenate([ref[owner, place, start:stop] for owner in range(ref.shape[0])], 1)


def turned_owner(owner):
    return owner % 2 * 2 + owner // 2


def key_blocks(ref, place, which):
    return jnp.concatenate([ref[turned_owner(owner), place, which] for owner in range(ref.shape[0])], 1)


def project_kernel(xa_ref, xb_ref, qk_ref, v_ref, b_ref, out_ref, t_ref, x_s):
    half = xa_ref.shape[0]
    group = pl.program_id(0)

    @pl.when(group == 0)
    def _():
        x_s[0:half] = xa_ref[...]
        x_s[half:] = xb_ref[...]
        t_ref[...] = x_s[...].T

    cols = v_ref.shape[2]
    places = [PAIR * group + p for p in range(PAIR)]
    for i in range(3):
        pick = (lambda place: row_blocks(v_ref, place, 0, cols)) if i == 2 else (lambda place: key_blocks(qk_ref, place, i))
        weights = jnp.concatenate([pick(place) for place in places], 0)
        value = dot(weights, x_s[...], ROW_NT) + b_ref[0, i]
        out_ref[0, i] = value.astype(BF).reshape(out_ref.shape[2:])


def project(xa, xb, w_qk, w_vo, bias):
    half, width = xa.shape
    owners, places, _, cols, part = w_qk.shape
    groups = places // PAIR
    heads = PAIR * cols // HEAD_DIM
    whole = pl.BlockSpec((half, width), lambda g: (0, 0))
    return call(
        project_kernel,
        (groups,),
        [
            whole,
            whole,
            pl.BlockSpec((owners, places, 2, cols, part), lambda g: (0, 0, 0, 0, 0)),
            pl.BlockSpec((owners, places, cols, part), lambda g: (0, 0, 0, 0)),
            pl.BlockSpec((1, 3, PAIR * cols, 1), lambda g: (g, 0, 0, 0)),
        ],
        [
            pl.BlockSpec((1, 3, heads, HEAD_DIM, 2 * half), lambda g: (g, 0, 0, 0, 0)),
            pl.BlockSpec((width, 2 * half), lambda g: (0, 0)),
        ],
        [shaped((groups, 3, heads, HEAD_DIM, 2 * half)), shaped((width, 2 * half))],
        (xa, xb, w_qk, w_vo, bias),
        [pltpu.VMEM((2 * half, width), BF)],
        name="project",
    )


def attend_kernel(seq, padded, step, q_ref, k_ref, v_ref, o_ref, row_ref, wide_ref, lse_ref, key_s, query_s, value_s, hold_s):
    key = k_ref[0, 0, 0]
    key_s[...] = jnp.concatenate([key, key, key, jnp.zeros((HEAD_DIM, seq), BF)], 0).T
    parts = three_parts(pad_columns(q_ref[0, 0, 0].astype(F32) * (LOG2E * HEAD_DIM**-0.5), padded))
    query_s[...] = jnp.concatenate([*parts, jnp.zeros((HEAD_DIM, padded), BF)], 0)
    value_s[0:HEAD_DIM] = v_ref[0, 0, 0]
    value_s[HEAD_DIM : HEAD_DIM + 16] = jnp.ones((16, seq), BF)
    for start, width, used in query_blocks(seq, step):
        scores = dot(key_s[...], query_s[:, start : start + width])
        top = jnp.max(scores, 0, keepdims=True)
        prob = jnp.exp2(scores - top).astype(BF)
        mixed = dot(value_s[...], prob)
        total = mixed[HEAD_DIM : HEAD_DIM + 1]
        result = (mixed[0:HEAD_DIM] * (1.0 / total))[:, :used]
        wide_ref[0, :, start : start + used] = result
        o_ref[0, :, start : start + used] = result.astype(BF)
        lse_ref[0, :, start : start + used] = (top + jnp.log2(total))[:, :used]
    odd = pl.program_id(0) % 2
    hold_s[pl.ds(pl.multiple_of(odd * HEAD_DIM, HEAD_DIM), HEAD_DIM)] = o_ref[0]

    @pl.when(odd == 1)
    def _():
        row_ref[...] = hold_s[...].T


def attend(qkv, group, step):
    _, _, heads, _, seq = qkv.shape
    padded = -(-seq // 128) * 128
    part = lambda i: pl.BlockSpec((1, 1, 1, HEAD_DIM, seq), lambda h: (group, i, h, 0, 0))
    spec = lambda rows: pl.BlockSpec((1, rows, seq), lambda h: (h, 0, 0))
    return call(
        functools.partial(attend_kernel, seq, padded, step),
        (heads,),
        [part(0), part(1), part(2)],
        [spec(HEAD_DIM), pl.BlockSpec((seq, 2 * HEAD_DIM), lambda h: (0, h // 2)), spec(HEAD_DIM), spec(1)],
        [
            shaped((heads, HEAD_DIM, seq)),
            shaped((seq, heads * HEAD_DIM)),
            shaped((heads, HEAD_DIM, seq), F32),
            shaped((heads, 1, seq), F32),
        ],
        (qkv, qkv, qkv),
        [
            pltpu.VMEM((seq, 4 * HEAD_DIM), BF),
            pltpu.VMEM((4 * HEAD_DIM, padded), BF),
            pltpu.VMEM((HEAD_DIM + 16, seq), BF),
            pltpu.VMEM((2 * HEAD_DIM, seq), BF),
        ],
        name="attend",
    )


def attend_back_kernel(
    seq, padded, step, q_ref, k_ref, v_ref, d_ref, lse_ref, delta_ref, out_ref, sum_ref, key_s, query_s, value_s, dmix_s, hold_s
):
    key = k_ref[0, 0, 0]
    ones = jnp.ones((16, seq), BF)
    key_s[...] = jnp.concatenate([key, key, key, ones, jnp.zeros((48, seq), BF)], 0).T
    value_s[...] = jnp.concatenate([v_ref[0, 0, 0], ones, jnp.zeros((48, seq), BF)], 0).T
    query = pad_columns(q_ref[0, 0, 0], padded).astype(F32)
    blank = jnp.zeros((13, padded), BF)
    tail = jnp.zeros((48, padded), BF)
    lse = jnp.concatenate([*three_parts(pad_columns(-lse_ref[0], padded)), blank], 0)
    delta = jnp.concatenate([*three_parts(pad_columns(-delta_ref[0], padded)), blank], 0)
    query_s[...] = jnp.concatenate([*three_parts(query * (LOG2E * HEAD_DIM**-0.5)), lse, tail], 0)
    dmix_s[...] = jnp.concatenate([pad_columns(d_ref[0], padded), delta, tail], 0)
    scaled = (query * HEAD_DIM**-0.5).astype(BF)
    odd = pl.program_id(0) % 2
    here = pl.ds(pl.multiple_of(odd * HEAD_DIM, HEAD_DIM), HEAD_DIM)
    d_keys = jnp.zeros((HEAD_DIM, seq), F32)
    d_values = jnp.zeros((HEAD_DIM, seq), F32)
    for start, width, used in query_blocks(seq, step):
        prob = jnp.exp2(dot(key_s[...], query_s[:, start : start + width]))
        d_scores = (prob * dot(value_s[...], dmix_s[:, start : start + width])).astype(BF)
        d_values = d_values + dot(dmix_s[0:HEAD_DIM, start : start + width], prob.astype(BF), ROW_NT)
        d_keys = d_keys + dot(scaled[:, start : start + width], d_scores, ROW_NT)
        d_query = dot(key, d_scores) * HEAD_DIM**-0.5
        hold_s[0, here, start : start + used] = d_query[:, :used].astype(BF)
    hold_s[1, here] = d_keys.astype(BF)
    hold_s[2, here] = d_values.astype(BF)

    @pl.when(odd == 1)
    def _():
        for i in range(3):
            turned = hold_s[i].T
            out_ref[i] = turned
            sum_ref[i] = jnp.sum(turned.astype(F32), 0, keepdims=True)


def attend_backward(qkv, d_mixed, lse, delta, group, first, count, step):
    _, _, inner, _, seq = qkv.shape
    padded = -(-seq // 128) * 128
    part = lambda i: pl.BlockSpec((1, 1, 1, HEAD_DIM, seq), lambda h: (group, i, first + h, 0, 0))
    spec = lambda rows: pl.BlockSpec((1, rows, seq), lambda h: (group * inner + first + h, 0, 0))
    return call(
        functools.partial(attend_back_kernel, seq, padded, step),
        (count,),
        [part(0), part(1), part(2), spec(HEAD_DIM), pl.BlockSpec((1, 1, seq), lambda h: (first + h, 0, 0)), spec(1)],
        [
            pl.BlockSpec((3, seq, 2 * HEAD_DIM), lambda h: (0, 0, h // 2)),
            pl.BlockSpec((3, 1, 2 * HEAD_DIM), lambda h: (0, 0, h // 2)),
        ],
        [shaped((3, seq, count * HEAD_DIM)), shaped((3, 1, count * HEAD_DIM), F32)],
        (qkv, qkv, qkv, d_mixed, lse, delta),
        [
            pltpu.VMEM((seq, 4 * HEAD_DIM), BF),
            pltpu.VMEM((4 * HEAD_DIM, padded), BF),
            pltpu.VMEM((seq, 2 * HEAD_DIM), BF),
            pltpu.VMEM((2 * HEAD_DIM, padded), BF),
            pltpu.VMEM((3, 2 * HEAD_DIM, seq), BF),
        ],
        name="attend_backward",
    )


def mix_kernel(oa_ref, ob_ref, w_ref, out_ref):
    places, cols = w_ref.shape[1:3]
    weights = [row_blocks(w_ref, j, 0, cols) for j in range(places)]
    out_ref[...] = dot(jnp.concatenate([oa_ref[...], ob_ref[...]], 1), jnp.concatenate(weights, 0))


def mix(rows, weights, which):
    seq, wide = rows[0].shape
    owners, places, _, part = weights.shape
    cols = PAIR * wide // places
    half = seq // 2
    return call(
        mix_kernel,
        (2,),
        [
            pl.BlockSpec((half, wide), lambda n: (which, 0)),
            pl.BlockSpec((half, wide), lambda n: (which, 0)),
            pl.BlockSpec((owners // 2, places, cols, part), lambda n: (n, 0, 1, 0)),
        ],
        pl.BlockSpec((half, owners * part // 2), lambda n: (0, n)),
        shaped((half, owners * part), F32),
        (*rows, weights),
        name="mix",
    )


def mix_back_kernel(bits_ref, da_ref, db_ref, w_ref, oa_ref, ob_ref, wa_ref, wb_ref, d_ref, delta_ref, *refs):
    *grad_refs, d_s = refs
    half, width = da_ref.shape
    cols = w_ref.shape[2]
    heads = oa_ref.shape[0]
    group = pl.program_id(0)

    @pl.when(group == 0)
    def _():
        d_s[0:half] = da_ref[...]
        d_s[half:] = db_ref[...]

    places = [PAIR * group + p for p in range(PAIR)]
    weights = jnp.concatenate([row_blocks(w_ref, place, 0, cols) for place in places], 0)
    d_heads = dot(weights, d_s[...], ROW_NT).astype(BF).reshape(oa_ref.shape)
    d_ref[...] = d_heads
    for which, o_ref, wide_ref in ((0, oa_ref, wa_ref), (1, ob_ref, wb_ref)):

        @pl.when(group == which)
        def _():
            delta_ref[...] = jnp.sum(d_heads.astype(F32) * wide_ref[...], 1, keepdims=True)
            grad = dot(o_ref[...].reshape(heads * HEAD_DIM, 2 * half), d_s[...]).astype(BF).T
            for p in range(PAIR):
                part = grad[:, p * cols : (p + 1) * cols]
                put_halves(bits_ref, part, p, grad_refs[2 * p], grad_refs[2 * p + 1], (slice(None), 0))


def mix_back(bits, da, db, weights, mixed, wide):
    half, width = da.shape
    owners, places, _, part = weights.shape
    heads, _, seq = mixed[0].shape
    groups = places // PAIR
    cols = heads * HEAD_DIM // PAIR
    whole = pl.BlockSpec((half, width), lambda g, bits: (0, 0))
    fixed = pl.BlockSpec((heads, HEAD_DIM, seq), lambda g, bits: (0, 0, 0))
    spec = lambda rows: pl.BlockSpec((heads, rows, seq), lambda g, bits: (g, 0, 0))
    grad = pl.BlockSpec((2, 1, width // 4, cols), lambda g, bits: (0, g, 0, 0))
    d_heads, delta, keep_a, send_a, keep_b, send_b = call(
        mix_back_kernel,
        (groups,),
        [whole, whole, pl.BlockSpec((owners, places, cols, part), lambda g, bits: (0, 0, 1, 0))] + [fixed] * 4,
        [spec(HEAD_DIM), spec(1)] + [grad] * 4,
        [shaped((groups * heads, HEAD_DIM, seq)), shaped((groups * heads, 1, seq), F32)]
        + [shaped((2, groups, width // 4, cols))] * 4,
        (bits, da, db, weights, *mixed, *wide),
        [pltpu.VMEM((seq, width), BF)],
        name="mix_back",
        prefetch=1,
    )
    return d_heads, delta, (keep_a, keep_b), (send_a, send_b)


def project_grad_kernel(bits_ref, t_ref, da_ref, db_ref, *refs):
    cols = da_ref.shape[2]
    grad = dot(t_ref[...], jnp.concatenate([da_ref[0], db_ref[0]], 1)).astype(BF)
    for p in range(PAIR):
        put_halves(bits_ref, grad[:, p * cols : (p + 1) * cols], p, refs[2 * p], refs[2 * p + 1], (slice(None), 0))


def project_grads(bits, turned, da, db):
    width, seq = turned.shape
    cols = da.shape[2]
    piece = pl.BlockSpec((1, seq, cols), lambda i, bits: (i, 0, 0))
    grad = pl.BlockSpec((2, 1, width // 4, cols), lambda i, bits: (0, i, 0, 0))
    keep_a, send_a, keep_b, send_b = call(
        project_grad_kernel,
        (3,),
        [pl.BlockSpec((width, seq), lambda i, bits: (0, 0)), piece, piece],
        [grad] * 4,
        [shaped((2, 3, width // 4, cols))] * 4,
        (bits, turned, da, db),
        name="project_grads",
        prefetch=1,
    )
    return (keep_a, keep_b), (send_a, send_b)


def project_back_kernel(a_ref, b_ref, c_ref, d_ref, qk_ref, v_ref, out_ref):
    total = None
    for first, refs in ((0, (a_ref, b_ref)), (PAIR, (c_ref, d_ref))):
        places = [first + p for p in range(PAIR)]
        left = [ref[i] for i in range(3) for ref in refs]
        right = [qk_ref[0, place, i] for i in range(2) for place in places] + [v_ref[0, place] for place in places]
        part = dot(jnp.concatenate(left, 1), jnp.concatenate(right, 0))
        total = part if total is None else total + part
    out_ref[...] = total


def project_back(pieces, w_qk, w_vo, which):
    seq = pieces[0].shape[1]
    owners, places, _, cols, part = w_qk.shape
    half = seq // 2
    return call(
        project_back_kernel,
        (owners,),
        [pl.BlockSpec((3, half, cols), lambda n: (0, which, 0)) for piece in pieces]
        + [
            pl.BlockSpec((1, places, 2, cols, part), lambda n: (turned_owner(n), 0, 0, 0, 0)),
            pl.BlockSpec((1, places, cols, part), lambda n: (n, 0, 0, 0)),
        ],
        pl.BlockSpec((half, part), lambda n: (0, n)),
        shaped((half, owners * part), F32),
        (*pieces, w_qk, w_vo),
        name="project_back",
    )


def gelu_pair(value):
    cdf = 0.5 * (1.0 + lax.erf(value * 0.7071067811865476))
    return value * cdf, cdf + value * (jnp.exp(-0.5 * value * value) * 0.3989422804014327)


def all_blocks(ref):
    return jnp.concatenate([ref[0, t] for t in range(ref.shape[1])], 1)


def relative_block(block, place, blocks):
    return lax.rem(block + blocks - place, blocks)


def either(first_ref, last_ref, index, pick):
    half = first_ref.shape[1]
    one = pick(first_ref, jnp.minimum(index, half - 1))
    return jnp.where(index < half, one, pick(last_ref, jnp.maximum(index - half, 0)))


def ffn_kernel(place_ref, x_ref, one_ref, two_ref, last_ref, b_ref, out_ref, g_ref, slope_ref, hold_s):
    blocks = hold_s.shape[0]
    step = pl.program_id(0)

    @pl.when(step < blocks)
    def _():
        ones = jnp.concatenate([one_ref[turned_owner(owner), 0] for owner in range(one_ref.shape[0])], 0)
        twos = two_ref[...].reshape(ones.shape)
        weights = jnp.where(relative_block(step, place_ref[0], blocks) < blocks // 2, ones, twos)
        pre = dot(x_ref[...], weights) + b_ref[0]
        active, slope = gelu_pair(pre)
        active = active.astype(BF)
        hold_s[step] = active
        g_ref[...] = active
        slope_ref[...] = slope.astype(BF)

    @pl.when(step >= blocks)
    def _():
        left = jnp.concatenate([hold_s[t] for t in range(blocks)], 1)
        out_ref[...] = dot(left, all_blocks(last_ref), ROW_NT)


def ffn_specs(rows, down):
    owners, blocks, part, units = down.shape
    early = lambda s: jnp.minimum(s, blocks - 1)
    late = lambda s: jnp.maximum(s - blocks, 0)
    return (
        blocks,
        early,
        late,
        pl.BlockSpec((rows, owners * part), lambda s, place: (0, 0)),
        pl.BlockSpec((rows, units), lambda s, place: (0, early(s))),
        pl.BlockSpec((1, 1, units), lambda s, place: (early(s), 0, 0)),
        pl.BlockSpec((rows, part), lambda s, place: (0, late(s))),
    )


def ffn_forward(place, x, up, down, bias):
    rows, width = x.shape
    owners, blocks, part, units = down.shape
    blocks, early, late, whole, column, thin, out = ffn_specs(rows, down)
    index = lambda s, place: relative_block(early(s), place[0], blocks)
    return call(
        ffn_kernel,
        (blocks + owners,),
        [
            whole,
            pl.BlockSpec((owners, 1, part, units), lambda s, place: (0, jnp.minimum(index(s, place), PAIR - 1), 0, 0)),
            pl.BlockSpec((owners, 1, part, units), lambda s, place: (0, jnp.maximum(index(s, place) - PAIR, 0), 0, 0)),
            pl.BlockSpec((1, blocks, part, units), lambda s, place: (late(s), 0, 0, 0)),
            thin,
        ],
        [out, column, column],
        [shaped((rows, width), F32), shaped((rows, blocks * units)), shaped((rows, blocks * units))],
        (place, x, *up, down, bias),
        [pltpu.VMEM((blocks, rows, units), BF)],
        name="ffn",
        prefetch=1,
    )


def ffn_back_kernel(place_ref, d_ref, first_ref, one_ref, two_ref, slope_ref, out_ref, dpre_ref, sum_ref, hold_s):
    blocks = hold_s.shape[0]
    step = pl.program_id(0)

    @pl.when(step < blocks)
    def _():
        d_pre = (dot(d_ref[...], first_ref[...].reshape(d_ref.shape[1], -1)) * slope_ref[...].astype(F32)).astype(BF)
        hold_s[step] = d_pre
        dpre_ref[...] = d_pre
        sum_ref[0] = jnp.sum(d_pre.astype(F32), 0, keepdims=True)

    @pl.when(step >= blocks)
    def _():
        left = jnp.concatenate([hold_s[t] for t in range(blocks)], 1)
        order = [relative_block(t, place_ref[0], blocks) for t in range(blocks)]
        weights = [either(one_ref, two_ref, index, lambda ref, i: ref[0, i]) for index in order]
        out_ref[...] = dot(left, jnp.concatenate(weights, 1), ROW_NT)


def ffn_backward(place, d_out, up, down, slope):
    rows, width = d_out.shape
    owners, blocks, part, units = down.shape
    blocks, early, late, whole, column, thin, out = ffn_specs(rows, down)
    return call(
        ffn_back_kernel,
        (blocks + owners,),
        [
            whole,
            pl.BlockSpec((owners, 1, part, units), lambda s, place: (0, early(s), 0, 0)),
            pl.BlockSpec((1, PAIR, part, units), lambda s, place: (turned_owner(late(s)), 0, 0, 0)),
            pl.BlockSpec((1, PAIR, part, units), lambda s, place: (late(s), 0, 0, 0)),
            column,
        ],
        [out, column, thin],
        [shaped((rows, width), F32), shaped((rows, blocks * units)), shaped((blocks, 1, units), F32)],
        (place, d_out, down, *up, slope),
        [pltpu.VMEM((blocks, rows, units), BF)],
        name="ffn_backward",
        prefetch=1,
    )


def put_halves(bits_ref, grad, which, keep_ref, send_ref, at):
    grad = grad.reshape((2, 2, grad.shape[0] // 4) + grad.shape[1:])
    pair = (grad[:, 0], grad[:, 1]) if which == 0 else (grad[0], grad[1])
    low = bits_ref[which] == 0
    keep_ref[at] = jnp.where(low, pair[0], pair[1])
    send_ref[at] = jnp.where(low, pair[1], pair[0])


def ffn_grad_kernel(bits_ref, xa_ref, xb_ref, ca_ref, cb_ref, keep_a, send_a, keep_b, send_b, x_s):
    step = pl.program_id(0)

    @pl.when(step == 0)
    def _():
        x_s[...] = jnp.concatenate([xa_ref[...], xb_ref[...]], 0).T

    column = jnp.concatenate([ca_ref[...], cb_ref[...]], 0)
    grad = dot(x_s[...], column).astype(BF)

    @pl.when(step < PAIR)
    def _():
        put_halves(bits_ref, grad, 0, keep_a, send_a, (slice(None), 0))

    @pl.when(step >= PAIR)
    def _():
        put_halves(bits_ref, grad, 1, keep_b, send_b, (slice(None), 0))


def ffn_grad(bits, xa, xb, ca, cb, blocks):
    rows, width = xa.shape
    units = ca.shape[1] // blocks
    whole = pl.BlockSpec((rows, width), lambda t, bits: (0, 0))
    column = pl.BlockSpec((rows, units), lambda t, bits: (0, t))
    first = pl.BlockSpec((2, 1, width // 4, units), lambda t, bits: (0, jnp.minimum(t, PAIR - 1), 0, 0))
    last = pl.BlockSpec((2, 1, width // 4, units), lambda t, bits: (0, jnp.maximum(t - PAIR, 0), 0, 0))
    keep_a, send_a, keep_b, send_b = call(
        ffn_grad_kernel,
        (blocks,),
        [whole, whole, column, column],
        [first, first, last, last],
        [shaped((2, PAIR, width // 4, units))] * 4,
        (bits, xa, xb, ca, cb),
        [pltpu.VMEM((width, 2 * rows), BF)],
        name="ffn_grad",
        prefetch=1,
    )
    return (keep_a, keep_b), (send_a, send_b)


def swap(value, axis):
    return lax.ppermute(value, axis, [(0, 1), (1, 0)])


def after(value, *others):
    return lax.optimization_barrier((value, *others))[0]


def together(*values):
    return lax.optimization_barrier(values)


def ordered(bit, mine, other, axis):
    return jnp.concatenate([jnp.where(bit == 0, mine, other), jnp.where(bit == 0, other, mine)], axis)


def chosen(value, bit, axis):
    return lax.dynamic_index_in_dim(value, bit, axis, keepdims=False)


def added(mine, other):
    return (mine.astype(F32) + other.astype(F32)).astype(BF)


def moments(value):
    mean = jnp.mean(value, -1, keepdims=True)
    centred = value - mean
    scale = lax.rsqrt(jnp.mean(centred * centred, -1, keepdims=True) + EPS)
    return centred, scale


def norm_back(d_value, centred, scale, gain):
    unit = centred * scale
    d_unit = d_value * gain
    grad_in = scale * (d_unit - jnp.mean(d_unit, -1, keepdims=True) - unit * jnp.mean(d_unit * unit, -1, keepdims=True))
    return grad_in, jnp.sum(d_value * unit, 0), jnp.sum(d_value, 0)


def clip_local(clips, w_qkv, w_out, w_up, w_down, norm_gain, shifts, bias_qv, up_bias, teacher):
    y, x, c, t = (lax.axis_index(name) for name in ("y", "x", "c", "t"))
    every = ("y", "x", "c", "t")
    steps = 4
    width = clips.shape[2]
    odd = t % 2

    first_way, second_way = [], []
    for column in range(4):
        for core in range(2):
            for place in range(4):
                source = (column * 2 + core) * 4 + place
                to = (column * 2 + place // 2) * 4 + 2 * core
                first_way.append((source, to + place % 2))
                second_way.append((source, to + 1 - place % 2))
    first_way = [(a, b) for a, b in first_way if a != b]
    back = lambda way: [(b, a) for a, b in way]
    stays = t // 2 == c

    def sent(pair):
        return lax.ppermute(pair[0], every, first_way), lax.ppermute(pair[1], every, second_way)

    def to_chip(value):
        return sent((chosen(value, odd, 0), chosen(value, 1 - odd, 0)))

    def from_chip(value):
        half = value.shape[0] // 2
        return lax.ppermute(value[:half], every, back(first_way)), lax.ppermute(value[half:], every, back(second_way))

    rings = [[(i, (i + away) % steps) for i in range(steps)] for away in range(steps)]

    def ring_gather(value):
        return tuple(lax.ppermute(value, "t", rings[-j % steps]) for j in range(1, steps))

    def ring_scatter(blocks):
        return tuple(lax.ppermute(blocks[j], "t", rings[j]) for j in range(1, steps))

    def placed(value, axis):
        return lax.dynamic_slice_in_dim(jnp.concatenate([value, value], axis), steps - t, steps, axis)

    def on_chip(value, near, far):
        return jnp.concatenate([jnp.where(stays, chosen(value, odd, 0), near), far])

    def as_clips(value, near, far):
        near = jnp.where(stays, value[: value.shape[0] // 2], near)
        return jnp.stack([jnp.where(odd == 0, near, far), jnp.where(odd == 0, far, near)])

    def scatter_start(sends):
        return swap(sends[0], "x"), swap(sends[1], "y")

    def sums_of(keeps, parts, row, column):
        pick = lambda values, bit: jnp.concatenate([chosen(value, bit, 0) for value in values])
        first = pick(keeps[0], row).astype(F32) + chosen(parts[0], row, 0).astype(F32)
        return first, pick(keeps[1], column).astype(F32) + chosen(parts[1], column, 0).astype(F32)

    def scatter_middle(keeps, parts):
        first, second = sums_of(keeps, parts, 1 - y, 1 - x)
        return swap(first.astype(BF), "y"), swap(second.astype(BF), "x")

    def scatter_end(keeps, parts, ends):
        first, second = sums_of(keeps, parts, y, x)
        return (first + ends[0].astype(F32)).astype(BF), (second + ends[1].astype(F32)).astype(BF)

    dims = w_qkv.shape[1]
    cols = w_out.shape[0] // 2
    lane = bias_qv.shape[1]
    units = w_up.shape[1] // 2
    attn = jnp.concatenate([jnp.swapaxes(w_qkv, 1, 2), w_out[None]]).reshape(4, 2, cols, dims)
    mine, other = chosen(attn, c, 1).reshape(4 * cols, dims), chosen(attn, 1 - c, 1).reshape(4 * cols, dims)
    attn_piece = ordered(c, mine, swap(other, "c"), 1)
    ff = jnp.stack([w_up, w_down.T]).reshape(2, dims, 2, units)
    ff_piece = ordered(c, chosen(ff, c, 2), swap(chosen(ff, 1 - c, 2), "c"), 1)

    pad = lambda value: jnp.pad(value, (0, dims - value.shape[0]))[None]
    tails = jnp.concatenate([pad(bias_qv[0]), pad(bias_qv[1]), pad(up_bias), jnp.zeros((7, dims), BF)])
    vectors = jnp.concatenate([norm_gain, shifts, tails])
    for bit, name in ((c, "c"), (x, "x"), (y, "y")):
        vectors = ordered(bit, vectors, swap(vectors, name), 1)
    gains, shift_all = vectors[0:2].astype(F32), vectors[2:6].astype(F32)
    tails = vectors[6:16]
    tails = jnp.stack([part[:3] for part in (tails, *ring_gather(tails))]).astype(F32)
    tails = lax.dynamic_slice_in_dim(tails, 4 * dims * c, 4 * dims, 2)
    pair = tails[:, :2].reshape(steps, 2, 4, dims)[..., :lane]
    bias_pair = jnp.swapaxes(pair, 0, 1).reshape(2, 2, 2 * cols)
    bias_in = jnp.stack([bias_pair[0], jnp.zeros_like(bias_pair[0]), bias_pair[1]], 1)[..., None]
    up_shift = placed(tails[:, 2:3], 0)

    whole = ("y", "x", "t")
    attn_rows = together(*ring_gather(attn_piece))
    near, far = to_chip(after(clips, attn_rows))
    attn_rows = (attn_piece, *attn_rows)
    qk_rows = jnp.stack([part[: 2 * cols] for part in attn_rows])
    vo_rows = jnp.stack([part[2 * cols :] for part in attn_rows])
    targets = chosen(teacher, odd, 0), chosen(teacher, 1 - odd, 0)
    swapped, near, targets, bias_in, up_shift = together(
        (swap(qk_rows, "y"), swap(vo_rows, "x")), near, targets, bias_in, up_shift
    )
    w_qk, w_vo = ordered(y, qk_rows[None], swapped[0][None], 0), ordered(x, vo_rows[None], swapped[1][None], 0)
    swapped, far = together((swap(w_qk, "x"), swap(w_vo, "y")), far)
    w_qk = ordered(x, w_qk[None], swapped[0][None], 0).reshape(4, steps, 2, cols, 2 * dims)
    w_vo = ordered(y, w_vo[None], swapped[1][None], 0).reshape(4, steps, 2 * cols, 2 * dims)
    up_piece, down_piece = ff_piece
    up_piece, down_piece, far = together(up_piece, down_piece, far)
    up_rows = ring_gather(up_piece)
    down_all = lax.all_gather(down_piece, whole, axis=0, tiled=False).reshape(4, steps, 2 * dims, units)
    place = t.reshape(1)

    inputs = on_chip(clips, near, far).astype(F32)
    centred_one, scale_one = moments(inputs)
    first = (centred_one * scale_one * gains[0] + shift_all[0]).astype(BF)
    first_other = swap(first, "c")
    qkv, turned = project(first, first_other, w_qk, w_vo, bias_in)
    mixed_a, rows_a, wide_a, lse_a = attend(qkv, 0, 1664)
    up_rows, rows_a = together(up_rows, rows_a)
    up_a, up_b = jnp.stack([up_piece, up_rows[0]]), jnp.stack(up_rows[1:])
    swapped = swap(up_a, "y"), swap(up_b, "x")
    mixed_b, rows_b, wide_b, lse_b = attend(after(qkv, rows_a), 1, 1664)
    swapped, rows_b = together(swapped, rows_b)
    up_a, up_b = ordered(y, up_a[None], swapped[0][None], 0), ordered(x, up_b[None], swapped[1][None], 0)
    swapped = swap(up_a, "x"), swap(up_b, "y")
    rows = (rows_a, rows_b)
    attn_other = mix(rows, w_vo, 1)
    attn_mine = mix((after(rows_a, attn_other), rows_b), w_vo, 0)
    hidden = inputs + (attn_mine + swap(attn_other, "c")) + shift_all[2]

    centred_two, scale_two = moments(hidden)
    second = (centred_two * scale_two * gains[1] + shift_all[1]).astype(BF)
    second_other = swap(second, "c")
    swapped, second = together(swapped, second)
    up_a = ordered(x, up_a[None], swapped[0][None], 0).reshape(4, PAIR, 2 * dims, units)
    up_b = ordered(y, up_b[None], swapped[1][None], 0).reshape(4, PAIR, 2 * dims, units)
    up_all = up_a, up_b
    targets, second, down_all = together(targets, second, down_all)
    near, far = sent(targets)
    out_mine, act_mine, slope_mine = ffn_forward(place, second, up_all, down_all, up_shift)
    out_mine, near = together(out_mine, near)
    out_other, act_other, slope_other = ffn_forward(place, after(second_other, near), up_all, down_all, up_shift)
    out_other, far = together(out_other, far)
    output = hidden + (out_mine + swap(out_other, "c")) + shift_all[3]
    d_out = output - on_chip(teacher, near, far).astype(F32)
    d_ffn = d_out.astype(BF)
    d_ffn_other = swap(d_ffn, "c")
    d_second, d_pre, sum_mine = ffn_backward(place, d_ffn, up_all, down_all, slope_mine)
    d_ffn_other, d_pre = together(d_ffn_other, d_pre)
    d_second_other, d_pre_other, sum_other = ffn_backward(place, d_ffn_other, up_all, down_all, slope_other)
    d_second_swapped = swap(d_second_other, "c")
    up_sum = (sum_mine + sum_other).reshape(steps, units)

    bits = jnp.stack([x, y])
    grad_down, sends = ffn_grad(bits, after(d_ffn, d_pre_other), d_ffn_other, act_mine, act_other, steps)
    down = scatter_start(sends)
    result, grad_down = together(output.astype(BF), grad_down)
    out_near, out_far = from_chip(result)
    d_second_swapped, grad_down = together(d_second_swapped, grad_down)
    d_second = d_second + d_second_swapped
    d_norm, grad_gain_two, grad_shift_two = norm_back(d_second, centred_two, scale_two, gains[1])
    d_hidden = d_out + d_norm
    d_attn = d_hidden.astype(BF)
    d_attn_other = swap(d_attn, "c")
    grad_up, sends = ffn_grad(bits, after(second, d_attn), second_other, d_pre, d_pre_other, steps)
    up = scatter_start(sends)
    d_attn_other, grad_up = together(d_attn_other, grad_up)

    d_heads, delta, grad_o, sends_o = mix_back(bits, d_attn, d_attn_other, w_vo, (mixed_a, mixed_b), (wide_a, wide_b))
    down, delta = together(down, delta)
    grad_down, grad_up = [[keep] for keep in grad_down], [[keep] for keep in grad_up]
    down_ends = scatter_middle(grad_down, down)
    back_a, sum_a = attend_backward(qkv, d_heads, lse_b, delta, 1, 0, 2, 256)
    up, out_near, back_a = together(up, out_near, back_a)
    up_ends = scatter_middle(grad_up, up)
    back_b, sum_b = attend_backward(qkv, after(d_heads, back_a), lse_b, delta, 1, 2, 2, 256)
    up_ends, down_ends, out_far, back_b = together(up_ends, down_ends, out_far, back_b)
    ups, downs = scatter_end(grad_up, up, up_ends), scatter_end(grad_down, down, down_ends)
    grad_ff = jnp.concatenate([jnp.stack(pair, 1) for pair in zip(ups, downs)]).reshape(steps * 4 * dims, units)
    ff_total = lax.psum_scatter(grad_ff, "t", scatter_dimension=0, tiled=True)
    grad_one, sends = project_grads(bits, turned, back_a, back_b)
    one = scatter_start([jnp.concatenate(pair, 1) for pair in zip(sends, sends_o)])
    grad_one = list(zip(grad_one, grad_o))
    delta, grad_ff, grad_one = together(delta, grad_ff, grad_one)
    back_c, sum_c = attend_backward(qkv, after(d_heads, back_b), lse_a, delta, 0, 2, 2, 256)
    one, back_c = together(one, back_c)
    one_ends = scatter_middle(grad_one, one)
    back_d, sum_d = attend_backward(qkv, after(d_heads, back_c), lse_a, delta, 0, 0, 2, 256)
    one_ends, back_d = together(one_ends, back_d)
    grad_two, sends = project_grads(bits, turned, back_d, back_c)
    two = scatter_start(sends)
    pieces = (back_d, back_c, back_a, back_b)
    d_first_other = project_back(pieces, w_qk, after(w_vo, grad_two), 1)
    d_first_swapped = swap(d_first_other, "c")
    one = scatter_end(grad_one, one, one_ends)
    early = [lax.ppermute(jnp.concatenate([one[p][:3], one[p][4:]]), "t", rings[PAIR + p]) for p in range(PAIR)]
    two, d_first_other = together(two, d_first_other)
    two_ends = scatter_middle([[keep] for keep in grad_two], two)
    d_first = project_back(pieces, w_qk, after(w_vo, d_first_other), 0)
    ff_total, early, d_first = together(ff_total, early, d_first)
    d_first_swapped, d_first = together(d_first_swapped, d_first)
    d_first = d_first + d_first_swapped
    d_norm, grad_gain_one, grad_shift_one = norm_back(d_first, centred_one, scale_one, gains[0])
    d_inputs = (d_hidden + d_norm).astype(BF)
    grad_near, grad_far = from_chip(d_inputs)
    small = (sum_a, sum_b, sum_c, sum_d, up_sum, grad_gain_one, grad_shift_one)
    two_ends, small, grad_near, out_near, out_far = together(two_ends, small, grad_near, out_near, out_far)
    sum_a, sum_b, sum_c, sum_d, up_sum, grad_gain_one, grad_shift_one = small
    two = scatter_end([[keep] for keep in grad_two], two, two_ends)
    late = lax.ppermute(jnp.concatenate([two[1], one[1][3:4]]), "t", rings[1])

    grad_ff = ff_total.astype(F32).reshape(2, 2, dims, units)
    grad_ff = ordered(c, chosen(grad_ff, c, 1), swap(chosen(grad_ff, 1 - c, 1), "c"), 2)
    grad_attn = jnp.concatenate([two[0], one[0][3:4]]).astype(F32)
    grad_attn = sum((part.astype(F32) for part in (*early, late)), grad_attn).reshape(4, 2, dims, cols)
    grad_attn = ordered(c, chosen(grad_attn, c, 1), swap(chosen(grad_attn, 1 - c, 1), "c"), 2)

    heads_sum = jnp.concatenate([sum_d, sum_c, sum_a, sum_b], 2).reshape(3, steps, 4, lane)
    heads_sum = placed(jnp.stack([heads_sum[0], heads_sum[2]]), 1)
    heads_sum = jnp.pad(heads_sum, ((0, 0), (0, 0), (0, 0), (0, dims - lane))).reshape(2 * steps, 4 * dims)
    own = jnp.concatenate([heads_sum, up_sum])
    own = jnp.concatenate([jnp.where(c == 0, own, 0.0), jnp.where(c == 1, own, 0.0)], 1)
    normed = jnp.stack([grad_gain_one, grad_gain_two, grad_shift_one, grad_shift_two, jnp.sum(d_hidden, 0), jnp.sum(d_out, 0)])
    sums = jnp.concatenate([normed, jnp.zeros((2, width), F32), own])
    for bit, name in ((y, "y"), (x, "x"), (c, "c")):
        half = sums.shape[1] // 2
        part = lambda which: lax.dynamic_slice_in_dim(sums, which * half, half, 1)
        sums = part(bit) + swap(part(1 - bit), name)
    sums = sum((lax.ppermute(sums, "t", rings[away]) for away in range(1, steps)), sums)
    thin = width // 32
    vector_sums = lax.dynamic_slice_in_dim(sums[:6], thin * t, thin, 1)
    place_sums = lax.dynamic_index_in_dim(sums[8:].reshape(3, steps, dims), t, 1, keepdims=False)
    return (
        as_clips(result, out_near, out_far),
        as_clips(d_inputs, grad_near, grad_far),
        grad_attn[:3],
        grad_attn[3].T,
        grad_ff[0],
        grad_ff[1].T,
        vector_sums[:2],
        vector_sums[2:],
        place_sums[:2, :lane],
        place_sums[2],
    )


def clip_per_chip(mesh):
    fine = Mesh(mesh.devices.reshape(2, 2, 2, 4), ("y", "x", "c", "t"))
    dp = ("y", "x", "c")
    in_specs = (
        P(dp, "t", None),
        P(None, dp, "t"),
        P("t", dp),
        P(dp, "t"),
        P("t", dp),
        P(None, dp),
        P(None, dp),
        P(None, ("t",) + dp),
        P(("t",) + dp),
        P(dp, "t", None),
    )
    out_specs = in_specs[:1] * 2 + in_specs[1:5] + (
        P(None, dp + ("t",)),
        P(None, dp + ("t",)),
        P(None, ("t",) + dp),
        P(("t",) + dp),
    )
    return jax.shard_map(clip_local, mesh=fine, in_specs=in_specs, out_specs=out_specs, check_vma=False)


def solution(mesh):
    if dict(mesh.shape) == {"dp": 8, "tensor": 4}:
        return clip_per_chip(mesh)
    in_specs = (
        P("dp", "tensor", None),
        P(None, "dp", "tensor"),
        P("tensor", "dp"),
        P("dp", "tensor"),
        P("tensor", "dp"),
        P(None, "dp"),
        P(None, "dp"),
        P(None, ("tensor", "dp")),
        P(("tensor", "dp")),
        P("dp", "tensor", None),
    )
    out_specs = (
        P("dp", "tensor", None),
        P("dp", "tensor", None),
        P(None, "dp", "tensor"),
        P("tensor", "dp"),
        P("dp", "tensor"),
        P("tensor", "dp"),
        P(None, ("dp", "tensor")),
        P(None, ("dp", "tensor")),
        P(None, ("tensor", "dp")),
        P(("tensor", "dp")),
    )
    return jax.shard_map(local, mesh=mesh, in_specs=in_specs, out_specs=out_specs, check_vma=False)
```

```python
import functools

import jax
import jax.numpy as jnp
from jax import lax
from jax.experimental import pallas as pl
from jax.experimental.pallas import tpu as pltpu
from jax.sharding import Mesh, PartitionSpec as P

HEAD_DIM = 64


EPS = 1e-05


def layer_norm(value, gain, shift):
    mean = jnp.mean(value, -1, keepdims=True)
    centred = value - mean
    spread = jnp.mean(centred * centred, -1, keepdims=True)
    return centred * lax.rsqrt(spread + EPS) * gain + shift


def exact_gelu(value):
    return jax.nn.gelu(value, approximate=False)


def attend_clip(query, keys, values, scale):
    scores = jnp.einsum("qhe,khe->hqk", query, keys, preferred_element_type=jnp.float32) * scale
    top = jnp.max(scores, -1, keepdims=True)
    expd = jnp.exp(scores - top)
    total = jnp.sum(expd, -1, keepdims=True)
    prob = (expd / total).astype(jnp.bfloat16)
    mixed = jnp.einsum("hqk,khe->qhe", prob, values, preferred_element_type=jnp.float32)
    return (mixed.astype(jnp.bfloat16), (top + jnp.log(total))[..., 0])


def attend_back(query, keys, values, d_mixed, logsum, scale):
    scores = jnp.einsum("qhe,khe->hqk", query, keys, preferred_element_type=jnp.float32) * scale
    prob = jnp.exp(scores - logsum[:, :, None])
    d_prob = jnp.einsum("qhe,khe->hqk", d_mixed, values, preferred_element_type=jnp.float32)
    delta = jnp.sum(d_prob * prob, -1, keepdims=True)
    d_scores = (prob * (d_prob - delta)).astype(jnp.bfloat16)
    d_values = jnp.einsum(
        "hqk,qhe->khe", prob.astype(jnp.bfloat16), d_mixed, preferred_element_type=jnp.float32
    )
    d_query = jnp.einsum("hqk,khe->qhe", d_scores, keys, preferred_element_type=jnp.float32) * scale
    d_keys = jnp.einsum("hqk,qhe->khe", d_scores, query, preferred_element_type=jnp.float32) * scale
    return jnp.stack([d_query, d_keys, d_values]).astype(jnp.bfloat16)


def local(clips, w_qkv, w_out, w_up, w_down, norm_gain, shifts, bias_qv, up_bias, teacher):
    wq, wo, wu, wd, gains, shift_all, bias_pair, up_shift = (
        lax.all_gather(w_qkv, "dp", axis=1, tiled=True),
        lax.all_gather(w_out, "dp", axis=1, tiled=True),
        lax.all_gather(w_up, "dp", axis=0, tiled=True),
        lax.all_gather(w_down, "dp", axis=1, tiled=True),
        lax.all_gather(norm_gain, "dp", axis=1, tiled=True),
        lax.all_gather(shifts, "dp", axis=1, tiled=True),
        lax.all_gather(bias_qv, "dp", axis=1, tiled=True),
        lax.all_gather(up_bias, "dp", axis=0, tiled=True),
    )
    gains = gains.astype(jnp.float32)
    shift_all = shift_all.astype(jnp.float32)
    bias_pair = bias_pair.astype(jnp.float32)
    up_shift = up_shift.astype(jnp.float32)
    width = wq.shape[2]
    heads_here = width // HEAD_DIM
    scale = HEAD_DIM ** (-0.5)
    inputs = jnp.swapaxes(clips, 0, 1).astype(jnp.float32)
    first = layer_norm(inputs, gains[0], shift_all[0]).astype(jnp.bfloat16)
    whole_first = lax.all_gather(first, "tensor", axis=0, tiled=True)
    seq = whole_first.shape[0]
    count = whole_first.shape[1]
    projected = jnp.einsum("scd,kde->ksce", whole_first, wq, preferred_element_type=jnp.float32)
    qkv_bias = jnp.stack([bias_pair[0], jnp.zeros_like(bias_pair[0]), bias_pair[1]])
    qkv = (projected + qkv_bias[:, None, None, :]).astype(jnp.bfloat16)

    def heads(value):
        return jnp.swapaxes(value, 0, 1).reshape(count, seq, heads_here, HEAD_DIM)

    query_h, keys_h, values_h = (heads(qkv[0]), heads(qkv[1]), heads(qkv[2]))
    attended, logsum = lax.map(
        lambda item: attend_clip(item[0], item[1], item[2], scale), (query_h, keys_h, values_h)
    )
    mixed = jnp.swapaxes(attended.reshape(count, seq, width), 0, 1)
    piece = mixed
    attn = lax.psum_scatter(
        jnp.einsum("scd,de->sce", piece, wo, preferred_element_type=jnp.float32),
        "tensor",
        scatter_dimension=0,
        tiled=True,
    )
    hidden = inputs + attn + shift_all[2]
    second = layer_norm(hidden, gains[1], shift_all[1]).astype(jnp.bfloat16)
    whole_second = lax.all_gather(second, "tensor", axis=0, tiled=True)
    pre = jnp.einsum("scd,df->scf", whole_second, wu, preferred_element_type=jnp.float32) + up_shift
    active = exact_gelu(pre).astype(jnp.bfloat16)
    piece = active
    ffn = lax.psum_scatter(
        jnp.einsum("scf,fe->sce", piece, wd, preferred_element_type=jnp.float32),
        "tensor",
        scatter_dimension=0,
        tiled=True,
    )
    output = hidden + ffn + shift_all[3]
    d_out = output - jnp.swapaxes(teacher, 0, 1).astype(jnp.float32)
    whole_d_ffn = lax.all_gather(d_out.astype(jnp.bfloat16), "tensor", axis=0, tiled=True)
    d_active = jnp.einsum("sce,fe->scf", whole_d_ffn, wd, preferred_element_type=jnp.float32)
    grad_down = jnp.einsum("scf,sce->fe", active, whole_d_ffn, preferred_element_type=jnp.float32)
    gelu_value, gelu_back = jax.vjp(exact_gelu, pre)
    d_pre = gelu_back(d_active)[0].astype(jnp.bfloat16)
    grad_up_shift = jnp.sum(d_pre.astype(jnp.float32), (0, 1))
    grad_up = jnp.einsum("scd,scf->df", whole_second, d_pre, preferred_element_type=jnp.float32)
    piece = d_pre
    d_second = lax.psum_scatter(
        jnp.einsum("scf,df->scd", piece, wu, preferred_element_type=jnp.float32),
        "tensor",
        scatter_dimension=0,
        tiled=True,
    )
    norm_value, second_back = jax.vjp(layer_norm, hidden, gains[1], shift_all[1])
    d_hidden_norm, grad_gain_two, grad_shift_two = second_back(d_second)
    d_hidden = d_out + d_hidden_norm
    whole_d_attn = lax.all_gather(d_hidden.astype(jnp.bfloat16), "tensor", axis=0, tiled=True)
    d_mixed = jnp.einsum(
        "sce,de->scd", whole_d_attn, wo, preferred_element_type=jnp.float32
    ).astype(jnp.bfloat16)
    grad_out = jnp.einsum("scd,sce->de", mixed, whole_d_attn, preferred_element_type=jnp.float32)
    d_heads = jnp.swapaxes(d_mixed, 0, 1).reshape(count, seq, heads_here, HEAD_DIM)
    d_stacked = lax.map(
        lambda item: attend_back(item[0], item[1], item[2], item[3], item[4], scale),
        (query_h, keys_h, values_h, d_heads, logsum),
    )
    d_qkv = jnp.transpose(d_stacked.reshape(count, 3, seq, width), (1, 2, 0, 3))
    bias_sums = jnp.sum(d_qkv.astype(jnp.float32), (1, 2))
    grad_pair = jnp.stack([bias_sums[0], bias_sums[2]])
    grad_qkv = jnp.einsum("scd,ksce->kde", whole_first, d_qkv, preferred_element_type=jnp.float32)
    piece = d_qkv
    d_first = lax.psum_scatter(
        jnp.einsum("ksce,kde->scd", piece, wq, preferred_element_type=jnp.float32),
        "tensor",
        scatter_dimension=0,
        tiled=True,
    )
    first_value, first_back = jax.vjp(layer_norm, inputs, gains[0], shift_all[0])
    d_in_norm, grad_gain_one, grad_shift_one = first_back(d_first)
    d_inputs = d_hidden + d_in_norm
    sums = (
        lax.psum_scatter(grad_qkv, "dp", scatter_dimension=1, tiled=True),
        lax.psum_scatter(grad_out, "dp", scatter_dimension=1, tiled=True),
        lax.psum_scatter(grad_up, "dp", scatter_dimension=0, tiled=True),
        lax.psum_scatter(grad_down, "dp", scatter_dimension=1, tiled=True),
        lax.psum_scatter(grad_pair, "dp", scatter_dimension=1, tiled=True),
        lax.psum_scatter(grad_up_shift, "dp", scatter_dimension=0, tiled=True),
    )
    grad_gain = jnp.stack([grad_gain_one, grad_gain_two])
    grad_shift = jnp.stack(
        [grad_shift_one, grad_shift_two, jnp.sum(d_hidden, (0, 1)), jnp.sum(d_out, (0, 1))]
    )
    norm_sums = (
        lax.psum_scatter(grad_gain, ("dp", "tensor"), scatter_dimension=1, tiled=True),
        lax.psum_scatter(grad_shift, ("dp", "tensor"), scatter_dimension=1, tiled=True),
    )
    result = jnp.swapaxes(output, 0, 1).astype(jnp.bfloat16)
    grad_in = jnp.swapaxes(d_inputs, 0, 1).astype(jnp.bfloat16)
    return (
        result,
        grad_in,
        sums[0],
        sums[1],
        sums[2],
        sums[3],
        norm_sums[0],
        norm_sums[1],
        sums[4],
        sums[5],
    )


BF = jnp.bfloat16
F32 = jnp.float32
LOG2E = 1.4426950408889634
VMEM_LIMIT = 56 * 2**20
ROW_NN = (((1,), (0,)), ((), ()))
ROW_NT = (((1,), (1,)), ((), ()))
PAIR = 2


def dot(left, right, dims=ROW_NN):
    return lax.dot_general(left, right, dims, preferred_element_type=F32)


def call(body, grid, in_specs, out_specs, out_shape, args, scratch=(), name=None, prefetch=0):
    return pl.pallas_call(
        body,
        grid_spec=pltpu.PrefetchScalarGridSpec(
            num_scalar_prefetch=prefetch, grid=grid, in_specs=in_specs, out_specs=out_specs, scratch_shapes=list(scratch)
        ),
        out_shape=out_shape,
        compiler_params=pltpu.CompilerParams(vmem_limit_bytes=VMEM_LIMIT),
        cost_estimate=pl.CostEstimate(flops=1000, bytes_accessed=1000, transcendentals=0),
        name=name,
    )(*args)


def shaped(shape, dtype=BF):
    return jax.ShapeDtypeStruct(shape, dtype)


def three_parts(value):
    high = value.astype(BF)
    rest = value - high.astype(F32)
    middle = rest.astype(BF)
    return high, middle, (rest - middle.astype(F32)).astype(BF)


def query_blocks(seq, step):
    blocks = []
    start = 0
    while start < seq:
        used = min(step, seq - start)
        blocks.append((start, -(-used // 128) * 128, used))
        start += used
    return blocks


def pad_columns(value, width):
    extra = width - value.shape[1]
    if extra == 0:
        return value
    return jnp.concatenate([value, jnp.zeros((value.shape[0], extra), value.dtype)], 1)


def row_blocks(ref, place, start, stop):
    return jnp.concatenate([ref[owner, place, start:stop] for owner in range(ref.shape[0])], 1)


def turned_owner(owner):
    return owner % 2 * 2 + owner // 2


def key_blocks(ref, place, which):
    return jnp.concatenate([ref[turned_owner(owner), place, which] for owner in range(ref.shape[0])], 1)


def project_kernel(xa_ref, xb_ref, qk_ref, v_ref, b_ref, out_ref, t_ref, x_s):
    half = xa_ref.shape[0]
    group = pl.program_id(0)

    @pl.when(group == 0)
    def _():
        x_s[0:half] = xa_ref[...]
        x_s[half:] = xb_ref[...]
        t_ref[...] = x_s[...].T

    cols = v_ref.shape[2]
    places = [PAIR * group + p for p in range(PAIR)]
    for i in range(3):
        pick = (lambda place: row_blocks(v_ref, place, 0, cols)) if i == 2 else (lambda place: key_blocks(qk_ref, place, i))
        weights = jnp.concatenate([pick(place) for place in places], 0)
        value = dot(weights, x_s[...], ROW_NT) + b_ref[0, i]
        out_ref[0, i] = value.astype(BF).reshape(out_ref.shape[2:])


def project(xa, xb, w_qk, w_vo, bias):
    half, width = xa.shape
    owners, places, _, cols, part = w_qk.shape
    groups = places // PAIR
    heads = PAIR * cols // HEAD_DIM
    whole = pl.BlockSpec((half, width), lambda g: (0, 0))
    return call(
        project_kernel,
        (groups,),
        [
            whole,
            whole,
            pl.BlockSpec((owners, places, 2, cols, part), lambda g: (0, 0, 0, 0, 0)),
            pl.BlockSpec((owners, places, cols, part), lambda g: (0, 0, 0, 0)),
            pl.BlockSpec((1, 3, PAIR * cols, 1), lambda g: (g, 0, 0, 0)),
        ],
        [
            pl.BlockSpec((1, 3, heads, HEAD_DIM, 2 * half), lambda g: (g, 0, 0, 0, 0)),
            pl.BlockSpec((width, 2 * half), lambda g: (0, 0)),
        ],
        [shaped((groups, 3, heads, HEAD_DIM, 2 * half)), shaped((width, 2 * half))],
        (xa, xb, w_qk, w_vo, bias),
        [pltpu.VMEM((2 * half, width), BF)],
        name="project",
    )


def attend_kernel(seq, padded, step, q_ref, k_ref, v_ref, o_ref, row_ref, wide_ref, lse_ref, key_s, query_s, value_s, hold_s):
    key = k_ref[0, 0, 0]
    key_s[...] = jnp.concatenate([key, key, key, jnp.zeros((HEAD_DIM, seq), BF)], 0).T
    parts = three_parts(pad_columns(q_ref[0, 0, 0].astype(F32) * (LOG2E * HEAD_DIM**-0.5), padded))
    query_s[...] = jnp.concatenate([*parts, jnp.zeros((HEAD_DIM, padded), BF)], 0)
    value_s[0:HEAD_DIM] = v_ref[0, 0, 0]
    value_s[HEAD_DIM : HEAD_DIM + 16] = jnp.ones((16, seq), BF)
    for start, width, used in query_blocks(seq, step):
        scores = dot(key_s[...], query_s[:, start : start + width])
        top = jnp.max(scores, 0, keepdims=True)
        prob = jnp.exp2(scores - top).astype(BF)
        mixed = dot(value_s[...], prob)
        total = mixed[HEAD_DIM : HEAD_DIM + 1]
        result = (mixed[0:HEAD_DIM] * (1.0 / total))[:, :used]
        wide_ref[0, :, start : start + used] = result
        o_ref[0, :, start : start + used] = result.astype(BF)
        lse_ref[0, :, start : start + used] = (top + jnp.log2(total))[:, :used]
    odd = pl.program_id(0) % 2
    hold_s[pl.ds(pl.multiple_of(odd * HEAD_DIM, HEAD_DIM), HEAD_DIM)] = o_ref[0]

    @pl.when(odd == 1)
    def _():
        row_ref[...] = hold_s[...].T


def attend(qkv, group, step):
    _, _, heads, _, seq = qkv.shape
    padded = -(-seq // 128) * 128
    part = lambda i: pl.BlockSpec((1, 1, 1, HEAD_DIM, seq), lambda h: (group, i, h, 0, 0))
    spec = lambda rows: pl.BlockSpec((1, rows, seq), lambda h: (h, 0, 0))
    return call(
        functools.partial(attend_kernel, seq, padded, step),
        (heads,),
        [part(0), part(1), part(2)],
        [spec(HEAD_DIM), pl.BlockSpec((seq, 2 * HEAD_DIM), lambda h: (0, h // 2)), spec(HEAD_DIM), spec(1)],
        [
            shaped((heads, HEAD_DIM, seq)),
            shaped((seq, heads * HEAD_DIM)),
            shaped((heads, HEAD_DIM, seq), F32),
            shaped((heads, 1, seq), F32),
        ],
        (qkv, qkv, qkv),
        [
            pltpu.VMEM((seq, 4 * HEAD_DIM), BF),
            pltpu.VMEM((4 * HEAD_DIM, padded), BF),
            pltpu.VMEM((HEAD_DIM + 16, seq), BF),
            pltpu.VMEM((2 * HEAD_DIM, seq), BF),
        ],
        name="attend",
    )


def attend_back_kernel(
    seq, padded, step, q_ref, k_ref, v_ref, d_ref, lse_ref, delta_ref, out_ref, sum_ref, key_s, query_s, value_s, dmix_s, hold_s
):
    key = k_ref[0, 0, 0]
    ones = jnp.ones((16, seq), BF)
    key_s[...] = jnp.concatenate([key, key, key, ones, jnp.zeros((48, seq), BF)], 0).T
    value_s[...] = jnp.concatenate([v_ref[0, 0, 0], ones, jnp.zeros((48, seq), BF)], 0).T
    query = pad_columns(q_ref[0, 0, 0], padded).astype(F32)
    blank = jnp.zeros((13, padded), BF)
    tail = jnp.zeros((48, padded), BF)
    lse = jnp.concatenate([*three_parts(pad_columns(-lse_ref[0], padded)), blank], 0)
    delta = jnp.concatenate([*three_parts(pad_columns(-delta_ref[0], padded)), blank], 0)
    query_s[...] = jnp.concatenate([*three_parts(query * (LOG2E * HEAD_DIM**-0.5)), lse, tail], 0)
    dmix_s[...] = jnp.concatenate([pad_columns(d_ref[0], padded), delta, tail], 0)
    scaled = (query * HEAD_DIM**-0.5).astype(BF)
    odd = pl.program_id(0) % 2
    here = pl.ds(pl.multiple_of(odd * HEAD_DIM, HEAD_DIM), HEAD_DIM)
    d_keys = jnp.zeros((HEAD_DIM, seq), F32)
    d_values = jnp.zeros((HEAD_DIM, seq), F32)
    for start, width, used in query_blocks(seq, step):
        prob = jnp.exp2(dot(key_s[...], query_s[:, start : start + width]))
        d_scores = (prob * dot(value_s[...], dmix_s[:, start : start + width])).astype(BF)
        d_values = d_values + dot(dmix_s[0:HEAD_DIM, start : start + width], prob.astype(BF), ROW_NT)
        d_keys = d_keys + dot(scaled[:, start : start + width], d_scores, ROW_NT)
        d_query = dot(key, d_scores) * HEAD_DIM**-0.5
        hold_s[0, here, start : start + used] = d_query[:, :used].astype(BF)
    hold_s[1, here] = d_keys.astype(BF)
    hold_s[2, here] = d_values.astype(BF)

    @pl.when(odd == 1)
    def _():
        for i in range(3):
            turned = hold_s[i].T
            out_ref[i] = turned
            sum_ref[i] = jnp.sum(turned.astype(F32), 0, keepdims=True)


def attend_backward(qkv, d_mixed, lse, delta, group, first, count, step):
    _, _, inner, _, seq = qkv.shape
    padded = -(-seq // 128) * 128
    part = lambda i: pl.BlockSpec((1, 1, 1, HEAD_DIM, seq), lambda h: (group, i, first + h, 0, 0))
    spec = lambda rows: pl.BlockSpec((1, rows, seq), lambda h: (group * inner + first + h, 0, 0))
    return call(
        functools.partial(attend_back_kernel, seq, padded, step),
        (count,),
        [part(0), part(1), part(2), spec(HEAD_DIM), pl.BlockSpec((1, 1, seq), lambda h: (first + h, 0, 0)), spec(1)],
        [
            pl.BlockSpec((3, seq, 2 * HEAD_DIM), lambda h: (0, 0, h // 2)),
            pl.BlockSpec((3, 1, 2 * HEAD_DIM), lambda h: (0, 0, h // 2)),
        ],
        [shaped((3, seq, count * HEAD_DIM)), shaped((3, 1, count * HEAD_DIM), F32)],
        (qkv, qkv, qkv, d_mixed, lse, delta),
        [
            pltpu.VMEM((seq, 4 * HEAD_DIM), BF),
            pltpu.VMEM((4 * HEAD_DIM, padded), BF),
            pltpu.VMEM((seq, 2 * HEAD_DIM), BF),
            pltpu.VMEM((2 * HEAD_DIM, padded), BF),
            pltpu.VMEM((3, 2 * HEAD_DIM, seq), BF),
        ],
        name="attend_backward",
    )


def mix_kernel(oa_ref, ob_ref, w_ref, out_ref):
    places, cols = w_ref.shape[1:3]
    weights = [row_blocks(w_ref, j, 0, cols) for j in range(places)]
    mixed = dot(jnp.concatenate([oa_ref[...], ob_ref[...]], 1), jnp.concatenate(weights, 0))
    out_ref[...] = mixed.astype(out_ref.dtype)


def mix(rows, weights, which, dtype):
    seq, wide = rows[0].shape
    owners, places, _, part = weights.shape
    cols = PAIR * wide // places
    half = seq // 2
    return call(
        mix_kernel,
        (2,),
        [
            pl.BlockSpec((half, wide), lambda n: (which, 0)),
            pl.BlockSpec((half, wide), lambda n: (which, 0)),
            pl.BlockSpec((owners // 2, places, cols, part), lambda n: (n, 0, 1, 0)),
        ],
        pl.BlockSpec((half, owners * part // 2), lambda n: (0, n)),
        shaped((half, owners * part), dtype),
        (*rows, weights),
        name="mix",
    )


def mix_back_kernel(bits_ref, da_ref, db_ref, w_ref, oa_ref, ob_ref, wa_ref, wb_ref, d_ref, delta_ref, *refs):
    *grad_refs, d_s = refs
    half, width = da_ref.shape
    cols = w_ref.shape[2]
    heads = oa_ref.shape[0]
    group = pl.program_id(0)

    @pl.when(group == 0)
    def _():
        d_s[0:half] = da_ref[...]
        d_s[half:] = db_ref[...]

    places = [PAIR * group + p for p in range(PAIR)]
    weights = jnp.concatenate([row_blocks(w_ref, place, 0, cols) for place in places], 0)
    d_heads = dot(weights, d_s[...], ROW_NT).astype(BF).reshape(oa_ref.shape)
    d_ref[...] = d_heads
    for which, o_ref, wide_ref in ((0, oa_ref, wa_ref), (1, ob_ref, wb_ref)):

        @pl.when(group == which)
        def _():
            delta_ref[...] = jnp.sum(d_heads.astype(F32) * wide_ref[...], 1, keepdims=True)
            grad = dot(o_ref[...].reshape(heads * HEAD_DIM, 2 * half), d_s[...]).astype(BF).T
            for p in range(PAIR):
                part = grad[:, p * cols : (p + 1) * cols]
                put_halves(bits_ref, part, p, grad_refs[2 * p], grad_refs[2 * p + 1], (slice(None), 0))


def mix_back(bits, da, db, weights, mixed, wide):
    half, width = da.shape
    owners, places, _, part = weights.shape
    heads, _, seq = mixed[0].shape
    groups = places // PAIR
    cols = heads * HEAD_DIM // PAIR
    whole = pl.BlockSpec((half, width), lambda g, bits: (0, 0))
    fixed = pl.BlockSpec((heads, HEAD_DIM, seq), lambda g, bits: (0, 0, 0))
    spec = lambda rows: pl.BlockSpec((heads, rows, seq), lambda g, bits: (g, 0, 0))
    grad = pl.BlockSpec((2, 1, width // 4, cols), lambda g, bits: (0, g, 0, 0))
    d_heads, delta, keep_a, send_a, keep_b, send_b = call(
        mix_back_kernel,
        (groups,),
        [whole, whole, pl.BlockSpec((owners, places, cols, part), lambda g, bits: (0, 0, 1, 0))] + [fixed] * 4,
        [spec(HEAD_DIM), spec(1)] + [grad] * 4,
        [shaped((groups * heads, HEAD_DIM, seq)), shaped((groups * heads, 1, seq), F32)]
        + [shaped((2, groups, width // 4, cols))] * 4,
        (bits, da, db, weights, *mixed, *wide),
        [pltpu.VMEM((seq, width), BF)],
        name="mix_back",
        prefetch=1,
    )
    return d_heads, delta, (keep_a, keep_b), (send_a, send_b)


def project_grad_kernel(bits_ref, t_ref, da_ref, db_ref, *refs):
    cols = da_ref.shape[2]
    grad = dot(t_ref[...], jnp.concatenate([da_ref[0], db_ref[0]], 1)).astype(BF)
    for p in range(PAIR):
        put_halves(bits_ref, grad[:, p * cols : (p + 1) * cols], p, refs[2 * p], refs[2 * p + 1], (slice(None), 0))


def project_grads(bits, turned, da, db):
    width, seq = turned.shape
    cols = da.shape[2]
    piece = pl.BlockSpec((1, seq, cols), lambda i, bits: (i, 0, 0))
    grad = pl.BlockSpec((2, 1, width // 4, cols), lambda i, bits: (0, i, 0, 0))
    keep_a, send_a, keep_b, send_b = call(
        project_grad_kernel,
        (3,),
        [pl.BlockSpec((width, seq), lambda i, bits: (0, 0)), piece, piece],
        [grad] * 4,
        [shaped((2, 3, width // 4, cols))] * 4,
        (bits, turned, da, db),
        name="project_grads",
        prefetch=1,
    )
    return (keep_a, keep_b), (send_a, send_b)


def project_back_kernel(a_ref, b_ref, c_ref, d_ref, qk_ref, v_ref, out_ref):
    total = None
    for first, refs in ((0, (a_ref, b_ref)), (PAIR, (c_ref, d_ref))):
        places = [first + p for p in range(PAIR)]
        left = [ref[i] for i in range(3) for ref in refs]
        right = [qk_ref[0, place, i] for i in range(2) for place in places] + [v_ref[0, place] for place in places]
        part = dot(jnp.concatenate(left, 1), jnp.concatenate(right, 0))
        total = part if total is None else total + part
    out_ref[...] = total


def project_back(pieces, w_qk, w_vo, which):
    seq = pieces[0].shape[1]
    owners, places, _, cols, part = w_qk.shape
    half = seq // 2
    return call(
        project_back_kernel,
        (owners,),
        [pl.BlockSpec((3, half, cols), lambda n: (0, which, 0)) for piece in pieces]
        + [
            pl.BlockSpec((1, places, 2, cols, part), lambda n: (turned_owner(n), 0, 0, 0, 0)),
            pl.BlockSpec((1, places, cols, part), lambda n: (n, 0, 0, 0)),
        ],
        pl.BlockSpec((half, part), lambda n: (0, n)),
        shaped((half, owners * part), F32),
        (*pieces, w_qk, w_vo),
        name="project_back",
    )


def gelu_pair(value):
    cdf = 0.5 * (1.0 + lax.erf(value * 0.7071067811865476))
    return value * cdf, cdf + value * (jnp.exp(-0.5 * value * value) * 0.3989422804014327)


def all_blocks(ref):
    return jnp.concatenate([ref[0, t] for t in range(ref.shape[1])], 1)


def relative_block(block, place, blocks):
    return lax.rem(block + blocks - place, blocks)


def either(first_ref, last_ref, index, pick):
    half = first_ref.shape[1]
    one = pick(first_ref, jnp.minimum(index, half - 1))
    return jnp.where(index < half, one, pick(last_ref, jnp.maximum(index - half, 0)))


def ffn_kernel(place_ref, x_ref, one_ref, two_ref, last_ref, b_ref, out_ref, g_ref, slope_ref, hold_s):
    blocks = hold_s.shape[0]
    step = pl.program_id(0)

    @pl.when(step < blocks)
    def _():
        ones = jnp.concatenate([one_ref[turned_owner(owner), 0] for owner in range(one_ref.shape[0])], 0)
        twos = two_ref[...].reshape(ones.shape)
        weights = jnp.where(relative_block(step, place_ref[0], blocks) < blocks // 2, ones, twos)
        pre = dot(x_ref[...], weights) + b_ref[0]
        active, slope = gelu_pair(pre)
        active = active.astype(BF)
        hold_s[step] = active
        g_ref[...] = active
        slope_ref[...] = slope.astype(BF)

    @pl.when(step >= blocks)
    def _():
        left = jnp.concatenate([hold_s[t] for t in range(blocks)], 1)
        out_ref[...] = dot(left, all_blocks(last_ref), ROW_NT).astype(out_ref.dtype)


def ffn_specs(rows, down):
    owners, blocks, part, units = down.shape
    early = lambda s: jnp.minimum(s, blocks - 1)
    late = lambda s: jnp.maximum(s - blocks, 0)
    return (
        blocks,
        early,
        late,
        pl.BlockSpec((rows, owners * part), lambda s, place: (0, 0)),
        pl.BlockSpec((rows, units), lambda s, place: (0, early(s))),
        pl.BlockSpec((1, 1, units), lambda s, place: (early(s), 0, 0)),
        pl.BlockSpec((rows, part), lambda s, place: (0, late(s))),
    )


def ffn_forward(place, x, up, down, bias, dtype):
    rows, width = x.shape
    owners, blocks, part, units = down.shape
    blocks, early, late, whole, column, thin, out = ffn_specs(rows, down)
    index = lambda s, place: relative_block(early(s), place[0], blocks)
    return call(
        ffn_kernel,
        (blocks + owners,),
        [
            whole,
            pl.BlockSpec((owners, 1, part, units), lambda s, place: (0, jnp.minimum(index(s, place), PAIR - 1), 0, 0)),
            pl.BlockSpec((owners, 1, part, units), lambda s, place: (0, jnp.maximum(index(s, place) - PAIR, 0), 0, 0)),
            pl.BlockSpec((1, blocks, part, units), lambda s, place: (late(s), 0, 0, 0)),
            thin,
        ],
        [out, column, column],
        [shaped((rows, width), dtype), shaped((rows, blocks * units)), shaped((rows, blocks * units))],
        (place, x, *up, down, bias),
        [pltpu.VMEM((blocks, rows, units), BF)],
        name="ffn",
        prefetch=1,
    )


def ffn_back_kernel(place_ref, d_ref, first_ref, one_ref, two_ref, slope_ref, out_ref, dpre_ref, sum_ref, hold_s):
    blocks = hold_s.shape[0]
    step = pl.program_id(0)

    @pl.when(step < blocks)
    def _():
        d_pre = (dot(d_ref[...], first_ref[...].reshape(d_ref.shape[1], -1)) * slope_ref[...].astype(F32)).astype(BF)
        hold_s[step] = d_pre
        dpre_ref[...] = d_pre
        sum_ref[0] = jnp.sum(d_pre.astype(F32), 0, keepdims=True)

    @pl.when(step >= blocks)
    def _():
        left = jnp.concatenate([hold_s[t] for t in range(blocks)], 1)
        order = [relative_block(t, place_ref[0], blocks) for t in range(blocks)]
        weights = [either(one_ref, two_ref, index, lambda ref, i: ref[0, i]) for index in order]
        out_ref[...] = dot(left, jnp.concatenate(weights, 1), ROW_NT).astype(out_ref.dtype)


def ffn_backward(place, d_out, up, down, slope, dtype):
    rows, width = d_out.shape
    owners, blocks, part, units = down.shape
    blocks, early, late, whole, column, thin, out = ffn_specs(rows, down)
    return call(
        ffn_back_kernel,
        (blocks + owners,),
        [
            whole,
            pl.BlockSpec((owners, 1, part, units), lambda s, place: (0, early(s), 0, 0)),
            pl.BlockSpec((1, PAIR, part, units), lambda s, place: (turned_owner(late(s)), 0, 0, 0)),
            pl.BlockSpec((1, PAIR, part, units), lambda s, place: (late(s), 0, 0, 0)),
            column,
        ],
        [out, column, thin],
        [shaped((rows, width), dtype), shaped((rows, blocks * units)), shaped((blocks, 1, units), F32)],
        (place, d_out, down, *up, slope),
        [pltpu.VMEM((blocks, rows, units), BF)],
        name="ffn_backward",
        prefetch=1,
    )


def put_halves(bits_ref, grad, which, keep_ref, send_ref, at):
    grad = grad.reshape((2, 2, grad.shape[0] // 4) + grad.shape[1:])
    pair = (grad[:, 0], grad[:, 1]) if which == 0 else (grad[0], grad[1])
    low = bits_ref[which] == 0
    keep_ref[at] = jnp.where(low, pair[0], pair[1])
    send_ref[at] = jnp.where(low, pair[1], pair[0])


def ffn_grad_kernel(bits_ref, xa_ref, xb_ref, ca_ref, cb_ref, keep_a, send_a, keep_b, send_b, x_s):
    step = pl.program_id(0)

    @pl.when(step == 0)
    def _():
        x_s[...] = jnp.concatenate([xa_ref[...], xb_ref[...]], 0).T

    column = jnp.concatenate([ca_ref[...], cb_ref[...]], 0)
    grad = dot(x_s[...], column).astype(BF)

    @pl.when(step < PAIR)
    def _():
        put_halves(bits_ref, grad, 0, keep_a, send_a, (slice(None), 0))

    @pl.when(step >= PAIR)
    def _():
        put_halves(bits_ref, grad, 1, keep_b, send_b, (slice(None), 0))


def ffn_grad(bits, xa, xb, ca, cb, blocks):
    rows, width = xa.shape
    units = ca.shape[1] // blocks
    whole = pl.BlockSpec((rows, width), lambda t, bits: (0, 0))
    column = pl.BlockSpec((rows, units), lambda t, bits: (0, t))
    first = pl.BlockSpec((2, 1, width // 4, units), lambda t, bits: (0, jnp.minimum(t, PAIR - 1), 0, 0))
    last = pl.BlockSpec((2, 1, width // 4, units), lambda t, bits: (0, jnp.maximum(t - PAIR, 0), 0, 0))
    keep_a, send_a, keep_b, send_b = call(
        ffn_grad_kernel,
        (blocks,),
        [whole, whole, column, column],
        [first, first, last, last],
        [shaped((2, PAIR, width // 4, units))] * 4,
        (bits, xa, xb, ca, cb),
        [pltpu.VMEM((width, 2 * rows), BF)],
        name="ffn_grad",
        prefetch=1,
    )
    return (keep_a, keep_b), (send_a, send_b)


def add_kernel(bits_ref, *refs):
    count = len(refs) // 3
    for i in range(count):
        refs[2 * count + i][0] = (refs[2 * i][0].astype(F32) + refs[2 * i + 1][0].astype(F32)).astype(BF)


def add_middle(bits, keeps, parts):
    args, in_specs = [], []
    for i, (keep, part) in enumerate(zip(keeps, parts)):
        args += [keep, part]
        block = (1,) + keep.shape[1:]
        in_specs += [pl.BlockSpec(block, lambda s, bits, i=i: (1 - bits[1 - i % 2], 0, 0, 0))] * 2
    shapes = [(1,) + keep.shape[1:] for keep in keeps]
    outs = call(
        add_kernel,
        (1,),
        in_specs,
        [pl.BlockSpec(shape, lambda s, bits: (0, 0, 0, 0)) for shape in shapes],
        [shaped(shape) for shape in shapes],
        (bits, *args),
        name="add_middle",
        prefetch=1,
    )
    return [out[0] for out in outs]


def add_end_kernel(bits_ref, *refs):
    out_ref = refs[-1]
    for i in range(len(refs) // 3):
        keep, part, end = refs[3 * i : 3 * i + 3]
        total = keep[0].astype(F32) + part[0].astype(F32) + end[...].astype(F32)
        half = total.shape[0]
        at = i % 2 * half
        out_ref[at : at + half, i // 2] = total.astype(BF)


def add_end(bits, keeps, parts, ends):
    args, in_specs = [], []
    for i, (keep, part, end) in enumerate(zip(keeps, parts, ends)):
        args += [keep, part, end]
        block = (1,) + keep.shape[1:]
        in_specs += [pl.BlockSpec(block, lambda s, bits, i=i: (bits[1 - i % 2], 0, 0, 0))] * 2
        in_specs.append(pl.BlockSpec(end.shape, lambda s, bits: (0, 0, 0)))
    _, blocks, rows, units = keeps[0].shape
    shape = (2 * blocks, len(keeps) // 2, rows, units)
    return call(
        add_end_kernel,
        (1,),
        in_specs,
        pl.BlockSpec(shape, lambda s, bits: (0, 0, 0, 0)),
        shaped(shape),
        (bits, *args),
        name="add_end",
        prefetch=1,
    )


def norm_back_block(da_ref, db_ref, x_ref, rest_ref, gain_ref, sum_ref):
    d_value = da_ref[...] + db_ref[...].astype(F32)
    value = x_ref[...].astype(F32)
    centred = value - jnp.mean(value, -1, keepdims=True)
    scale = lax.rsqrt(jnp.mean(centred * centred, -1, keepdims=True) + EPS)
    unit = centred * scale
    d_unit = d_value * gain_ref[...]
    inner = jnp.mean(d_unit * unit, -1, keepdims=True)
    rest = rest_ref[...]
    result = rest + scale * (d_unit - jnp.mean(d_unit, -1, keepdims=True) - unit * inner)
    parts = [d_value * unit, d_value, result, rest]
    sums = jnp.concatenate([jnp.sum(part, 0, keepdims=True) for part in parts] + [jnp.zeros((4, value.shape[1]), F32)], 0)

    @pl.when(pl.program_id(0) == 0)
    def _():
        sum_ref[...] = sums

    @pl.when(pl.program_id(0) > 0)
    def _():
        sum_ref[...] += sums

    return result


def norm_back_kernel(da_ref, db_ref, x_ref, rest_ref, gain_ref, out_ref, low_ref, sum_ref):
    result = norm_back_block(da_ref, db_ref, x_ref, rest_ref, gain_ref, sum_ref)
    out_ref[...] = result
    low_ref[...] = result.astype(BF)


def norm_back_halves_kernel(da_ref, db_ref, x_ref, rest_ref, gain_ref, near_ref, far_ref, sum_ref):
    result = norm_back_block(da_ref, db_ref, x_ref, rest_ref, gain_ref, sum_ref).astype(BF)

    @pl.when(pl.program_id(0) == 0)
    def _():
        near_ref[...] = result

    @pl.when(pl.program_id(0) == 1)
    def _():
        far_ref[...] = result


def norm_backward(da, db, x, rest, gain, halves):
    rows, width = da.shape
    steps = 2 if halves else 1
    row = pl.BlockSpec((rows // steps, width), lambda i: (i, 0))
    whole = lambda count: pl.BlockSpec((count, width), lambda i: (0, 0))
    return call(
        norm_back_halves_kernel if halves else norm_back_kernel,
        (steps,),
        [row] * 4 + [whole(1)],
        [whole(rows // 2)] * 2 + [whole(8)] if halves else [row, row, whole(8)],
        ([shaped((rows // 2, width))] * 2 if halves else [shaped((rows, width), F32), shaped((rows, width))])
        + [shaped((8, width), F32)],
        (da, db, x, rest, gain[None]),
        name="norm_backward",
    )


def swap(value, axis):
    return lax.ppermute(value, axis, [(0, 1), (1, 0)])


def after(value, *others):
    return lax.optimization_barrier((value, *others))[0]


def together(*values):
    return lax.optimization_barrier(values)


def ordered(bit, mine, other, axis):
    return jnp.concatenate([jnp.where(bit == 0, mine, other), jnp.where(bit == 0, other, mine)], axis)


def chosen(value, bit, axis):
    return lax.dynamic_index_in_dim(value, bit, axis, keepdims=False)


def added(mine, other):
    return (mine.astype(F32) + other.astype(F32)).astype(BF)


def moments(value):
    mean = jnp.mean(value, -1, keepdims=True)
    centred = value - mean
    scale = lax.rsqrt(jnp.mean(centred * centred, -1, keepdims=True) + EPS)
    return centred, scale


def clip_local(clips, w_qkv, w_out, w_up, w_down, norm_gain, shifts, bias_qv, up_bias, teacher):
    y, x, c, t = (lax.axis_index(name) for name in ("y", "x", "c", "t"))
    every = ("y", "x", "c", "t")
    steps = 4
    width = clips.shape[2]
    odd = t % 2

    first_way, second_way = [], []
    for column in range(4):
        for core in range(2):
            for place in range(4):
                source = (column * 2 + core) * 4 + place
                to = (column * 2 + place // 2) * 4 + 2 * core
                first_way.append((source, to + place % 2))
                second_way.append((source, to + 1 - place % 2))
    first_way = [(a, b) for a, b in first_way if a != b]
    back = lambda way: [(b, a) for a, b in way]
    stays = t // 2 == c

    def sent(pair):
        return lax.ppermute(pair[0], every, first_way), lax.ppermute(pair[1], every, second_way)

    def to_chip(value):
        return sent((chosen(value, odd, 0), chosen(value, 1 - odd, 0)))

    def sent_back(near, far):
        return lax.ppermute(near, every, back(first_way)), lax.ppermute(far, every, back(second_way))

    def from_chip(value):
        half = value.shape[0] // 2
        return sent_back(value[:half], value[half:])

    rings = [[(i, (i + away) % steps) for i in range(steps)] for away in range(steps)]

    def ring_gather(value):
        return tuple(lax.ppermute(value, "t", rings[-j % steps]) for j in range(1, steps))

    def ring_scatter(blocks):
        return tuple(lax.ppermute(blocks[j], "t", rings[j]) for j in range(1, steps))

    def placed(value, axis):
        return lax.dynamic_slice_in_dim(jnp.concatenate([value, value], axis), steps - t, steps, axis)

    def on_chip(value, near, far):
        return jnp.concatenate([jnp.where(stays, chosen(value, odd, 0), near), far])

    def as_clips(mine, near, far):
        near = jnp.where(stays, mine, near)
        return jnp.stack([jnp.where(odd == 0, near, far), jnp.where(odd == 0, far, near)])

    def scatter_start(sends):
        return swap(sends[0], "x"), swap(sends[1], "y")

    def sums_of(keeps, parts, row, column):
        pick = lambda values, bit: jnp.concatenate([chosen(value, bit, 0) for value in values])
        first = pick(keeps[0], row).astype(F32) + chosen(parts[0], row, 0).astype(F32)
        return first, pick(keeps[1], column).astype(F32) + chosen(parts[1], column, 0).astype(F32)

    def scatter_middle(keeps, parts):
        first, second = sums_of(keeps, parts, 1 - y, 1 - x)
        return swap(first.astype(BF), "y"), swap(second.astype(BF), "x")

    def scatter_end(keeps, parts, ends):
        first, second = sums_of(keeps, parts, y, x)
        return (first + ends[0].astype(F32)).astype(BF), (second + ends[1].astype(F32)).astype(BF)

    dims = w_qkv.shape[1]
    cols = w_out.shape[0] // 2
    lane = bias_qv.shape[1]
    units = w_up.shape[1] // 2
    attn = jnp.concatenate([jnp.swapaxes(w_qkv, 1, 2), w_out[None]]).reshape(4, 2, cols, dims)
    mine, other = chosen(attn, c, 1).reshape(4 * cols, dims), chosen(attn, 1 - c, 1).reshape(4 * cols, dims)
    attn_piece = ordered(c, mine, swap(other, "c"), 1)
    ff = jnp.stack([w_up, w_down.T]).reshape(2, dims, 2, units)
    ff_piece = ordered(c, chosen(ff, c, 2), swap(chosen(ff, 1 - c, 2), "c"), 1)

    pad = lambda value: jnp.pad(value, (0, dims - value.shape[0]))[None]
    tails = jnp.concatenate([pad(bias_qv[0]), pad(bias_qv[1]), pad(up_bias), jnp.zeros((7, dims), BF)])
    vectors = jnp.concatenate([norm_gain, shifts, tails])
    for bit, name in ((c, "c"), (x, "x"), (y, "y")):
        vectors = ordered(bit, vectors, swap(vectors, name), 1)
    gains, shift_all = vectors[0:2].astype(F32), vectors[2:6].astype(F32)
    tails = vectors[6:16]
    tails = jnp.stack([part[:3] for part in (tails, *ring_gather(tails))]).astype(F32)
    tails = lax.dynamic_slice_in_dim(tails, 4 * dims * c, 4 * dims, 2)
    pair = tails[:, :2].reshape(steps, 2, 4, dims)[..., :lane]
    bias_pair = jnp.swapaxes(pair, 0, 1).reshape(2, 2, 2 * cols)
    bias_in = jnp.stack([bias_pair[0], jnp.zeros_like(bias_pair[0]), bias_pair[1]], 1)[..., None]
    up_shift = placed(tails[:, 2:3], 0)

    whole = ("y", "x", "t")
    attn_rows = together(*ring_gather(attn_piece))
    near, far = to_chip(after(clips, attn_rows))
    attn_rows = (attn_piece, *attn_rows)
    qk_rows = jnp.stack([part[: 2 * cols] for part in attn_rows])
    vo_rows = jnp.stack([part[2 * cols :] for part in attn_rows])
    targets = chosen(teacher, odd, 0), chosen(teacher, 1 - odd, 0)
    swapped, near, targets, bias_in, up_shift = together(
        (swap(qk_rows, "y"), swap(vo_rows, "x")), near, targets, bias_in, up_shift
    )
    w_qk, w_vo = ordered(y, qk_rows[None], swapped[0][None], 0), ordered(x, vo_rows[None], swapped[1][None], 0)
    swapped, far = together((swap(w_qk, "x"), swap(w_vo, "y")), far)
    w_qk = ordered(x, w_qk[None], swapped[0][None], 0).reshape(4, steps, 2, cols, 2 * dims)
    w_vo = ordered(y, w_vo[None], swapped[1][None], 0).reshape(4, steps, 2 * cols, 2 * dims)
    up_piece, down_piece = ff_piece
    up_piece, down_piece, far = together(up_piece, down_piece, far)
    up_rows = ring_gather(up_piece)
    down_all = lax.all_gather(down_piece, whole, axis=0, tiled=False).reshape(4, steps, 2 * dims, units)
    place = t.reshape(1)

    inputs = on_chip(clips, near, far).astype(F32)
    centred_one, scale_one = moments(inputs)
    first = (centred_one * scale_one * gains[0] + shift_all[0]).astype(BF)
    first_other = swap(first, "c")
    half = first.shape[0] // 2
    qkv, turned = project(first, first_other, w_qk, w_vo, bias_in)
    mixed_a, rows_a, wide_a, lse_a = attend(qkv, 0, 1664)
    up_rows, rows_a = together(up_rows, rows_a)
    up_a, up_b = jnp.stack([up_piece, up_rows[0]]), jnp.stack(up_rows[1:])
    swapped = swap(up_a, "y"), swap(up_b, "x")
    mixed_b, rows_b, wide_b, lse_b = attend(after(qkv, rows_a), 1, 1664)
    swapped, rows_b = together(swapped, rows_b)
    up_a, up_b = ordered(y, up_a[None], swapped[0][None], 0), ordered(x, up_b[None], swapped[1][None], 0)
    swapped = swap(up_a, "x"), swap(up_b, "y")
    rows = (rows_a, rows_b)
    attn_other = mix(rows, w_vo, 1, BF)
    attn_mine = mix((after(rows_a, attn_other), rows_b), w_vo, 0, F32)
    hidden = inputs + (attn_mine + swap(attn_other, "c").astype(F32)) + shift_all[2]

    centred_two, scale_two = moments(hidden)
    second = (centred_two * scale_two * gains[1] + shift_all[1]).astype(BF)
    second_other = swap(second, "c")
    swapped, second = together(swapped, second)
    up_a = ordered(x, up_a[None], swapped[0][None], 0).reshape(4, PAIR, 2 * dims, units)
    up_b = ordered(y, up_b[None], swapped[1][None], 0).reshape(4, PAIR, 2 * dims, units)
    up_all = up_a, up_b
    targets, second, down_all = together(targets, second, down_all)
    near, far = sent(targets)
    out_mine, act_mine, slope_mine = ffn_forward(place, second, up_all, down_all, up_shift, F32)
    out_mine, near = together(out_mine, near)
    out_other, act_other, slope_other = ffn_forward(place, after(second_other, near), up_all, down_all, up_shift, BF)
    out_other, far = together(out_other, far)
    output = hidden + (out_mine + swap(out_other, "c").astype(F32)) + shift_all[3]
    d_out = output - on_chip(teacher, near, far).astype(F32)
    d_ffn = d_out.astype(BF)
    d_ffn_other = swap(d_ffn, "c")
    d_second, d_pre, sum_mine = ffn_backward(place, d_ffn, up_all, down_all, slope_mine, F32)
    d_ffn_other, d_pre = together(d_ffn_other, d_pre)
    d_second_other, d_pre_other, sum_other = ffn_backward(place, d_ffn_other, up_all, down_all, slope_other, BF)
    d_second_swapped = swap(d_second_other, "c")
    up_sum = (sum_mine + sum_other).reshape(steps, units)

    bits = jnp.stack([x, y])
    grad_down, sends = ffn_grad(bits, after(d_ffn, d_pre_other), d_ffn_other, act_mine, act_other, steps)
    down = scatter_start(sends)
    result, grad_down = together(output.astype(BF), grad_down)
    out_near, out_far = from_chip(result)
    d_second_swapped, grad_down = together(d_second_swapped, grad_down)
    d_hidden, d_attn, sums_two = norm_backward(d_second, d_second_swapped, hidden, d_out, gains[1], False)
    d_attn_other = swap(d_attn, "c")
    grad_up, sends = ffn_grad(bits, after(second, d_attn), second_other, d_pre, d_pre_other, steps)
    up = scatter_start(sends)
    d_attn_other, grad_up = together(d_attn_other, grad_up)

    d_heads, delta, grad_o, sends_o = mix_back(bits, d_attn, d_attn_other, w_vo, (mixed_a, mixed_b), (wide_a, wide_b))
    keeps = (*grad_up, *grad_down)
    back_a, sum_a = attend_backward(qkv, d_heads, lse_b, delta, 1, 0, 2, 256)
    up, down, out_near, back_a = together(up, down, out_near, back_a)
    ends = add_middle(bits, keeps, (*up, *down))
    ends = [swap(part, name) for part, name in zip(ends, ("y", "x", "y", "x"))]
    back_b, sum_b = attend_backward(qkv, after(d_heads, back_a), lse_b, delta, 1, 2, 2, 256)
    ends, out_far, back_b = together(ends, out_far, back_b)
    grad_ff = add_end(bits, keeps, (*up, *down), ends).reshape(steps * 4 * dims, units)
    ff_total = lax.psum_scatter(grad_ff, "t", scatter_dimension=0, tiled=True)
    grad_one, sends = project_grads(bits, turned, back_a, back_b)
    one = scatter_start([jnp.concatenate(pair, 1) for pair in zip(sends, sends_o)])
    grad_one = list(zip(grad_one, grad_o))
    delta, grad_ff, grad_one = together(delta, grad_ff, grad_one)
    back_c, sum_c = attend_backward(qkv, after(d_heads, back_b), lse_a, delta, 0, 2, 2, 256)
    one, back_c = together(one, back_c)
    one_ends = scatter_middle(grad_one, one)
    back_d, sum_d = attend_backward(qkv, after(d_heads, back_c), lse_a, delta, 0, 0, 2, 256)
    one_ends, back_d = together(one_ends, back_d)
    grad_two, sends = project_grads(bits, turned, back_d, back_c)
    two = scatter_start(sends)
    pieces = (back_d, back_c, back_a, back_b)
    d_first_other = project_back(pieces, w_qk, after(w_vo, grad_two), 1)
    d_first_swapped = swap(d_first_other, "c")
    one = scatter_end(grad_one, one, one_ends)
    early = [lax.ppermute(jnp.concatenate([one[p][:3], one[p][4:]]), "t", rings[PAIR + p]) for p in range(PAIR)]
    two, d_first_other = together(two, d_first_other)
    two_ends = scatter_middle([[keep] for keep in grad_two], two)
    d_first = project_back(pieces, w_qk, after(w_vo, d_first_other), 0)
    ff_total, d_first = together(ff_total, d_first)
    d_first_swapped, d_first = together(d_first_swapped, d_first)
    *d_inputs, sums_one = norm_backward(d_first, d_first_swapped, inputs, d_hidden, gains[0], True)
    early, sums_one = together(early, sums_one)
    grad_near, grad_far = sent_back(*d_inputs)
    small = (sum_a, sum_b, sum_c, sum_d, up_sum, sums_one)
    small, d_inputs = together(small, d_inputs)
    two_ends, grad_near, out_near, out_far = together(two_ends, grad_near, out_near, out_far)
    sum_a, sum_b, sum_c, sum_d, up_sum, sums_one = small
    two = scatter_end([[keep] for keep in grad_two], two, two_ends)
    late = lax.ppermute(jnp.concatenate([two[1], one[1][3:4]]), "t", rings[1])

    grad_ff = ff_total.astype(F32).reshape(2, 2, dims, units)
    grad_ff = ordered(c, chosen(grad_ff, c, 1), swap(chosen(grad_ff, 1 - c, 1), "c"), 2)
    grad_attn = jnp.concatenate([two[0], one[0][3:4]]).astype(F32)
    grad_attn = sum((part.astype(F32) for part in (*early, late)), grad_attn).reshape(4, 2, dims, cols)
    grad_attn = ordered(c, chosen(grad_attn, c, 1), swap(chosen(grad_attn, 1 - c, 1), "c"), 2)

    heads_sum = jnp.concatenate([sum_d, sum_c, sum_a, sum_b], 2).reshape(3, steps, 4, lane)
    heads_sum = placed(jnp.stack([heads_sum[0], heads_sum[2]]), 1)
    heads_sum = jnp.pad(heads_sum, ((0, 0), (0, 0), (0, 0), (0, dims - lane))).reshape(2 * steps, 4 * dims)
    own = jnp.concatenate([heads_sum, up_sum])
    own = jnp.concatenate([jnp.where(c == 0, own, 0.0), jnp.where(c == 1, own, 0.0)], 1)
    normed = [sums_one[0:1], sums_two[0:1], sums_one[1:2], sums_two[1:4]]
    sums = jnp.concatenate(normed + [jnp.zeros((2, width), F32), own])
    for bit, name in ((y, "y"), (x, "x"), (c, "c")):
        half = sums.shape[1] // 2
        part = lambda which: lax.dynamic_slice_in_dim(sums, which * half, half, 1)
        sums = part(bit) + swap(part(1 - bit), name)
    sums, grad_near = together(sums, grad_near)
    sums = sum((lax.ppermute(sums, "t", rings[away]) for away in range(1, steps)), sums)
    thin = width // 32
    vector_sums = lax.dynamic_slice_in_dim(sums[:6], thin * t, thin, 1)
    place_sums = lax.dynamic_index_in_dim(sums[8:].reshape(3, steps, dims), t, 1, keepdims=False)
    return (
        as_clips(result[: result.shape[0] // 2], out_near, out_far),
        as_clips(d_inputs[0], grad_near, grad_far),
        grad_attn[:3],
        grad_attn[3].T,
        grad_ff[0],
        grad_ff[1].T,
        vector_sums[:2],
        vector_sums[2:],
        place_sums[:2, :lane],
        place_sums[2],
    )


def clip_per_chip(mesh):
    fine = Mesh(mesh.devices.reshape(2, 2, 2, 4), ("y", "x", "c", "t"))
    dp = ("y", "x", "c")
    in_specs = (
        P(dp, "t", None),
        P(None, dp, "t"),
        P("t", dp),
        P(dp, "t"),
        P("t", dp),
        P(None, dp),
        P(None, dp),
        P(None, ("t",) + dp),
        P(("t",) + dp),
        P(dp, "t", None),
    )
    out_specs = in_specs[:1] * 2 + in_specs[1:5] + (
        P(None, dp + ("t",)),
        P(None, dp + ("t",)),
        P(None, ("t",) + dp),
        P(("t",) + dp),
    )
    return jax.shard_map(clip_local, mesh=fine, in_specs=in_specs, out_specs=out_specs, check_vma=False)


def solution(mesh):
    if dict(mesh.shape) == {"dp": 8, "tensor": 4}:
        return clip_per_chip(mesh)
    in_specs = (
        P("dp", "tensor", None),
        P(None, "dp", "tensor"),
        P("tensor", "dp"),
        P("dp", "tensor"),
        P("tensor", "dp"),
        P(None, "dp"),
        P(None, "dp"),
        P(None, ("tensor", "dp")),
        P(("tensor", "dp")),
        P("dp", "tensor", None),
    )
    out_specs = (
        P("dp", "tensor", None),
        P("dp", "tensor", None),
        P(None, "dp", "tensor"),
        P("tensor", "dp"),
        P("dp", "tensor"),
        P("tensor", "dp"),
        P(None, ("dp", "tensor")),
        P(None, ("dp", "tensor")),
        P(None, ("tensor", "dp")),
        P(("tensor", "dp")),
    )
    return jax.shard_map(local, mesh=mesh, in_specs=in_specs, out_specs=out_specs, check_vma=False)
```

```python
import functools

import jax
import jax.numpy as jnp
from jax import lax
from jax.experimental import pallas as pl
from jax.experimental.pallas import tpu as pltpu
from jax.sharding import Mesh, PartitionSpec as P

HEAD_DIM = 64


EPS = 1e-05


def layer_norm(value, gain, shift):
    mean = jnp.mean(value, -1, keepdims=True)
    centred = value - mean
    spread = jnp.mean(centred * centred, -1, keepdims=True)
    return centred * lax.rsqrt(spread + EPS) * gain + shift


def exact_gelu(value):
    return jax.nn.gelu(value, approximate=False)


def attend_clip(query, keys, values, scale):
    scores = jnp.einsum("qhe,khe->hqk", query, keys, preferred_element_type=jnp.float32) * scale
    top = jnp.max(scores, -1, keepdims=True)
    expd = jnp.exp(scores - top)
    total = jnp.sum(expd, -1, keepdims=True)
    prob = (expd / total).astype(jnp.bfloat16)
    mixed = jnp.einsum("hqk,khe->qhe", prob, values, preferred_element_type=jnp.float32)
    return (mixed.astype(jnp.bfloat16), (top + jnp.log(total))[..., 0])


def attend_back(query, keys, values, d_mixed, logsum, scale):
    scores = jnp.einsum("qhe,khe->hqk", query, keys, preferred_element_type=jnp.float32) * scale
    prob = jnp.exp(scores - logsum[:, :, None])
    d_prob = jnp.einsum("qhe,khe->hqk", d_mixed, values, preferred_element_type=jnp.float32)
    delta = jnp.sum(d_prob * prob, -1, keepdims=True)
    d_scores = (prob * (d_prob - delta)).astype(jnp.bfloat16)
    d_values = jnp.einsum(
        "hqk,qhe->khe", prob.astype(jnp.bfloat16), d_mixed, preferred_element_type=jnp.float32
    )
    d_query = jnp.einsum("hqk,khe->qhe", d_scores, keys, preferred_element_type=jnp.float32) * scale
    d_keys = jnp.einsum("hqk,qhe->khe", d_scores, query, preferred_element_type=jnp.float32) * scale
    return jnp.stack([d_query, d_keys, d_values]).astype(jnp.bfloat16)


def local(clips, w_qkv, w_out, w_up, w_down, norm_gain, shifts, bias_qv, up_bias, teacher):
    wq, wo, wu, wd, gains, shift_all, bias_pair, up_shift = (
        lax.all_gather(w_qkv, "dp", axis=1, tiled=True),
        lax.all_gather(w_out, "dp", axis=1, tiled=True),
        lax.all_gather(w_up, "dp", axis=0, tiled=True),
        lax.all_gather(w_down, "dp", axis=1, tiled=True),
        lax.all_gather(norm_gain, "dp", axis=1, tiled=True),
        lax.all_gather(shifts, "dp", axis=1, tiled=True),
        lax.all_gather(bias_qv, "dp", axis=1, tiled=True),
        lax.all_gather(up_bias, "dp", axis=0, tiled=True),
    )
    gains = gains.astype(jnp.float32)
    shift_all = shift_all.astype(jnp.float32)
    bias_pair = bias_pair.astype(jnp.float32)
    up_shift = up_shift.astype(jnp.float32)
    width = wq.shape[2]
    heads_here = width // HEAD_DIM
    scale = HEAD_DIM ** (-0.5)
    inputs = jnp.swapaxes(clips, 0, 1).astype(jnp.float32)
    first = layer_norm(inputs, gains[0], shift_all[0]).astype(jnp.bfloat16)
    whole_first = lax.all_gather(first, "tensor", axis=0, tiled=True)
    seq = whole_first.shape[0]
    count = whole_first.shape[1]
    projected = jnp.einsum("scd,kde->ksce", whole_first, wq, preferred_element_type=jnp.float32)
    qkv_bias = jnp.stack([bias_pair[0], jnp.zeros_like(bias_pair[0]), bias_pair[1]])
    qkv = (projected + qkv_bias[:, None, None, :]).astype(jnp.bfloat16)

    def heads(value):
        return jnp.swapaxes(value, 0, 1).reshape(count, seq, heads_here, HEAD_DIM)

    query_h, keys_h, values_h = (heads(qkv[0]), heads(qkv[1]), heads(qkv[2]))
    attended, logsum = lax.map(
        lambda item: attend_clip(item[0], item[1], item[2], scale), (query_h, keys_h, values_h)
    )
    mixed = jnp.swapaxes(attended.reshape(count, seq, width), 0, 1)
    piece = mixed
    attn = lax.psum_scatter(
        jnp.einsum("scd,de->sce", piece, wo, preferred_element_type=jnp.float32),
        "tensor",
        scatter_dimension=0,
        tiled=True,
    )
    hidden = inputs + attn + shift_all[2]
    second = layer_norm(hidden, gains[1], shift_all[1]).astype(jnp.bfloat16)
    whole_second = lax.all_gather(second, "tensor", axis=0, tiled=True)
    pre = jnp.einsum("scd,df->scf", whole_second, wu, preferred_element_type=jnp.float32) + up_shift
    active = exact_gelu(pre).astype(jnp.bfloat16)
    piece = active
    ffn = lax.psum_scatter(
        jnp.einsum("scf,fe->sce", piece, wd, preferred_element_type=jnp.float32),
        "tensor",
        scatter_dimension=0,
        tiled=True,
    )
    output = hidden + ffn + shift_all[3]
    d_out = output - jnp.swapaxes(teacher, 0, 1).astype(jnp.float32)
    whole_d_ffn = lax.all_gather(d_out.astype(jnp.bfloat16), "tensor", axis=0, tiled=True)
    d_active = jnp.einsum("sce,fe->scf", whole_d_ffn, wd, preferred_element_type=jnp.float32)
    grad_down = jnp.einsum("scf,sce->fe", active, whole_d_ffn, preferred_element_type=jnp.float32)
    gelu_value, gelu_back = jax.vjp(exact_gelu, pre)
    d_pre = gelu_back(d_active)[0].astype(jnp.bfloat16)
    grad_up_shift = jnp.sum(d_pre.astype(jnp.float32), (0, 1))
    grad_up = jnp.einsum("scd,scf->df", whole_second, d_pre, preferred_element_type=jnp.float32)
    piece = d_pre
    d_second = lax.psum_scatter(
        jnp.einsum("scf,df->scd", piece, wu, preferred_element_type=jnp.float32),
        "tensor",
        scatter_dimension=0,
        tiled=True,
    )
    norm_value, second_back = jax.vjp(layer_norm, hidden, gains[1], shift_all[1])
    d_hidden_norm, grad_gain_two, grad_shift_two = second_back(d_second)
    d_hidden = d_out + d_hidden_norm
    whole_d_attn = lax.all_gather(d_hidden.astype(jnp.bfloat16), "tensor", axis=0, tiled=True)
    d_mixed = jnp.einsum(
        "sce,de->scd", whole_d_attn, wo, preferred_element_type=jnp.float32
    ).astype(jnp.bfloat16)
    grad_out = jnp.einsum("scd,sce->de", mixed, whole_d_attn, preferred_element_type=jnp.float32)
    d_heads = jnp.swapaxes(d_mixed, 0, 1).reshape(count, seq, heads_here, HEAD_DIM)
    d_stacked = lax.map(
        lambda item: attend_back(item[0], item[1], item[2], item[3], item[4], scale),
        (query_h, keys_h, values_h, d_heads, logsum),
    )
    d_qkv = jnp.transpose(d_stacked.reshape(count, 3, seq, width), (1, 2, 0, 3))
    bias_sums = jnp.sum(d_qkv.astype(jnp.float32), (1, 2))
    grad_pair = jnp.stack([bias_sums[0], bias_sums[2]])
    grad_qkv = jnp.einsum("scd,ksce->kde", whole_first, d_qkv, preferred_element_type=jnp.float32)
    piece = d_qkv
    d_first = lax.psum_scatter(
        jnp.einsum("ksce,kde->scd", piece, wq, preferred_element_type=jnp.float32),
        "tensor",
        scatter_dimension=0,
        tiled=True,
    )
    first_value, first_back = jax.vjp(layer_norm, inputs, gains[0], shift_all[0])
    d_in_norm, grad_gain_one, grad_shift_one = first_back(d_first)
    d_inputs = d_hidden + d_in_norm
    sums = (
        lax.psum_scatter(grad_qkv, "dp", scatter_dimension=1, tiled=True),
        lax.psum_scatter(grad_out, "dp", scatter_dimension=1, tiled=True),
        lax.psum_scatter(grad_up, "dp", scatter_dimension=0, tiled=True),
        lax.psum_scatter(grad_down, "dp", scatter_dimension=1, tiled=True),
        lax.psum_scatter(grad_pair, "dp", scatter_dimension=1, tiled=True),
        lax.psum_scatter(grad_up_shift, "dp", scatter_dimension=0, tiled=True),
    )
    grad_gain = jnp.stack([grad_gain_one, grad_gain_two])
    grad_shift = jnp.stack(
        [grad_shift_one, grad_shift_two, jnp.sum(d_hidden, (0, 1)), jnp.sum(d_out, (0, 1))]
    )
    norm_sums = (
        lax.psum_scatter(grad_gain, ("dp", "tensor"), scatter_dimension=1, tiled=True),
        lax.psum_scatter(grad_shift, ("dp", "tensor"), scatter_dimension=1, tiled=True),
    )
    result = jnp.swapaxes(output, 0, 1).astype(jnp.bfloat16)
    grad_in = jnp.swapaxes(d_inputs, 0, 1).astype(jnp.bfloat16)
    return (
        result,
        grad_in,
        sums[0],
        sums[1],
        sums[2],
        sums[3],
        norm_sums[0],
        norm_sums[1],
        sums[4],
        sums[5],
    )


BF = jnp.bfloat16
F32 = jnp.float32
LOG2E = 1.4426950408889634
VMEM_LIMIT = 56 * 2**20
ROW_NN = (((1,), (0,)), ((), ()))
ROW_NT = (((1,), (1,)), ((), ()))
PAIR = 2


def dot(left, right, dims=ROW_NN):
    return lax.dot_general(left, right, dims, preferred_element_type=F32)


def call(body, grid, in_specs, out_specs, out_shape, args, scratch=(), name=None, prefetch=0, aliases=None):
    return pl.pallas_call(
        body,
        grid_spec=pltpu.PrefetchScalarGridSpec(
            num_scalar_prefetch=prefetch, grid=grid, in_specs=in_specs, out_specs=out_specs, scratch_shapes=list(scratch)
        ),
        out_shape=out_shape,
        input_output_aliases=aliases or {},
        compiler_params=pltpu.CompilerParams(vmem_limit_bytes=VMEM_LIMIT),
        cost_estimate=pl.CostEstimate(flops=1000, bytes_accessed=1000, transcendentals=0),
        name=name,
    )(*args)


def shaped(shape, dtype=BF):
    return jax.ShapeDtypeStruct(shape, dtype)


def three_parts(value):
    high = value.astype(BF)
    rest = value - high.astype(F32)
    middle = rest.astype(BF)
    return high, middle, (rest - middle.astype(F32)).astype(BF)


def query_blocks(seq, step):
    blocks = []
    start = 0
    while start < seq:
        used = min(step, seq - start)
        blocks.append((start, -(-used // 128) * 128, used))
        start += used
    return blocks


def pad_columns(value, width):
    extra = width - value.shape[1]
    if extra == 0:
        return value
    return jnp.concatenate([value, jnp.zeros((value.shape[0], extra), value.dtype)], 1)


def row_blocks(ref, place, start, stop):
    return jnp.concatenate([ref[owner, place, start:stop] for owner in range(ref.shape[0])], 1)


def turned_owner(owner):
    return owner % 2 * 2 + owner // 2


def owners_of(bits_ref, which, mine_ref, other_ref, pick):
    parts = []
    for owner in range(4):
        row, column = owner // 2, owner % 2
        inner, outer = (row, column) if which == 0 else (column, row)
        parts.append(jnp.where(bits_ref[which] == outer, pick(mine_ref, inner), pick(other_ref, inner)))
    return parts


def project_kernel(bits_ref, xa_ref, xb_ref, qk_ref, qk_other, v_ref, v_other, b_ref, out_ref, t_ref, x_s):
    half = xa_ref.shape[0]
    group = pl.program_id(0)

    @pl.when(group == 0)
    def _():
        x_s[0:half] = xa_ref[...]
        x_s[half:] = xb_ref[...]
        t_ref[...] = x_s[...].T

    cols = v_ref.shape[2]
    for i in range(3):
        rows = slice(i * cols, (i + 1) * cols)
        weights = []
        for p in range(PAIR):
            if i == 2:
                parts = owners_of(bits_ref, 1, v_ref, v_other, lambda ref, inner: ref[inner, p])
            else:
                parts = owners_of(bits_ref, 0, qk_ref, qk_other, lambda ref, inner: ref[inner, p, rows])
            weights.append(jnp.concatenate(parts, 1))
        value = dot(jnp.concatenate(weights, 0), x_s[...], ROW_NT) + b_ref[0, i]
        out_ref[0, i] = value.astype(BF).reshape(out_ref.shape[2:])


def project(bits, xa, xb, w_qk, w_vo, bias):
    half, width = xa.shape
    _, places, rows, part = w_qk[0].shape
    cols = rows // 2
    groups = places // PAIR
    heads = PAIR * cols // HEAD_DIM
    whole = pl.BlockSpec((half, width), lambda g, bits: (0, 0))
    return call(
        project_kernel,
        (groups,),
        [whole, whole]
        + [pl.BlockSpec((2, PAIR, rows, part), lambda g, bits: (0, g, 0, 0))] * 2
        + [pl.BlockSpec((2, PAIR, cols, part), lambda g, bits: (0, g, 0, 0))] * 2
        + [pl.BlockSpec((1, 3, PAIR * cols, 1), lambda g, bits: (g, 0, 0, 0))],
        [
            pl.BlockSpec((1, 3, heads, HEAD_DIM, 2 * half), lambda g, bits: (g, 0, 0, 0, 0)),
            pl.BlockSpec((width, 2 * half), lambda g, bits: (0, 0)),
        ],
        [shaped((groups, 3, heads, HEAD_DIM, 2 * half)), shaped((width, 2 * half))],
        (bits, xa, xb, *w_qk, *w_vo, bias),
        [pltpu.VMEM((2 * half, width), BF)],
        name="project",
        prefetch=1,
    )


def attend_kernel(seq, padded, step, q_ref, k_ref, v_ref, *refs):
    o_ref, row_ref, wide_ref, lse_ref, key_s, query_s, value_s, hold_s = refs[-8:]
    key = k_ref[0, 0, 0]
    key_s[...] = jnp.concatenate([key, key, key, jnp.zeros((HEAD_DIM, seq), BF)], 0).T
    parts = three_parts(pad_columns(q_ref[0, 0, 0].astype(F32) * (LOG2E * HEAD_DIM**-0.5), padded))
    query_s[...] = jnp.concatenate([*parts, jnp.zeros((HEAD_DIM, padded), BF)], 0)
    value_s[0:HEAD_DIM] = v_ref[0, 0, 0]
    value_s[HEAD_DIM : HEAD_DIM + 16] = jnp.ones((16, seq), BF)
    for start, width, used in query_blocks(seq, step):
        scores = dot(key_s[...], query_s[:, start : start + width])
        top = jnp.max(scores, 0, keepdims=True)
        prob = jnp.exp2(scores - top).astype(BF)
        mixed = dot(value_s[...], prob)
        total = mixed[HEAD_DIM : HEAD_DIM + 1]
        result = (mixed[0:HEAD_DIM] * (1.0 / total))[:, :used]
        wide_ref[0, :, start : start + used] = result
        o_ref[0, :, start : start + used] = result.astype(BF)
        lse_ref[0, :, start : start + used] = (top + jnp.log2(total))[:, :used]
    odd = pl.program_id(0) % 2
    hold_s[pl.ds(pl.multiple_of(odd * HEAD_DIM, HEAD_DIM), HEAD_DIM)] = o_ref[0]

    @pl.when(odd == 1)
    def _():
        row_ref[...] = hold_s[...].T


def attend(qkv, group, step, into=()):
    groups, _, heads, _, seq = qkv.shape
    padded = -(-seq // 128) * 128
    part = lambda i: pl.BlockSpec((1, 1, 1, HEAD_DIM, seq), lambda h: (group, i, h, 0, 0))
    spec = lambda rows: pl.BlockSpec((1, rows, seq), lambda h: (group * heads + h, 0, 0))
    total = groups * heads
    return call(
        functools.partial(attend_kernel, seq, padded, step),
        (heads,),
        [part(0), part(1), part(2)] + [pl.BlockSpec(memory_space=pl.ANY)] * len(into),
        [
            spec(HEAD_DIM),
            pl.BlockSpec((seq, 2 * HEAD_DIM), lambda h: (0, group * heads // 2 + h // 2)),
            spec(HEAD_DIM),
            spec(1),
        ],
        [
            shaped((total, HEAD_DIM, seq)),
            shaped((seq, total * HEAD_DIM)),
            shaped((total, HEAD_DIM, seq), F32),
            shaped((total, 1, seq), F32),
        ],
        (qkv, qkv, qkv, *into),
        [
            pltpu.VMEM((seq, 4 * HEAD_DIM), BF),
            pltpu.VMEM((4 * HEAD_DIM, padded), BF),
            pltpu.VMEM((HEAD_DIM + 16, seq), BF),
            pltpu.VMEM((2 * HEAD_DIM, seq), BF),
        ],
        name="attend",
        aliases={3 + i: i for i in range(len(into))},
    )


def attend_back_kernel(
    seq, padded, step, q_ref, k_ref, v_ref, d_ref, lse_ref, delta_ref, out_ref, sum_ref, key_s, query_s, value_s, dmix_s, hold_s
):
    key = k_ref[0, 0, 0]
    ones = jnp.ones((16, seq), BF)
    key_s[...] = jnp.concatenate([key, key, key, ones, jnp.zeros((48, seq), BF)], 0).T
    value_s[...] = jnp.concatenate([v_ref[0, 0, 0], ones, jnp.zeros((48, seq), BF)], 0).T
    query = pad_columns(q_ref[0, 0, 0], padded).astype(F32)
    blank = jnp.zeros((13, padded), BF)
    tail = jnp.zeros((48, padded), BF)
    lse = jnp.concatenate([*three_parts(pad_columns(-lse_ref[0], padded)), blank], 0)
    delta = jnp.concatenate([*three_parts(pad_columns(-delta_ref[0], padded)), blank], 0)
    query_s[...] = jnp.concatenate([*three_parts(query * (LOG2E * HEAD_DIM**-0.5)), lse, tail], 0)
    dmix_s[...] = jnp.concatenate([pad_columns(d_ref[0], padded), delta, tail], 0)
    scaled = (query * HEAD_DIM**-0.5).astype(BF)
    odd = pl.program_id(0) % 2
    here = pl.ds(pl.multiple_of(odd * HEAD_DIM, HEAD_DIM), HEAD_DIM)
    d_keys = jnp.zeros((HEAD_DIM, seq), F32)
    d_values = jnp.zeros((HEAD_DIM, seq), F32)
    for start, width, used in query_blocks(seq, step):
        prob = jnp.exp2(dot(key_s[...], query_s[:, start : start + width]))
        d_scores = (prob * dot(value_s[...], dmix_s[:, start : start + width])).astype(BF)
        d_values = d_values + dot(dmix_s[0:HEAD_DIM, start : start + width], prob.astype(BF), ROW_NT)
        d_keys = d_keys + dot(scaled[:, start : start + width], d_scores, ROW_NT)
        d_query = dot(key, d_scores) * HEAD_DIM**-0.5
        hold_s[0, here, start : start + used] = d_query[:, :used].astype(BF)
    hold_s[1, here] = d_keys.astype(BF)
    hold_s[2, here] = d_values.astype(BF)

    @pl.when(odd == 1)
    def _():
        for i in range(3):
            turned = hold_s[i].T
            out_ref[i] = turned
            sum_ref[i] = jnp.sum(turned.astype(F32), 0, keepdims=True)


def attend_backward(qkv, d_mixed, lse, delta, group, first, count, step):
    _, _, inner, _, seq = qkv.shape
    padded = -(-seq // 128) * 128
    part = lambda i: pl.BlockSpec((1, 1, 1, HEAD_DIM, seq), lambda h: (group, i, first + h, 0, 0))
    spec = lambda rows: pl.BlockSpec((1, rows, seq), lambda h: (group * inner + first + h, 0, 0))
    return call(
        functools.partial(attend_back_kernel, seq, padded, step),
        (count,),
        [part(0), part(1), part(2), spec(HEAD_DIM), spec(1), spec(1)],
        [
            pl.BlockSpec((3, seq, 2 * HEAD_DIM), lambda h: (0, 0, h // 2)),
            pl.BlockSpec((3, 1, 2 * HEAD_DIM), lambda h: (0, 0, h // 2)),
        ],
        [shaped((3, seq, count * HEAD_DIM)), shaped((3, 1, count * HEAD_DIM), F32)],
        (qkv, qkv, qkv, d_mixed, lse, delta),
        [
            pltpu.VMEM((seq, 4 * HEAD_DIM), BF),
            pltpu.VMEM((4 * HEAD_DIM, padded), BF),
            pltpu.VMEM((seq, 2 * HEAD_DIM), BF),
            pltpu.VMEM((2 * HEAD_DIM, padded), BF),
            pltpu.VMEM((3, 2 * HEAD_DIM, seq), BF),
        ],
        name="attend_backward",
    )


def mix_kernel(o_ref, w_ref, out_ref):
    places, cols = w_ref.shape[1:3]
    weights = [row_blocks(w_ref, j, 0, cols) for j in range(places)]
    out_ref[...] = dot(o_ref[...], jnp.concatenate(weights, 0)).astype(out_ref.dtype)


def mix(rows, weights, which, dtype):
    seq, wide = rows.shape
    owners, places, _, part = weights.shape
    cols = wide // places
    half = seq // 2
    return call(
        mix_kernel,
        (2,),
        [
            pl.BlockSpec((half, wide), lambda n: (which, 0)),
            pl.BlockSpec((owners // 2, places, cols, part), lambda n: (n, 0, 1, 0)),
        ],
        pl.BlockSpec((half, owners * part // 2), lambda n: (0, n)),
        shaped((half, owners * part), dtype),
        (rows, weights),
        name="mix",
    )


def mix_back_kernel(bits_ref, da_ref, db_ref, w_ref, o_ref, wide_ref, d_ref, delta_ref, *refs):
    *grad_refs, d_s = refs
    half, width = da_ref.shape
    cols = w_ref.shape[2]
    heads = o_ref.shape[0]

    @pl.when(pl.program_id(0) == 0)
    def _():
        d_s[0:half] = da_ref[...]
        d_s[half:] = db_ref[...]

    weights = jnp.concatenate([row_blocks(w_ref, p, 0, cols) for p in range(PAIR)], 0)
    d_heads = dot(weights, d_s[...], ROW_NT).astype(BF).reshape(o_ref.shape)
    d_ref[...] = d_heads
    delta_ref[...] = jnp.sum(d_heads.astype(F32) * wide_ref[...], 1, keepdims=True)
    grad = dot(o_ref[...].reshape(heads * HEAD_DIM, 2 * half), d_s[...]).astype(BF).T
    for p in range(PAIR):
        part = grad[:, p * cols : (p + 1) * cols]
        put_halves(bits_ref, part, p, grad_refs[2 * p], grad_refs[2 * p + 1], (slice(None), 0))


def mix_back(bits, da, db, weights, mixed, wide):
    half, width = da.shape
    owners, places, _, part = weights.shape
    heads, _, seq = mixed.shape
    groups = places // PAIR
    cols = heads * HEAD_DIM // places
    whole = pl.BlockSpec((half, width), lambda g, bits: (0, 0))
    spec = lambda rows: pl.BlockSpec((heads // groups, rows, seq), lambda g, bits: (g, 0, 0))
    grad = pl.BlockSpec((2, 1, width // 4, cols), lambda g, bits: (0, g, 0, 0))
    d_heads, delta, keep_a, send_a, keep_b, send_b = call(
        mix_back_kernel,
        (groups,),
        [whole, whole, pl.BlockSpec((owners, PAIR, cols, part), lambda g, bits: (0, g, 1, 0)), spec(HEAD_DIM), spec(HEAD_DIM)],
        [spec(HEAD_DIM), spec(1)] + [grad] * 4,
        [shaped((heads, HEAD_DIM, seq)), shaped((heads, 1, seq), F32)] + [shaped((2, groups, width // 4, cols))] * 4,
        (bits, da, db, weights, mixed, wide),
        [pltpu.VMEM((seq, width), BF)],
        name="mix_back",
        prefetch=1,
    )
    return d_heads, delta, (keep_a, keep_b), (send_a, send_b)


def project_grad_kernel(bits_ref, t_ref, da_ref, db_ref, *refs):
    cols = da_ref.shape[2]
    grad = dot(t_ref[...], jnp.concatenate([da_ref[0], db_ref[0]], 1)).astype(BF)
    for p in range(PAIR):
        put_halves(bits_ref, grad[:, p * cols : (p + 1) * cols], p, refs[2 * p], refs[2 * p + 1], (slice(None), 0))


def project_grads(bits, turned, da, db):
    width, seq = turned.shape
    cols = da.shape[2]
    piece = pl.BlockSpec((1, seq, cols), lambda i, bits: (i, 0, 0))
    grad = pl.BlockSpec((2, 1, width // 4, cols), lambda i, bits: (0, i, 0, 0))
    keep_a, send_a, keep_b, send_b = call(
        project_grad_kernel,
        (3,),
        [pl.BlockSpec((width, seq), lambda i, bits: (0, 0)), piece, piece],
        [grad] * 4,
        [shaped((2, 3, width // 4, cols))] * 4,
        (bits, turned, da, db),
        name="project_grads",
        prefetch=1,
    )
    return (keep_a, keep_b), (send_a, send_b)


def project_back_kernel(a_ref, b_ref, c_ref, d_ref, qk_ref, v_ref, out_ref):
    total = None
    for first, refs in ((0, (a_ref, b_ref)), (PAIR, (c_ref, d_ref))):
        places = [first + p for p in range(PAIR)]
        left = [ref[i] for i in range(3) for ref in refs]
        right = [qk_ref[0, place, i] for i in range(2) for place in places] + [v_ref[0, place] for place in places]
        part = dot(jnp.concatenate(left, 1), jnp.concatenate(right, 0))
        total = part if total is None else total + part
    out_ref[...] = total


def project_back(pieces, w_qk, w_vo, which):
    seq = pieces[0].shape[1]
    owners, places, _, cols, part = w_qk.shape
    half = seq // 2
    return call(
        project_back_kernel,
        (owners,),
        [pl.BlockSpec((3, half, cols), lambda n: (0, which, 0)) for piece in pieces]
        + [
            pl.BlockSpec((1, places, 2, cols, part), lambda n: (turned_owner(n), 0, 0, 0, 0)),
            pl.BlockSpec((1, places, cols, part), lambda n: (n, 0, 0, 0)),
        ],
        pl.BlockSpec((half, part), lambda n: (0, n)),
        shaped((half, owners * part), F32),
        (*pieces, w_qk, w_vo),
        name="project_back",
    )


def gelu_pair(value):
    cdf = 0.5 * (1.0 + lax.erf(value * 0.7071067811865476))
    return value * cdf, cdf + value * (jnp.exp(-0.5 * value * value) * 0.3989422804014327)


def all_blocks(ref):
    return jnp.concatenate([ref[0, t] for t in range(ref.shape[1])], 1)


def relative_block(block, place, blocks):
    return lax.rem(block + blocks - place, blocks)


def either(first_ref, last_ref, index, pick):
    half = first_ref.shape[1]
    one = pick(first_ref, jnp.minimum(index, half - 1))
    return jnp.where(index < half, one, pick(last_ref, jnp.maximum(index - half, 0)))


def ffn_kernel(place_ref, x_ref, one_ref, two_ref, last_ref, b_ref, out_ref, g_ref, slope_ref, hold_s):
    blocks = hold_s.shape[0]
    step = pl.program_id(0)

    @pl.when(step < blocks)
    def _():
        ones = jnp.concatenate([one_ref[turned_owner(owner), 0] for owner in range(one_ref.shape[0])], 0)
        twos = two_ref[...].reshape(ones.shape)
        weights = jnp.where(relative_block(step, place_ref[0], blocks) < blocks // 2, ones, twos)
        pre = dot(x_ref[...], weights) + b_ref[0]
        active, slope = gelu_pair(pre)
        active = active.astype(BF)
        hold_s[step] = active
        g_ref[...] = active
        slope_ref[...] = slope.astype(BF)

    @pl.when(step >= blocks)
    def _():
        left = jnp.concatenate([hold_s[t] for t in range(blocks)], 1)
        out_ref[...] = dot(left, all_blocks(last_ref), ROW_NT).astype(out_ref.dtype)


def ffn_specs(rows, down):
    owners, blocks, part, units = down.shape
    early = lambda s: jnp.minimum(s, blocks - 1)
    late = lambda s: jnp.maximum(s - blocks, 0)
    return (
        blocks,
        early,
        late,
        pl.BlockSpec((rows, owners * part), lambda s, place: (0, 0)),
        pl.BlockSpec((rows, units), lambda s, place: (0, early(s))),
        pl.BlockSpec((1, 1, units), lambda s, place: (early(s), 0, 0)),
        pl.BlockSpec((rows, part), lambda s, place: (0, late(s))),
    )


def ffn_forward(place, x, up, down, bias, dtype):
    rows, width = x.shape
    owners, blocks, part, units = down.shape
    blocks, early, late, whole, column, thin, out = ffn_specs(rows, down)
    index = lambda s, place: relative_block(early(s), place[0], blocks)
    return call(
        ffn_kernel,
        (blocks + owners,),
        [
            whole,
            pl.BlockSpec((owners, 1, part, units), lambda s, place: (0, jnp.minimum(index(s, place), PAIR - 1), 0, 0)),
            pl.BlockSpec((owners, 1, part, units), lambda s, place: (0, jnp.maximum(index(s, place) - PAIR, 0), 0, 0)),
            pl.BlockSpec((1, blocks, part, units), lambda s, place: (late(s), 0, 0, 0)),
            thin,
        ],
        [out, column, column],
        [shaped((rows, width), dtype), shaped((rows, blocks * units)), shaped((rows, blocks * units))],
        (place, x, *up, down, bias),
        [pltpu.VMEM((blocks, rows, units), BF)],
        name="ffn",
        prefetch=1,
    )


def ffn_back_kernel(place_ref, d_ref, first_ref, one_ref, two_ref, slope_ref, out_ref, dpre_ref, sum_ref, hold_s):
    blocks = hold_s.shape[0]
    step = pl.program_id(0)

    @pl.when(step < blocks)
    def _():
        d_pre = (dot(d_ref[...], first_ref[...].reshape(d_ref.shape[1], -1)) * slope_ref[...].astype(F32)).astype(BF)
        hold_s[step] = d_pre
        dpre_ref[...] = d_pre
        sum_ref[0] = jnp.sum(d_pre.astype(F32), 0, keepdims=True)

    @pl.when(step >= blocks)
    def _():
        left = jnp.concatenate([hold_s[t] for t in range(blocks)], 1)
        order = [relative_block(t, place_ref[0], blocks) for t in range(blocks)]
        weights = [either(one_ref, two_ref, index, lambda ref, i: ref[0, i]) for index in order]
        out_ref[...] = dot(left, jnp.concatenate(weights, 1), ROW_NT).astype(out_ref.dtype)


def ffn_backward(place, d_out, up, down, slope, dtype):
    rows, width = d_out.shape
    owners, blocks, part, units = down.shape
    blocks, early, late, whole, column, thin, out = ffn_specs(rows, down)
    return call(
        ffn_back_kernel,
        (blocks + owners,),
        [
            whole,
            pl.BlockSpec((owners, 1, part, units), lambda s, place: (0, early(s), 0, 0)),
            pl.BlockSpec((1, PAIR, part, units), lambda s, place: (turned_owner(late(s)), 0, 0, 0)),
            pl.BlockSpec((1, PAIR, part, units), lambda s, place: (late(s), 0, 0, 0)),
            column,
        ],
        [out, column, thin],
        [shaped((rows, width), dtype), shaped((rows, blocks * units)), shaped((blocks, 1, units), F32)],
        (place, d_out, down, *up, slope),
        [pltpu.VMEM((blocks, rows, units), BF)],
        name="ffn_backward",
        prefetch=1,
    )


def put_halves(bits_ref, grad, which, keep_ref, send_ref, at):
    grad = grad.reshape((2, 2, grad.shape[0] // 4) + grad.shape[1:])
    pair = (grad[:, 0], grad[:, 1]) if which == 0 else (grad[0], grad[1])
    low = bits_ref[which] == 0
    keep_ref[at] = jnp.where(low, pair[0], pair[1])
    send_ref[at] = jnp.where(low, pair[1], pair[0])


def ffn_grad_kernel(bits_ref, xa_ref, xb_ref, ca_ref, cb_ref, keep_a, send_a, keep_b, send_b, x_s):
    step = pl.program_id(0)

    @pl.when(step == 0)
    def _():
        x_s[...] = jnp.concatenate([xa_ref[...], xb_ref[...]], 0).T

    column = jnp.concatenate([ca_ref[...], cb_ref[...]], 0)
    grad = dot(x_s[...], column).astype(BF)

    @pl.when(step < PAIR)
    def _():
        put_halves(bits_ref, grad, 0, keep_a, send_a, (slice(None), 0))

    @pl.when(step >= PAIR)
    def _():
        put_halves(bits_ref, grad, 1, keep_b, send_b, (slice(None), 0))


def ffn_grad(bits, xa, xb, ca, cb, blocks):
    rows, width = xa.shape
    units = ca.shape[1] // blocks
    whole = pl.BlockSpec((rows, width), lambda t, bits: (0, 0))
    column = pl.BlockSpec((rows, units), lambda t, bits: (0, t))
    first = pl.BlockSpec((2, 1, width // 4, units), lambda t, bits: (0, jnp.minimum(t, PAIR - 1), 0, 0))
    last = pl.BlockSpec((2, 1, width // 4, units), lambda t, bits: (0, jnp.maximum(t - PAIR, 0), 0, 0))
    keep_a, send_a, keep_b, send_b = call(
        ffn_grad_kernel,
        (blocks,),
        [whole, whole, column, column],
        [first, first, last, last],
        [shaped((2, PAIR, width // 4, units))] * 4,
        (bits, xa, xb, ca, cb),
        [pltpu.VMEM((width, 2 * rows), BF)],
        name="ffn_grad",
        prefetch=1,
    )
    return (keep_a, keep_b), (send_a, send_b)


def add_kernel(bits_ref, *refs):
    count = len(refs) // 3
    for i in range(count):
        refs[2 * count + i][...] = (refs[2 * i][0].astype(F32) + refs[2 * i + 1][0].astype(F32)).astype(BF)


def add_middle(bits, keeps, parts):
    _, blocks, rows, units = keeps[0].shape
    args, in_specs = [], []
    for i, pair in enumerate(zip(keeps, parts)):
        args += pair
        in_specs += [pl.BlockSpec((1, 1, rows, units), lambda s, bits, i=i: (1 - bits[1 - i % 2], s, 0, 0))] * 2
    return call(
        add_kernel,
        (blocks,),
        in_specs,
        [pl.BlockSpec((1, rows, units), lambda s, bits: (s, 0, 0))] * len(keeps),
        [shaped((blocks, rows, units))] * len(keeps),
        (bits, *args),
        name="add_middle",
        prefetch=1,
    )


def add_end_kernel(bits_ref, *refs):
    for i in range(len(refs) // 3):
        keep, part, end = refs[3 * i : 3 * i + 3]
        total = keep[0, 0].astype(F32) + part[0, 0].astype(F32) + end[0].astype(F32)
        refs[-1][i % 2, 0, i // 2] = total.astype(BF)


def add_end(bits, keeps, parts, ends):
    _, blocks, rows, units = keeps[0].shape
    args, in_specs = [], []
    for i, triple in enumerate(zip(keeps, parts, ends)):
        args += triple
        in_specs += [pl.BlockSpec((1, 1, rows, units), lambda s, bits, i=i: (bits[1 - i % 2], s, 0, 0))] * 2
        in_specs.append(pl.BlockSpec((1, rows, units), lambda s, bits: (s, 0, 0)))
    count = len(keeps) // 2
    return call(
        add_end_kernel,
        (blocks,),
        in_specs,
        pl.BlockSpec((2, 1, count, rows, units), lambda s, bits: (0, s, 0, 0, 0)),
        shaped((2, blocks, count, rows, units)),
        (bits, *args),
        name="add_end",
        prefetch=1,
    )


def norm_back_block(da_ref, db_ref, x_ref, rest_ref, gain_ref, sum_ref):
    d_value = da_ref[...] + db_ref[...].astype(F32)
    value = x_ref[...].astype(F32)
    centred = value - jnp.mean(value, -1, keepdims=True)
    scale = lax.rsqrt(jnp.mean(centred * centred, -1, keepdims=True) + EPS)
    unit = centred * scale
    d_unit = d_value * gain_ref[...]
    inner = jnp.mean(d_unit * unit, -1, keepdims=True)
    rest = rest_ref[...]
    result = rest + scale * (d_unit - jnp.mean(d_unit, -1, keepdims=True) - unit * inner)
    parts = [d_value * unit, d_value, result, rest]
    sums = jnp.concatenate([jnp.sum(part, 0, keepdims=True) for part in parts] + [jnp.zeros((4, value.shape[1]), F32)], 0)

    @pl.when(pl.program_id(0) == 0)
    def _():
        sum_ref[...] = sums

    @pl.when(pl.program_id(0) > 0)
    def _():
        sum_ref[...] += sums

    return result


def norm_back_kernel(da_ref, db_ref, x_ref, rest_ref, gain_ref, out_ref, low_ref, sum_ref):
    result = norm_back_block(da_ref, db_ref, x_ref, rest_ref, gain_ref, sum_ref)
    out_ref[...] = result
    low_ref[...] = result.astype(BF)


def norm_back_halves_kernel(da_ref, db_ref, x_ref, rest_ref, gain_ref, near_ref, far_ref, sum_ref):
    result = norm_back_block(da_ref, db_ref, x_ref, rest_ref, gain_ref, sum_ref).astype(BF)

    @pl.when(pl.program_id(0) == 0)
    def _():
        near_ref[...] = result

    @pl.when(pl.program_id(0) == 1)
    def _():
        far_ref[...] = result


def norm_backward(da, db, x, rest, gain, halves):
    rows, width = da.shape
    steps = 2 if halves else 1
    row = pl.BlockSpec((rows // steps, width), lambda i: (i, 0))
    whole = lambda count: pl.BlockSpec((count, width), lambda i: (0, 0))
    return call(
        norm_back_halves_kernel if halves else norm_back_kernel,
        (steps,),
        [row] * 4 + [whole(1)],
        [whole(rows // 2)] * 2 + [whole(8)] if halves else [row, row, whole(8)],
        ([shaped((rows // 2, width))] * 2 if halves else [shaped((rows, width), F32), shaped((rows, width))])
        + [shaped((8, width), F32)],
        (da, db, x, rest, gain[None]),
        name="norm_backward",
    )


def swap(value, axis):
    return lax.ppermute(value, axis, [(0, 1), (1, 0)])


def after(value, *others):
    return lax.optimization_barrier((value, *others))[0]


def together(*values):
    return lax.optimization_barrier(values)


def ordered(bit, mine, other, axis):
    return jnp.concatenate([jnp.where(bit == 0, mine, other), jnp.where(bit == 0, other, mine)], axis)


def chosen(value, bit, axis):
    return lax.dynamic_index_in_dim(value, bit, axis, keepdims=False)


def added(mine, other):
    return (mine.astype(F32) + other.astype(F32)).astype(BF)


def moments(value):
    mean = jnp.mean(value, -1, keepdims=True)
    centred = value - mean
    scale = lax.rsqrt(jnp.mean(centred * centred, -1, keepdims=True) + EPS)
    return centred, scale


def clip_local(clips, w_qkv, w_out, w_up, w_down, norm_gain, shifts, bias_qv, up_bias, teacher):
    y, x, c, t = (lax.axis_index(name) for name in ("y", "x", "c", "t"))
    every = ("y", "x", "c", "t")
    steps = 4
    width = clips.shape[2]
    odd = t % 2

    first_way, second_way = [], []
    for column in range(4):
        for core in range(2):
            for place in range(4):
                source = (column * 2 + core) * 4 + place
                to = (column * 2 + place // 2) * 4 + 2 * core
                first_way.append((source, to + place % 2))
                second_way.append((source, to + 1 - place % 2))
    first_way = [(a, b) for a, b in first_way if a != b]
    back = lambda way: [(b, a) for a, b in way]
    stays = t // 2 == c

    def sent(pair):
        return lax.ppermute(pair[0], every, first_way), lax.ppermute(pair[1], every, second_way)

    def to_chip(value):
        return sent((chosen(value, odd, 0), chosen(value, 1 - odd, 0)))

    def sent_back(near, far):
        return lax.ppermute(near, every, back(first_way)), lax.ppermute(far, every, back(second_way))

    def from_chip(value):
        half = value.shape[0] // 2
        return sent_back(value[:half], value[half:])

    rings = [[(i, (i + away) % steps) for i in range(steps)] for away in range(steps)]

    def ring_gather(value):
        return tuple(lax.ppermute(value, "t", rings[-j % steps]) for j in range(1, steps))

    def ring_scatter(blocks):
        return tuple(lax.ppermute(blocks[j], "t", rings[j]) for j in range(1, steps))

    def placed(value, axis):
        return lax.dynamic_slice_in_dim(jnp.concatenate([value, value], axis), steps - t, steps, axis)

    def on_chip(value, near, far):
        return jnp.concatenate([jnp.where(stays, chosen(value, odd, 0), near), far])

    def as_clips(mine, near, far):
        near = jnp.where(stays, mine, near)
        return jnp.stack([jnp.where(odd == 0, near, far), jnp.where(odd == 0, far, near)])

    def scatter_start(sends):
        return swap(sends[0], "x"), swap(sends[1], "y")

    def sums_of(keeps, parts, row, column):
        pick = lambda values, bit: jnp.concatenate([chosen(value, bit, 0) for value in values])
        first = pick(keeps[0], row).astype(F32) + chosen(parts[0], row, 0).astype(F32)
        return first, pick(keeps[1], column).astype(F32) + chosen(parts[1], column, 0).astype(F32)

    def scatter_middle(keeps, parts):
        first, second = sums_of(keeps, parts, 1 - y, 1 - x)
        return swap(first.astype(BF), "y"), swap(second.astype(BF), "x")

    def scatter_end(keeps, parts, ends):
        first, second = sums_of(keeps, parts, y, x)
        return (first + ends[0].astype(F32)).astype(BF), (second + ends[1].astype(F32)).astype(BF)

    dims = w_qkv.shape[1]
    cols = w_out.shape[0] // 2
    lane = bias_qv.shape[1]
    units = w_up.shape[1] // 2
    attn = jnp.concatenate([jnp.swapaxes(w_qkv, 1, 2), w_out[None]]).reshape(4, 2, cols, dims)
    mine, other = chosen(attn, c, 1).reshape(4 * cols, dims), chosen(attn, 1 - c, 1).reshape(4 * cols, dims)
    attn_piece = ordered(c, mine, swap(other, "c"), 1)
    ff = jnp.stack([w_up, w_down.T]).reshape(2, dims, 2, units)
    ff_piece = ordered(c, chosen(ff, c, 2), swap(chosen(ff, 1 - c, 2), "c"), 1)

    pad = lambda value: jnp.pad(value, (0, dims - value.shape[0]))[None]
    tails = jnp.concatenate([pad(bias_qv[0]), pad(bias_qv[1]), pad(up_bias), jnp.zeros((7, dims), BF)])
    vectors = jnp.concatenate([norm_gain, shifts, tails])
    for bit, name in ((c, "c"), (x, "x"), (y, "y")):
        vectors = ordered(bit, vectors, swap(vectors, name), 1)
    gains, shift_all = vectors[0:2].astype(F32), vectors[2:6].astype(F32)
    tails = vectors[6:16]
    tails = jnp.stack([part[:3] for part in (tails, *ring_gather(tails))]).astype(F32)
    tails = lax.dynamic_slice_in_dim(tails, 4 * dims * c, 4 * dims, 2)
    pair = tails[:, :2].reshape(steps, 2, 4, dims)[..., :lane]
    bias_pair = jnp.swapaxes(pair, 0, 1).reshape(2, 2, 2 * cols)
    bias_in = jnp.stack([bias_pair[0], jnp.zeros_like(bias_pair[0]), bias_pair[1]], 1)[..., None]
    up_shift = placed(tails[:, 2:3], 0)

    whole = ("y", "x", "t")
    attn_rows = together(*ring_gather(attn_piece))
    near, far = to_chip(after(clips, attn_rows))
    attn_rows = (attn_piece, *attn_rows)
    qk_rows = jnp.stack([part[: 2 * cols] for part in attn_rows])
    vo_rows = jnp.stack([part[2 * cols :] for part in attn_rows])
    targets = chosen(teacher, odd, 0), chosen(teacher, 1 - odd, 0)
    swapped, near, targets, bias_in, up_shift = together(
        (swap(qk_rows, "y"), swap(vo_rows, "x")), near, targets, bias_in, up_shift
    )
    w_qk, w_vo = ordered(y, qk_rows[None], swapped[0][None], 0), ordered(x, vo_rows[None], swapped[1][None], 0)
    swapped, far = together((swap(w_qk, "x"), swap(w_vo, "y")), far)
    bits = jnp.stack([x, y])
    parts_qk, parts_vo = (w_qk, swapped[0]), (w_vo, swapped[1])
    up_piece, down_piece = ff_piece
    up_piece, down_piece, far = together(up_piece, down_piece, far)
    up_rows = ring_gather(up_piece)
    down_all = lax.all_gather(down_piece, whole, axis=0, tiled=False).reshape(4, steps, 2 * dims, units)
    place = t.reshape(1)

    inputs = on_chip(clips, near, far).astype(F32)
    centred_one, scale_one = moments(inputs)
    first = (centred_one * scale_one * gains[0] + shift_all[0]).astype(BF)
    first_other = swap(first, "c")
    half = first.shape[0] // 2
    qkv, turned = project(bits, first, first_other, parts_qk, parts_vo, bias_in)
    parts_qk, parts_vo, qkv = together(parts_qk, parts_vo, qkv)
    w_qk = ordered(x, parts_qk[0][None], parts_qk[1][None], 0).reshape(4, steps, 2, cols, 2 * dims)
    w_vo = ordered(y, parts_vo[0][None], parts_vo[1][None], 0).reshape(4, steps, 2 * cols, 2 * dims)
    mixed, rows, wide, lse = attend(qkv, 0, 1664)
    up_rows, rows = together(up_rows, rows)
    up_a, up_b = jnp.stack([up_piece, up_rows[0]]), jnp.stack(up_rows[1:])
    swapped = swap(up_a, "y"), swap(up_b, "x")
    mixed, rows, wide, lse = attend(qkv, 1, 1664, (mixed, rows, wide, lse))
    swapped, rows = together(swapped, rows)
    up_a, up_b = ordered(y, up_a[None], swapped[0][None], 0), ordered(x, up_b[None], swapped[1][None], 0)
    swapped = swap(up_a, "x"), swap(up_b, "y")
    attn_other = mix(rows, w_vo, 1, BF)
    attn_mine = mix(after(rows, attn_other), w_vo, 0, F32)
    hidden = inputs + (attn_mine + swap(attn_other, "c").astype(F32)) + shift_all[2]

    centred_two, scale_two = moments(hidden)
    second = (centred_two * scale_two * gains[1] + shift_all[1]).astype(BF)
    second_other = swap(second, "c")
    swapped, second = together(swapped, second)
    up_a = ordered(x, up_a[None], swapped[0][None], 0).reshape(4, PAIR, 2 * dims, units)
    up_b = ordered(y, up_b[None], swapped[1][None], 0).reshape(4, PAIR, 2 * dims, units)
    up_all = up_a, up_b
    targets, second, down_all = together(targets, second, down_all)
    near, far = sent(targets)
    out_mine, act_mine, slope_mine = ffn_forward(place, second, up_all, down_all, up_shift, F32)
    out_mine, near = together(out_mine, near)
    out_other, act_other, slope_other = ffn_forward(place, after(second_other, near), up_all, down_all, up_shift, BF)
    out_other, far = together(out_other, far)
    output = hidden + (out_mine + swap(out_other, "c").astype(F32)) + shift_all[3]
    d_out = output - on_chip(teacher, near, far).astype(F32)
    d_ffn = d_out.astype(BF)
    d_ffn_other = swap(d_ffn, "c")
    d_second, d_pre, sum_mine = ffn_backward(place, d_ffn, up_all, down_all, slope_mine, F32)
    d_ffn_other, d_pre = together(d_ffn_other, d_pre)
    d_second_other, d_pre_other, sum_other = ffn_backward(place, d_ffn_other, up_all, down_all, slope_other, BF)
    d_second_swapped = swap(d_second_other, "c")
    up_sum = (sum_mine + sum_other).reshape(steps, units)

    grad_down, sends = ffn_grad(bits, after(d_ffn, d_pre_other), d_ffn_other, act_mine, act_other, steps)
    down = scatter_start(sends)
    result, grad_down = together(output.astype(BF), grad_down)
    out_near, out_far = from_chip(result)
    d_second_swapped, grad_down = together(d_second_swapped, grad_down)
    d_hidden, d_attn, sums_two = norm_backward(d_second, d_second_swapped, hidden, d_out, gains[1], False)
    d_attn_other = swap(d_attn, "c")
    grad_up, sends = ffn_grad(bits, after(second, d_attn), second_other, d_pre, d_pre_other, steps)
    up = scatter_start(sends)
    d_attn_other, grad_up = together(d_attn_other, grad_up)

    d_heads, delta, grad_o, sends_o = mix_back(bits, d_attn, d_attn_other, w_vo, mixed, wide)
    keeps = (*grad_up, *grad_down)
    back_a, sum_a = attend_backward(qkv, d_heads, lse, delta, 1, 0, 2, 256)
    up, down, out_near, back_a = together(up, down, out_near, back_a)
    ends = add_middle(bits, keeps, (*up, *down))
    ends = [swap(part, name) for part, name in zip(ends, ("y", "x", "y", "x"))]
    back_b, sum_b = attend_backward(qkv, after(d_heads, back_a), lse, delta, 1, 2, 2, 256)
    ends, out_far, back_b = together(ends, out_far, back_b)
    grad_ff = add_end(bits, keeps, (*up, *down), ends).reshape(steps * 4 * dims, units)
    ff_total = lax.psum_scatter(grad_ff, "t", scatter_dimension=0, tiled=True)
    grad_one, sends = project_grads(bits, turned, back_a, back_b)
    one = scatter_start([jnp.concatenate(pair, 1) for pair in zip(sends, sends_o)])
    grad_one = list(zip(grad_one, grad_o))
    delta, grad_ff, grad_one = together(delta, grad_ff, grad_one)
    back_c, sum_c = attend_backward(qkv, after(d_heads, back_b), lse, delta, 0, 2, 2, 256)
    one, back_c = together(one, back_c)
    one_ends = scatter_middle(grad_one, one)
    back_d, sum_d = attend_backward(qkv, after(d_heads, back_c), lse, delta, 0, 0, 2, 256)
    one_ends, back_d = together(one_ends, back_d)
    grad_two, sends = project_grads(bits, turned, back_d, back_c)
    two = scatter_start(sends)
    pieces = (back_d, back_c, back_a, back_b)
    d_first_other = project_back(pieces, w_qk, after(w_vo, grad_two), 1)
    d_first_swapped = swap(d_first_other, "c")
    one = scatter_end(grad_one, one, one_ends)
    early = [lax.ppermute(jnp.concatenate([one[p][:3], one[p][4:]]), "t", rings[PAIR + p]) for p in range(PAIR)]
    two, d_first_other = together(two, d_first_other)
    two_ends = scatter_middle([[keep] for keep in grad_two], two)
    d_first = project_back(pieces, w_qk, after(w_vo, d_first_other), 0)
    ff_total, d_first = together(ff_total, d_first)
    d_first_swapped, d_first = together(d_first_swapped, d_first)
    *d_inputs, sums_one = norm_backward(d_first, d_first_swapped, inputs, d_hidden, gains[0], True)
    early, sums_one = together(early, sums_one)
    grad_near, grad_far = sent_back(*d_inputs)
    small = (sum_a, sum_b, sum_c, sum_d, up_sum, sums_one)
    small, d_inputs = together(small, d_inputs)
    two_ends, grad_near, out_near, out_far = together(two_ends, grad_near, out_near, out_far)
    sum_a, sum_b, sum_c, sum_d, up_sum, sums_one = small
    two = scatter_end([[keep] for keep in grad_two], two, two_ends)
    late = lax.ppermute(jnp.concatenate([two[1], one[1][3:4]]), "t", rings[1])

    grad_ff = ff_total.astype(F32).reshape(2, 2, dims, units)
    grad_ff = ordered(c, chosen(grad_ff, c, 1), swap(chosen(grad_ff, 1 - c, 1), "c"), 2)
    grad_attn = jnp.concatenate([two[0], one[0][3:4]]).astype(F32)
    grad_attn = sum((part.astype(F32) for part in (*early, late)), grad_attn).reshape(4, 2, dims, cols)
    grad_attn = ordered(c, chosen(grad_attn, c, 1), swap(chosen(grad_attn, 1 - c, 1), "c"), 2)

    heads_sum = jnp.concatenate([sum_d, sum_c, sum_a, sum_b], 2).reshape(3, steps, 4, lane)
    heads_sum = placed(jnp.stack([heads_sum[0], heads_sum[2]]), 1)
    heads_sum = jnp.pad(heads_sum, ((0, 0), (0, 0), (0, 0), (0, dims - lane))).reshape(2 * steps, 4 * dims)
    own = jnp.concatenate([heads_sum, up_sum])
    own = jnp.concatenate([jnp.where(c == 0, own, 0.0), jnp.where(c == 1, own, 0.0)], 1)
    normed = [sums_one[0:1], sums_two[0:1], sums_one[1:2], sums_two[1:4]]
    sums = jnp.concatenate(normed + [jnp.zeros((2, width), F32), own])
    for bit, name in ((y, "y"), (x, "x"), (c, "c")):
        half = sums.shape[1] // 2
        part = lambda which: lax.dynamic_slice_in_dim(sums, which * half, half, 1)
        sums = part(bit) + swap(part(1 - bit), name)
    sums, grad_near = together(sums, grad_near)
    sums = sum((lax.ppermute(sums, "t", rings[away]) for away in range(1, steps)), sums)
    thin = width // 32
    vector_sums = lax.dynamic_slice_in_dim(sums[:6], thin * t, thin, 1)
    place_sums = lax.dynamic_index_in_dim(sums[8:].reshape(3, steps, dims), t, 1, keepdims=False)
    return (
        as_clips(result[: result.shape[0] // 2], out_near, out_far),
        as_clips(d_inputs[0], grad_near, grad_far),
        grad_attn[:3],
        grad_attn[3].T,
        grad_ff[0],
        grad_ff[1].T,
        vector_sums[:2],
        vector_sums[2:],
        place_sums[:2, :lane],
        place_sums[2],
    )


def clip_per_chip(mesh):
    fine = Mesh(mesh.devices.reshape(2, 2, 2, 4), ("y", "x", "c", "t"))
    dp = ("y", "x", "c")
    in_specs = (
        P(dp, "t", None),
        P(None, dp, "t"),
        P("t", dp),
        P(dp, "t"),
        P("t", dp),
        P(None, dp),
        P(None, dp),
        P(None, ("t",) + dp),
        P(("t",) + dp),
        P(dp, "t", None),
    )
    out_specs = in_specs[:1] * 2 + in_specs[1:5] + (
        P(None, dp + ("t",)),
        P(None, dp + ("t",)),
        P(None, ("t",) + dp),
        P(("t",) + dp),
    )
    return jax.shard_map(clip_local, mesh=fine, in_specs=in_specs, out_specs=out_specs, check_vma=False)


def solution(mesh):
    if dict(mesh.shape) == {"dp": 8, "tensor": 4}:
        return clip_per_chip(mesh)
    in_specs = (
        P("dp", "tensor", None),
        P(None, "dp", "tensor"),
        P("tensor", "dp"),
        P("dp", "tensor"),
        P("tensor", "dp"),
        P(None, "dp"),
        P(None, "dp"),
        P(None, ("tensor", "dp")),
        P(("tensor", "dp")),
        P("dp", "tensor", None),
    )
    out_specs = (
        P("dp", "tensor", None),
        P("dp", "tensor", None),
        P(None, "dp", "tensor"),
        P("tensor", "dp"),
        P("dp", "tensor"),
        P("tensor", "dp"),
        P(None, ("dp", "tensor")),
        P(None, ("dp", "tensor")),
        P(None, ("tensor", "dp")),
        P(("tensor", "dp")),
    )
    return jax.shard_map(local, mesh=mesh, in_specs=in_specs, out_specs=out_specs, check_vma=False)
```

```python
import functools

import jax
import jax.numpy as jnp
from jax import lax
from jax.experimental import pallas as pl
from jax.experimental.pallas import tpu as pltpu
from jax.sharding import Mesh, PartitionSpec as P

HEAD_DIM = 64


EPS = 1e-05


def layer_norm(value, gain, shift):
    mean = jnp.mean(value, -1, keepdims=True)
    centred = value - mean
    spread = jnp.mean(centred * centred, -1, keepdims=True)
    return centred * lax.rsqrt(spread + EPS) * gain + shift


def exact_gelu(value):
    return jax.nn.gelu(value, approximate=False)


def attend_clip(query, keys, values, scale):
    scores = jnp.einsum("qhe,khe->hqk", query, keys, preferred_element_type=jnp.float32) * scale
    top = jnp.max(scores, -1, keepdims=True)
    expd = jnp.exp(scores - top)
    total = jnp.sum(expd, -1, keepdims=True)
    prob = (expd / total).astype(jnp.bfloat16)
    mixed = jnp.einsum("hqk,khe->qhe", prob, values, preferred_element_type=jnp.float32)
    return (mixed.astype(jnp.bfloat16), (top + jnp.log(total))[..., 0])


def attend_back(query, keys, values, d_mixed, logsum, scale):
    scores = jnp.einsum("qhe,khe->hqk", query, keys, preferred_element_type=jnp.float32) * scale
    prob = jnp.exp(scores - logsum[:, :, None])
    d_prob = jnp.einsum("qhe,khe->hqk", d_mixed, values, preferred_element_type=jnp.float32)
    delta = jnp.sum(d_prob * prob, -1, keepdims=True)
    d_scores = (prob * (d_prob - delta)).astype(jnp.bfloat16)
    d_values = jnp.einsum(
        "hqk,qhe->khe", prob.astype(jnp.bfloat16), d_mixed, preferred_element_type=jnp.float32
    )
    d_query = jnp.einsum("hqk,khe->qhe", d_scores, keys, preferred_element_type=jnp.float32) * scale
    d_keys = jnp.einsum("hqk,qhe->khe", d_scores, query, preferred_element_type=jnp.float32) * scale
    return jnp.stack([d_query, d_keys, d_values]).astype(jnp.bfloat16)


def local(clips, w_qkv, w_out, w_up, w_down, norm_gain, shifts, bias_qv, up_bias, teacher):
    wq, wo, wu, wd, gains, shift_all, bias_pair, up_shift = (
        lax.all_gather(w_qkv, "dp", axis=1, tiled=True),
        lax.all_gather(w_out, "dp", axis=1, tiled=True),
        lax.all_gather(w_up, "dp", axis=0, tiled=True),
        lax.all_gather(w_down, "dp", axis=1, tiled=True),
        lax.all_gather(norm_gain, "dp", axis=1, tiled=True),
        lax.all_gather(shifts, "dp", axis=1, tiled=True),
        lax.all_gather(bias_qv, "dp", axis=1, tiled=True),
        lax.all_gather(up_bias, "dp", axis=0, tiled=True),
    )
    gains = gains.astype(jnp.float32)
    shift_all = shift_all.astype(jnp.float32)
    bias_pair = bias_pair.astype(jnp.float32)
    up_shift = up_shift.astype(jnp.float32)
    width = wq.shape[2]
    heads_here = width // HEAD_DIM
    scale = HEAD_DIM ** (-0.5)
    inputs = jnp.swapaxes(clips, 0, 1).astype(jnp.float32)
    first = layer_norm(inputs, gains[0], shift_all[0]).astype(jnp.bfloat16)
    whole_first = lax.all_gather(first, "tensor", axis=0, tiled=True)
    seq = whole_first.shape[0]
    count = whole_first.shape[1]
    projected = jnp.einsum("scd,kde->ksce", whole_first, wq, preferred_element_type=jnp.float32)
    qkv_bias = jnp.stack([bias_pair[0], jnp.zeros_like(bias_pair[0]), bias_pair[1]])
    qkv = (projected + qkv_bias[:, None, None, :]).astype(jnp.bfloat16)

    def heads(value):
        return jnp.swapaxes(value, 0, 1).reshape(count, seq, heads_here, HEAD_DIM)

    query_h, keys_h, values_h = (heads(qkv[0]), heads(qkv[1]), heads(qkv[2]))
    attended, logsum = lax.map(
        lambda item: attend_clip(item[0], item[1], item[2], scale), (query_h, keys_h, values_h)
    )
    mixed = jnp.swapaxes(attended.reshape(count, seq, width), 0, 1)
    piece = mixed
    attn = lax.psum_scatter(
        jnp.einsum("scd,de->sce", piece, wo, preferred_element_type=jnp.float32),
        "tensor",
        scatter_dimension=0,
        tiled=True,
    )
    hidden = inputs + attn + shift_all[2]
    second = layer_norm(hidden, gains[1], shift_all[1]).astype(jnp.bfloat16)
    whole_second = lax.all_gather(second, "tensor", axis=0, tiled=True)
    pre = jnp.einsum("scd,df->scf", whole_second, wu, preferred_element_type=jnp.float32) + up_shift
    active = exact_gelu(pre).astype(jnp.bfloat16)
    piece = active
    ffn = lax.psum_scatter(
        jnp.einsum("scf,fe->sce", piece, wd, preferred_element_type=jnp.float32),
        "tensor",
        scatter_dimension=0,
        tiled=True,
    )
    output = hidden + ffn + shift_all[3]
    d_out = output - jnp.swapaxes(teacher, 0, 1).astype(jnp.float32)
    whole_d_ffn = lax.all_gather(d_out.astype(jnp.bfloat16), "tensor", axis=0, tiled=True)
    d_active = jnp.einsum("sce,fe->scf", whole_d_ffn, wd, preferred_element_type=jnp.float32)
    grad_down = jnp.einsum("scf,sce->fe", active, whole_d_ffn, preferred_element_type=jnp.float32)
    gelu_value, gelu_back = jax.vjp(exact_gelu, pre)
    d_pre = gelu_back(d_active)[0].astype(jnp.bfloat16)
    grad_up_shift = jnp.sum(d_pre.astype(jnp.float32), (0, 1))
    grad_up = jnp.einsum("scd,scf->df", whole_second, d_pre, preferred_element_type=jnp.float32)
    piece = d_pre
    d_second = lax.psum_scatter(
        jnp.einsum("scf,df->scd", piece, wu, preferred_element_type=jnp.float32),
        "tensor",
        scatter_dimension=0,
        tiled=True,
    )
    norm_value, second_back = jax.vjp(layer_norm, hidden, gains[1], shift_all[1])
    d_hidden_norm, grad_gain_two, grad_shift_two = second_back(d_second)
    d_hidden = d_out + d_hidden_norm
    whole_d_attn = lax.all_gather(d_hidden.astype(jnp.bfloat16), "tensor", axis=0, tiled=True)
    d_mixed = jnp.einsum(
        "sce,de->scd", whole_d_attn, wo, preferred_element_type=jnp.float32
    ).astype(jnp.bfloat16)
    grad_out = jnp.einsum("scd,sce->de", mixed, whole_d_attn, preferred_element_type=jnp.float32)
    d_heads = jnp.swapaxes(d_mixed, 0, 1).reshape(count, seq, heads_here, HEAD_DIM)
    d_stacked = lax.map(
        lambda item: attend_back(item[0], item[1], item[2], item[3], item[4], scale),
        (query_h, keys_h, values_h, d_heads, logsum),
    )
    d_qkv = jnp.transpose(d_stacked.reshape(count, 3, seq, width), (1, 2, 0, 3))
    bias_sums = jnp.sum(d_qkv.astype(jnp.float32), (1, 2))
    grad_pair = jnp.stack([bias_sums[0], bias_sums[2]])
    grad_qkv = jnp.einsum("scd,ksce->kde", whole_first, d_qkv, preferred_element_type=jnp.float32)
    piece = d_qkv
    d_first = lax.psum_scatter(
        jnp.einsum("ksce,kde->scd", piece, wq, preferred_element_type=jnp.float32),
        "tensor",
        scatter_dimension=0,
        tiled=True,
    )
    first_value, first_back = jax.vjp(layer_norm, inputs, gains[0], shift_all[0])
    d_in_norm, grad_gain_one, grad_shift_one = first_back(d_first)
    d_inputs = d_hidden + d_in_norm
    sums = (
        lax.psum_scatter(grad_qkv, "dp", scatter_dimension=1, tiled=True),
        lax.psum_scatter(grad_out, "dp", scatter_dimension=1, tiled=True),
        lax.psum_scatter(grad_up, "dp", scatter_dimension=0, tiled=True),
        lax.psum_scatter(grad_down, "dp", scatter_dimension=1, tiled=True),
        lax.psum_scatter(grad_pair, "dp", scatter_dimension=1, tiled=True),
        lax.psum_scatter(grad_up_shift, "dp", scatter_dimension=0, tiled=True),
    )
    grad_gain = jnp.stack([grad_gain_one, grad_gain_two])
    grad_shift = jnp.stack(
        [grad_shift_one, grad_shift_two, jnp.sum(d_hidden, (0, 1)), jnp.sum(d_out, (0, 1))]
    )
    norm_sums = (
        lax.psum_scatter(grad_gain, ("dp", "tensor"), scatter_dimension=1, tiled=True),
        lax.psum_scatter(grad_shift, ("dp", "tensor"), scatter_dimension=1, tiled=True),
    )
    result = jnp.swapaxes(output, 0, 1).astype(jnp.bfloat16)
    grad_in = jnp.swapaxes(d_inputs, 0, 1).astype(jnp.bfloat16)
    return (
        result,
        grad_in,
        sums[0],
        sums[1],
        sums[2],
        sums[3],
        norm_sums[0],
        norm_sums[1],
        sums[4],
        sums[5],
    )


BF = jnp.bfloat16
F32 = jnp.float32
LOG2E = 1.4426950408889634
VMEM_LIMIT = 56 * 2**20
ROW_NN = (((1,), (0,)), ((), ()))
ROW_NT = (((1,), (1,)), ((), ()))
PAIR = 2


def dot(left, right, dims=ROW_NN):
    return lax.dot_general(left, right, dims, preferred_element_type=F32)


def call(body, grid, in_specs, out_specs, out_shape, args, scratch=(), name=None, prefetch=0, aliases=None):
    return pl.pallas_call(
        body,
        grid_spec=pltpu.PrefetchScalarGridSpec(
            num_scalar_prefetch=prefetch, grid=grid, in_specs=in_specs, out_specs=out_specs, scratch_shapes=list(scratch)
        ),
        out_shape=out_shape,
        input_output_aliases=aliases or {},
        compiler_params=pltpu.CompilerParams(vmem_limit_bytes=VMEM_LIMIT),
        cost_estimate=pl.CostEstimate(flops=1000, bytes_accessed=1000, transcendentals=0),
        name=name,
    )(*args)


def shaped(shape, dtype=BF):
    return jax.ShapeDtypeStruct(shape, dtype)


def three_parts(value):
    high = value.astype(BF)
    rest = value - high.astype(F32)
    middle = rest.astype(BF)
    return high, middle, (rest - middle.astype(F32)).astype(BF)


def query_blocks(seq, step):
    blocks = []
    start = 0
    while start < seq:
        used = min(step, seq - start)
        blocks.append((start, -(-used // 128) * 128, used))
        start += used
    return blocks


def pad_columns(value, width):
    extra = width - value.shape[1]
    if extra == 0:
        return value
    return jnp.concatenate([value, jnp.zeros((value.shape[0], extra), value.dtype)], 1)


def row_blocks(ref, place, start, stop):
    return jnp.concatenate([ref[owner, place, start:stop] for owner in range(ref.shape[0])], 1)


def turned_owner(owner):
    return owner % 2 * 2 + owner // 2


def owners_of(bits_ref, which, mine_ref, other_ref, pick):
    parts = []
    for owner in range(4):
        row, column = owner // 2, owner % 2
        inner, outer = (row, column) if which == 0 else (column, row)
        parts.append(jnp.where(bits_ref[which] == outer, pick(mine_ref, inner), pick(other_ref, inner)))
    return parts


def project_kernel(bits_ref, xa_ref, xb_ref, qk_ref, qk_other, v_ref, v_other, b_ref, out_ref, t_ref, x_s):
    half = xa_ref.shape[0]
    group = pl.program_id(0)

    @pl.when(group == 0)
    def _():
        x_s[0:half] = xa_ref[...]
        x_s[half:] = xb_ref[...]
        t_ref[...] = x_s[...].T

    cols = v_ref.shape[2]
    for i in range(3):
        rows = slice(i * cols, (i + 1) * cols)
        weights = []
        for p in range(PAIR):
            if i == 2:
                parts = owners_of(bits_ref, 1, v_ref, v_other, lambda ref, inner: ref[inner, p])
            else:
                parts = owners_of(bits_ref, 0, qk_ref, qk_other, lambda ref, inner: ref[inner, p, rows])
            weights.append(jnp.concatenate(parts, 1))
        value = dot(jnp.concatenate(weights, 0), x_s[...], ROW_NT) + b_ref[0, i]
        out_ref[0, i] = value.astype(BF).reshape(out_ref.shape[2:])


def project(bits, xa, xb, w_qk, w_vo, bias):
    half, width = xa.shape
    _, places, rows, part = w_qk[0].shape
    cols = rows // 2
    groups = places // PAIR
    heads = PAIR * cols // HEAD_DIM
    whole = pl.BlockSpec((half, width), lambda g, bits: (0, 0))
    return call(
        project_kernel,
        (groups,),
        [whole, whole]
        + [pl.BlockSpec((2, PAIR, rows, part), lambda g, bits: (0, g, 0, 0))] * 2
        + [pl.BlockSpec((2, PAIR, cols, part), lambda g, bits: (0, g, 0, 0))] * 2
        + [pl.BlockSpec((1, 3, PAIR * cols, 1), lambda g, bits: (g, 0, 0, 0))],
        [
            pl.BlockSpec((1, 3, heads, HEAD_DIM, 2 * half), lambda g, bits: (g, 0, 0, 0, 0)),
            pl.BlockSpec((width, 2 * half), lambda g, bits: (0, 0)),
        ],
        [shaped((groups, 3, heads, HEAD_DIM, 2 * half)), shaped((width, 2 * half))],
        (bits, xa, xb, *w_qk, *w_vo, bias),
        [pltpu.VMEM((2 * half, width), BF)],
        name="project",
        prefetch=1,
    )


def attend_kernel(seq, padded, step, q_ref, k_ref, v_ref, *refs):
    o_ref, row_ref, wide_ref, lse_ref, key_s, query_s, value_s, hold_s = refs[-8:]
    key = k_ref[0, 0, 0]
    key_s[...] = jnp.concatenate([key, key, key, jnp.zeros((HEAD_DIM, seq), BF)], 0).T
    parts = three_parts(pad_columns(q_ref[0, 0, 0].astype(F32) * (LOG2E * HEAD_DIM**-0.5), padded))
    query_s[...] = jnp.concatenate([*parts, jnp.zeros((HEAD_DIM, padded), BF)], 0)
    value_s[0:HEAD_DIM] = v_ref[0, 0, 0]
    value_s[HEAD_DIM : HEAD_DIM + 16] = jnp.ones((16, seq), BF)
    for start, width, used in query_blocks(seq, step):
        scores = dot(key_s[...], query_s[:, start : start + width])
        top = jnp.max(scores, 0, keepdims=True)
        prob = jnp.exp2(scores - top).astype(BF)
        mixed = dot(value_s[...], prob)
        total = mixed[HEAD_DIM : HEAD_DIM + 1]
        result = (mixed[0:HEAD_DIM] * (1.0 / total))[:, :used]
        wide_ref[0, :, start : start + used] = result
        o_ref[0, :, start : start + used] = result.astype(BF)
        lse_ref[0, :, start : start + used] = (top + jnp.log2(total))[:, :used]
    odd = pl.program_id(0) % 2
    hold_s[pl.ds(pl.multiple_of(odd * HEAD_DIM, HEAD_DIM), HEAD_DIM)] = o_ref[0]

    @pl.when(odd == 1)
    def _():
        row_ref[...] = hold_s[...].T


def attend(qkv, group, step, into=()):
    groups, _, heads, _, seq = qkv.shape
    padded = -(-seq // 128) * 128
    part = lambda i: pl.BlockSpec((1, 1, 1, HEAD_DIM, seq), lambda h: (group, i, h, 0, 0))
    spec = lambda rows: pl.BlockSpec((1, rows, seq), lambda h: (group * heads + h, 0, 0))
    total = groups * heads
    return call(
        functools.partial(attend_kernel, seq, padded, step),
        (heads,),
        [part(0), part(1), part(2)] + [pl.BlockSpec(memory_space=pl.ANY)] * len(into),
        [
            spec(HEAD_DIM),
            pl.BlockSpec((seq, 2 * HEAD_DIM), lambda h: (0, group * heads // 2 + h // 2)),
            spec(HEAD_DIM),
            spec(1),
        ],
        [
            shaped((total, HEAD_DIM, seq)),
            shaped((seq, total * HEAD_DIM)),
            shaped((total, HEAD_DIM, seq), F32),
            shaped((total, 1, seq), F32),
        ],
        (qkv, qkv, qkv, *into),
        [
            pltpu.VMEM((seq, 4 * HEAD_DIM), BF),
            pltpu.VMEM((4 * HEAD_DIM, padded), BF),
            pltpu.VMEM((HEAD_DIM + 16, seq), BF),
            pltpu.VMEM((2 * HEAD_DIM, seq), BF),
        ],
        name="attend",
        aliases={3 + i: i for i in range(len(into))},
    )


def attend_back_kernel(
    seq, padded, step, q_ref, k_ref, v_ref, d_ref, lse_ref, delta_ref, out_ref, sum_ref, key_s, query_s, value_s, dmix_s, hold_s
):
    key = k_ref[0, 0, 0]
    ones = jnp.ones((16, seq), BF)
    key_s[...] = jnp.concatenate([key, key, key, ones, jnp.zeros((48, seq), BF)], 0).T
    value_s[...] = jnp.concatenate([v_ref[0, 0, 0], ones, jnp.zeros((48, seq), BF)], 0).T
    query = pad_columns(q_ref[0, 0, 0], padded).astype(F32)
    blank = jnp.zeros((13, padded), BF)
    tail = jnp.zeros((48, padded), BF)
    lse = jnp.concatenate([*three_parts(pad_columns(-lse_ref[0], padded)), blank], 0)
    delta = jnp.concatenate([*three_parts(pad_columns(-delta_ref[0], padded)), blank], 0)
    query_s[...] = jnp.concatenate([*three_parts(query * (LOG2E * HEAD_DIM**-0.5)), lse, tail], 0)
    dmix_s[...] = jnp.concatenate([pad_columns(d_ref[0], padded), delta, tail], 0)
    scaled = (query * HEAD_DIM**-0.5).astype(BF)
    odd = pl.program_id(0) % 2
    here = pl.ds(pl.multiple_of(odd * HEAD_DIM, HEAD_DIM), HEAD_DIM)
    d_keys = jnp.zeros((HEAD_DIM, seq), F32)
    d_values = jnp.zeros((HEAD_DIM, seq), F32)
    for start, width, used in query_blocks(seq, step):
        prob = jnp.exp2(dot(key_s[...], query_s[:, start : start + width]))
        d_scores = (prob * dot(value_s[...], dmix_s[:, start : start + width])).astype(BF)
        d_values = d_values + dot(dmix_s[0:HEAD_DIM, start : start + width], prob.astype(BF), ROW_NT)
        d_keys = d_keys + dot(scaled[:, start : start + width], d_scores, ROW_NT)
        d_query = dot(key, d_scores) * HEAD_DIM**-0.5
        hold_s[0, here, start : start + used] = d_query[:, :used].astype(BF)
    hold_s[1, here] = d_keys.astype(BF)
    hold_s[2, here] = d_values.astype(BF)

    @pl.when(odd == 1)
    def _():
        for i in range(3):
            turned = hold_s[i].T
            out_ref[i] = turned
            sum_ref[i] = jnp.sum(turned.astype(F32), 0, keepdims=True)


def attend_backward(qkv, d_mixed, lse, delta, group, first, count, step):
    _, _, inner, _, seq = qkv.shape
    padded = -(-seq // 128) * 128
    part = lambda i: pl.BlockSpec((1, 1, 1, HEAD_DIM, seq), lambda h: (group, i, first + h, 0, 0))
    spec = lambda rows: pl.BlockSpec((1, rows, seq), lambda h: (group * inner + first + h, 0, 0))
    return call(
        functools.partial(attend_back_kernel, seq, padded, step),
        (count,),
        [part(0), part(1), part(2), spec(HEAD_DIM), spec(1), spec(1)],
        [
            pl.BlockSpec((3, seq, 2 * HEAD_DIM), lambda h: (0, 0, h // 2)),
            pl.BlockSpec((3, 1, 2 * HEAD_DIM), lambda h: (0, 0, h // 2)),
        ],
        [shaped((3, seq, count * HEAD_DIM)), shaped((3, 1, count * HEAD_DIM), F32)],
        (qkv, qkv, qkv, d_mixed, lse, delta),
        [
            pltpu.VMEM((seq, 4 * HEAD_DIM), BF),
            pltpu.VMEM((4 * HEAD_DIM, padded), BF),
            pltpu.VMEM((seq, 2 * HEAD_DIM), BF),
            pltpu.VMEM((2 * HEAD_DIM, padded), BF),
            pltpu.VMEM((3, 2 * HEAD_DIM, seq), BF),
        ],
        name="attend_backward",
    )


def mix_kernel(o_ref, w_ref, out_ref):
    places, cols = w_ref.shape[1:3]
    weights = [row_blocks(w_ref, j, 0, cols) for j in range(places)]
    out_ref[...] = dot(o_ref[...], jnp.concatenate(weights, 0)).astype(out_ref.dtype)


def mix(rows, weights, which, dtype):
    seq, wide = rows.shape
    owners, places, _, part = weights.shape
    cols = wide // places
    half = seq // 2
    return call(
        mix_kernel,
        (2,),
        [
            pl.BlockSpec((half, wide), lambda n: (which, 0)),
            pl.BlockSpec((owners // 2, places, cols, part), lambda n: (n, 0, 1, 0)),
        ],
        pl.BlockSpec((half, owners * part // 2), lambda n: (0, n)),
        shaped((half, owners * part), dtype),
        (rows, weights),
        name="mix",
    )


def mix_back_kernel(bits_ref, da_ref, db_ref, w_ref, o_ref, wide_ref, d_ref, delta_ref, *refs):
    *grad_refs, d_s = refs
    half, width = da_ref.shape
    cols = w_ref.shape[2]
    heads = o_ref.shape[0]

    @pl.when(pl.program_id(0) == 0)
    def _():
        d_s[0:half] = da_ref[...]
        d_s[half:] = db_ref[...]

    weights = jnp.concatenate([row_blocks(w_ref, p, 0, cols) for p in range(PAIR)], 0)
    d_heads = dot(weights, d_s[...], ROW_NT).astype(BF).reshape(o_ref.shape)
    d_ref[...] = d_heads
    delta_ref[...] = jnp.sum(d_heads.astype(F32) * wide_ref[...], 1, keepdims=True)
    grad = dot(o_ref[...].reshape(heads * HEAD_DIM, 2 * half), d_s[...]).astype(BF).T
    for p in range(PAIR):
        part = grad[:, p * cols : (p + 1) * cols]
        put_halves(bits_ref, part, p, grad_refs[2 * p], grad_refs[2 * p + 1], (slice(None), 0))


def mix_back(bits, da, db, weights, mixed, wide):
    half, width = da.shape
    owners, places, _, part = weights.shape
    heads, _, seq = mixed.shape
    groups = places // PAIR
    cols = heads * HEAD_DIM // places
    whole = pl.BlockSpec((half, width), lambda g, bits: (0, 0))
    spec = lambda rows: pl.BlockSpec((heads // groups, rows, seq), lambda g, bits: (g, 0, 0))
    grad = pl.BlockSpec((2, 1, width // 4, cols), lambda g, bits: (0, g, 0, 0))
    d_heads, delta, keep_a, send_a, keep_b, send_b = call(
        mix_back_kernel,
        (groups,),
        [whole, whole, pl.BlockSpec((owners, PAIR, cols, part), lambda g, bits: (0, g, 1, 0)), spec(HEAD_DIM), spec(HEAD_DIM)],
        [spec(HEAD_DIM), spec(1)] + [grad] * 4,
        [shaped((heads, HEAD_DIM, seq)), shaped((heads, 1, seq), F32)] + [shaped((2, groups, width // 4, cols))] * 4,
        (bits, da, db, weights, mixed, wide),
        [pltpu.VMEM((seq, width), BF)],
        name="mix_back",
        prefetch=1,
    )
    return d_heads, delta, (keep_a, keep_b), (send_a, send_b)


def project_grad_kernel(bits_ref, t_ref, *refs):
    *d_refs, _, _, _, _ = refs
    refs = refs[-4:]
    cols = refs[0].shape[3]
    grad = dot(t_ref[...], jnp.concatenate([ref[0] for ref in d_refs], 1)).astype(BF)
    for p in range(PAIR):
        put_halves(bits_ref, grad[:, p * cols : (p + 1) * cols], p, refs[2 * p], refs[2 * p + 1], (slice(None), 0))


def project_grads(bits, turned, *pieces):
    width, seq = turned.shape
    cols = sum(piece.shape[2] for piece in pieces) // PAIR
    specs = [pl.BlockSpec((1, seq, piece.shape[2]), lambda i, bits: (i, 0, 0)) for piece in pieces]
    grad = pl.BlockSpec((2, 1, width // 4, cols), lambda i, bits: (0, i, 0, 0))
    keep_a, send_a, keep_b, send_b = call(
        project_grad_kernel,
        (3,),
        [pl.BlockSpec((width, seq), lambda i, bits: (0, 0))] + specs,
        [grad] * 4,
        [shaped((2, 3, width // 4, cols))] * 4,
        (bits, turned, *pieces),
        name="project_grads",
        prefetch=1,
    )
    return (keep_a, keep_b), (send_a, send_b)


def project_back_kernel(a_ref, c_ref, d_ref, qk_ref, v_ref, out_ref):
    total = None
    for first, refs in ((0, (a_ref,)), (PAIR, (c_ref, d_ref))):
        places = [first + p for p in range(PAIR)]
        left = [ref[i] for i in range(3) for ref in refs]
        right = [qk_ref[0, place, i] for i in range(2) for place in places] + [v_ref[0, place] for place in places]
        part = dot(jnp.concatenate(left, 1), jnp.concatenate(right, 0))
        total = part if total is None else total + part
    out_ref[...] = total


def project_back(pieces, w_qk, w_vo, which):
    seq = pieces[0].shape[1]
    owners, places, _, cols, part = w_qk.shape
    half = seq // 2
    return call(
        project_back_kernel,
        (owners,),
        [pl.BlockSpec((3, half, piece.shape[2]), lambda n: (0, which, 0)) for piece in pieces]
        + [
            pl.BlockSpec((1, places, 2, cols, part), lambda n: (turned_owner(n), 0, 0, 0, 0)),
            pl.BlockSpec((1, places, cols, part), lambda n: (n, 0, 0, 0)),
        ],
        pl.BlockSpec((half, part), lambda n: (0, n)),
        shaped((half, owners * part), F32),
        (*pieces, w_qk, w_vo),
        name="project_back",
    )


def gelu_pair(value):
    cdf = 0.5 * (1.0 + lax.erf(value * 0.7071067811865476))
    return value * cdf, cdf + value * (jnp.exp(-0.5 * value * value) * 0.3989422804014327)


def all_blocks(ref):
    return jnp.concatenate([ref[0, t] for t in range(ref.shape[1])], 1)


def relative_block(block, place, blocks):
    return lax.rem(block + blocks - place, blocks)


def either(first_ref, last_ref, index, pick):
    half = first_ref.shape[1]
    one = pick(first_ref, jnp.minimum(index, half - 1))
    return jnp.where(index < half, one, pick(last_ref, jnp.maximum(index - half, 0)))


def ffn_kernel(place_ref, x_ref, one_ref, two_ref, last_ref, b_ref, out_ref, g_ref, slope_ref, hold_s):
    blocks = hold_s.shape[0]
    step = pl.program_id(0)

    @pl.when(step < blocks)
    def _():
        ones = jnp.concatenate([one_ref[turned_owner(owner), 0] for owner in range(one_ref.shape[0])], 0)
        twos = two_ref[...].reshape(ones.shape)
        weights = jnp.where(relative_block(step, place_ref[0], blocks) < blocks // 2, ones, twos)
        pre = dot(x_ref[...], weights) + b_ref[0]
        active, slope = gelu_pair(pre)
        active = active.astype(BF)
        hold_s[step] = active
        g_ref[...] = active
        slope_ref[...] = slope.astype(BF)

    @pl.when(step >= blocks)
    def _():
        left = jnp.concatenate([hold_s[t] for t in range(blocks)], 1)
        out_ref[...] = dot(left, all_blocks(last_ref), ROW_NT).astype(out_ref.dtype)


def ffn_specs(rows, down):
    owners, blocks, part, units = down.shape
    early = lambda s: jnp.minimum(s, blocks - 1)
    late = lambda s: jnp.maximum(s - blocks, 0)
    return (
        blocks,
        early,
        late,
        pl.BlockSpec((rows, owners * part), lambda s, place: (0, 0)),
        pl.BlockSpec((rows, units), lambda s, place: (0, early(s))),
        pl.BlockSpec((1, 1, units), lambda s, place: (early(s), 0, 0)),
        pl.BlockSpec((rows, part), lambda s, place: (0, late(s))),
    )


def ffn_forward(place, x, up, down, bias, dtype):
    rows, width = x.shape
    owners, blocks, part, units = down.shape
    blocks, early, late, whole, column, thin, out = ffn_specs(rows, down)
    index = lambda s, place: relative_block(early(s), place[0], blocks)
    return call(
        ffn_kernel,
        (blocks + owners,),
        [
            whole,
            pl.BlockSpec((owners, 1, part, units), lambda s, place: (0, jnp.minimum(index(s, place), PAIR - 1), 0, 0)),
            pl.BlockSpec((owners, 1, part, units), lambda s, place: (0, jnp.maximum(index(s, place) - PAIR, 0), 0, 0)),
            pl.BlockSpec((1, blocks, part, units), lambda s, place: (late(s), 0, 0, 0)),
            thin,
        ],
        [out, column, column],
        [shaped((rows, width), dtype), shaped((rows, blocks * units)), shaped((rows, blocks * units))],
        (place, x, *up, down, bias),
        [pltpu.VMEM((blocks, rows, units), BF)],
        name="ffn",
        prefetch=1,
    )


def ffn_back_kernel(place_ref, d_ref, first_ref, one_ref, two_ref, slope_ref, out_ref, dpre_ref, sum_ref, hold_s):
    blocks = hold_s.shape[0]
    step = pl.program_id(0)

    @pl.when(step < blocks)
    def _():
        d_pre = (dot(d_ref[...], first_ref[...].reshape(d_ref.shape[1], -1)) * slope_ref[...].astype(F32)).astype(BF)
        hold_s[step] = d_pre
        dpre_ref[...] = d_pre
        sum_ref[0] = jnp.sum(d_pre.astype(F32), 0, keepdims=True)

    @pl.when(step >= blocks)
    def _():
        left = jnp.concatenate([hold_s[t] for t in range(blocks)], 1)
        order = [relative_block(t, place_ref[0], blocks) for t in range(blocks)]
        weights = [either(one_ref, two_ref, index, lambda ref, i: ref[0, i]) for index in order]
        out_ref[...] = dot(left, jnp.concatenate(weights, 1), ROW_NT).astype(out_ref.dtype)


def ffn_backward(place, d_out, up, down, slope, dtype):
    rows, width = d_out.shape
    owners, blocks, part, units = down.shape
    blocks, early, late, whole, column, thin, out = ffn_specs(rows, down)
    return call(
        ffn_back_kernel,
        (blocks + owners,),
        [
            whole,
            pl.BlockSpec((owners, 1, part, units), lambda s, place: (0, early(s), 0, 0)),
            pl.BlockSpec((1, PAIR, part, units), lambda s, place: (turned_owner(late(s)), 0, 0, 0)),
            pl.BlockSpec((1, PAIR, part, units), lambda s, place: (late(s), 0, 0, 0)),
            column,
        ],
        [out, column, thin],
        [shaped((rows, width), dtype), shaped((rows, blocks * units)), shaped((blocks, 1, units), F32)],
        (place, d_out, down, *up, slope),
        [pltpu.VMEM((blocks, rows, units), BF)],
        name="ffn_backward",
        prefetch=1,
    )


def put_halves(bits_ref, grad, which, keep_ref, send_ref, at):
    grad = grad.reshape((2, 2, grad.shape[0] // 4) + grad.shape[1:])
    pair = (grad[:, 0], grad[:, 1]) if which == 0 else (grad[0], grad[1])
    low = bits_ref[which] == 0
    keep_ref[at] = jnp.where(low, pair[0], pair[1])
    send_ref[at] = jnp.where(low, pair[1], pair[0])


def ffn_grad_kernel(bits_ref, xa_ref, xb_ref, ca_ref, cb_ref, keep_a, send_a, keep_b, send_b, x_s):
    step = pl.program_id(0)

    @pl.when(step == 0)
    def _():
        x_s[...] = jnp.concatenate([xa_ref[...], xb_ref[...]], 0).T

    column = jnp.concatenate([ca_ref[...], cb_ref[...]], 0)
    grad = dot(x_s[...], column).astype(BF)

    @pl.when(step < PAIR)
    def _():
        put_halves(bits_ref, grad, 0, keep_a, send_a, (slice(None), 0))

    @pl.when(step >= PAIR)
    def _():
        put_halves(bits_ref, grad, 1, keep_b, send_b, (slice(None), 0))


def ffn_grad(bits, xa, xb, ca, cb, blocks):
    rows, width = xa.shape
    units = ca.shape[1] // blocks
    whole = pl.BlockSpec((rows, width), lambda t, bits: (0, 0))
    column = pl.BlockSpec((rows, units), lambda t, bits: (0, t))
    first = pl.BlockSpec((2, 1, width // 4, units), lambda t, bits: (0, jnp.minimum(t, PAIR - 1), 0, 0))
    last = pl.BlockSpec((2, 1, width // 4, units), lambda t, bits: (0, jnp.maximum(t - PAIR, 0), 0, 0))
    keep_a, send_a, keep_b, send_b = call(
        ffn_grad_kernel,
        (blocks,),
        [whole, whole, column, column],
        [first, first, last, last],
        [shaped((2, PAIR, width // 4, units))] * 4,
        (bits, xa, xb, ca, cb),
        [pltpu.VMEM((width, 2 * rows), BF)],
        name="ffn_grad",
        prefetch=1,
    )
    return (keep_a, keep_b), (send_a, send_b)


def add_kernel(bits_ref, *refs):
    count = len(refs) // 3
    for i in range(count):
        refs[2 * count + i][...] = (refs[2 * i][0].astype(F32) + refs[2 * i + 1][0].astype(F32)).astype(BF)


def add_middle(bits, keeps, parts):
    _, blocks, rows, units = keeps[0].shape
    args, in_specs = [], []
    for i, pair in enumerate(zip(keeps, parts)):
        args += pair
        in_specs += [pl.BlockSpec((1, 1, rows, units), lambda s, bits, i=i: (1 - bits[1 - i % 2], s, 0, 0))] * 2
    return call(
        add_kernel,
        (blocks,),
        in_specs,
        [pl.BlockSpec((1, rows, units), lambda s, bits: (s, 0, 0))] * len(keeps),
        [shaped((blocks, rows, units))] * len(keeps),
        (bits, *args),
        name="add_middle",
        prefetch=1,
    )


def add_end_kernel(bits_ref, *refs):
    for i in range(len(refs) // 3):
        keep, part, end = refs[3 * i : 3 * i + 3]
        total = keep[0, 0].astype(F32) + part[0, 0].astype(F32) + end[0].astype(F32)
        refs[-1][i % 2, 0, i // 2] = total.astype(BF)


def add_end(bits, keeps, parts, ends):
    _, blocks, rows, units = keeps[0].shape
    args, in_specs = [], []
    for i, triple in enumerate(zip(keeps, parts, ends)):
        args += triple
        in_specs += [pl.BlockSpec((1, 1, rows, units), lambda s, bits, i=i: (bits[1 - i % 2], s, 0, 0))] * 2
        in_specs.append(pl.BlockSpec((1, rows, units), lambda s, bits: (s, 0, 0)))
    count = len(keeps) // 2
    return call(
        add_end_kernel,
        (blocks,),
        in_specs,
        pl.BlockSpec((2, 1, count, rows, units), lambda s, bits: (0, s, 0, 0, 0)),
        shaped((2, blocks, count, rows, units)),
        (bits, *args),
        name="add_end",
        prefetch=1,
    )


def norm_back_block(da_ref, db_ref, x_ref, rest_ref, gain_ref, sum_ref):
    d_value = da_ref[...] + db_ref[...].astype(F32)
    value = x_ref[...].astype(F32)
    centred = value - jnp.mean(value, -1, keepdims=True)
    scale = lax.rsqrt(jnp.mean(centred * centred, -1, keepdims=True) + EPS)
    unit = centred * scale
    d_unit = d_value * gain_ref[...]
    inner = jnp.mean(d_unit * unit, -1, keepdims=True)
    rest = rest_ref[...]
    result = rest + scale * (d_unit - jnp.mean(d_unit, -1, keepdims=True) - unit * inner)
    parts = [d_value * unit, d_value, result, rest]
    sums = jnp.concatenate([jnp.sum(part, 0, keepdims=True) for part in parts] + [jnp.zeros((4, value.shape[1]), F32)], 0)

    @pl.when(pl.program_id(0) == 0)
    def _():
        sum_ref[...] = sums

    @pl.when(pl.program_id(0) > 0)
    def _():
        sum_ref[...] += sums

    return result


def norm_back_kernel(da_ref, db_ref, x_ref, rest_ref, gain_ref, out_ref, low_ref, sum_ref):
    result = norm_back_block(da_ref, db_ref, x_ref, rest_ref, gain_ref, sum_ref)
    out_ref[...] = result
    low_ref[...] = result.astype(BF)


def norm_back_halves_kernel(da_ref, db_ref, x_ref, rest_ref, gain_ref, near_ref, far_ref, sum_ref):
    result = norm_back_block(da_ref, db_ref, x_ref, rest_ref, gain_ref, sum_ref).astype(BF)

    @pl.when(pl.program_id(0) == 0)
    def _():
        near_ref[...] = result

    @pl.when(pl.program_id(0) == 1)
    def _():
        far_ref[...] = result


def norm_backward(da, db, x, rest, gain, halves):
    rows, width = da.shape
    steps = 2 if halves else 1
    row = pl.BlockSpec((rows // steps, width), lambda i: (i, 0))
    whole = lambda count: pl.BlockSpec((count, width), lambda i: (0, 0))
    return call(
        norm_back_halves_kernel if halves else norm_back_kernel,
        (steps,),
        [row] * 4 + [whole(1)],
        [whole(rows // 2)] * 2 + [whole(8)] if halves else [row, row, whole(8)],
        ([shaped((rows // 2, width))] * 2 if halves else [shaped((rows, width), F32), shaped((rows, width))])
        + [shaped((8, width), F32)],
        (da, db, x, rest, gain[None]),
        name="norm_backward",
    )


def swap(value, axis):
    return lax.ppermute(value, axis, [(0, 1), (1, 0)])


def after(value, *others):
    return lax.optimization_barrier((value, *others))[0]


def together(*values):
    return lax.optimization_barrier(values)


def ordered(bit, mine, other, axis):
    return jnp.concatenate([jnp.where(bit == 0, mine, other), jnp.where(bit == 0, other, mine)], axis)


def chosen(value, bit, axis):
    return lax.dynamic_index_in_dim(value, bit, axis, keepdims=False)


def added(mine, other):
    return (mine.astype(F32) + other.astype(F32)).astype(BF)


def moments(value):
    mean = jnp.mean(value, -1, keepdims=True)
    centred = value - mean
    scale = lax.rsqrt(jnp.mean(centred * centred, -1, keepdims=True) + EPS)
    return centred, scale


def clip_local(clips, w_qkv, w_out, w_up, w_down, norm_gain, shifts, bias_qv, up_bias, teacher):
    y, x, c, t = (lax.axis_index(name) for name in ("y", "x", "c", "t"))
    every = ("y", "x", "c", "t")
    steps = 4
    width = clips.shape[2]
    odd = t % 2

    first_way, second_way = [], []
    for column in range(4):
        for core in range(2):
            for place in range(4):
                source = (column * 2 + core) * 4 + place
                to = (column * 2 + place // 2) * 4 + 2 * core
                first_way.append((source, to + place % 2))
                second_way.append((source, to + 1 - place % 2))
    first_way = [(a, b) for a, b in first_way if a != b]
    back = lambda way: [(b, a) for a, b in way]
    stays = t // 2 == c

    def sent(pair):
        return lax.ppermute(pair[0], every, first_way), lax.ppermute(pair[1], every, second_way)

    def to_chip(value):
        return sent((chosen(value, odd, 0), chosen(value, 1 - odd, 0)))

    def sent_back(near, far):
        return lax.ppermute(near, every, back(first_way)), lax.ppermute(far, every, back(second_way))

    def from_chip(value):
        half = value.shape[0] // 2
        return sent_back(value[:half], value[half:])

    rings = [[(i, (i + away) % steps) for i in range(steps)] for away in range(steps)]

    def ring_gather(value):
        return tuple(lax.ppermute(value, "t", rings[-j % steps]) for j in range(1, steps))

    def ring_scatter(blocks):
        return tuple(lax.ppermute(blocks[j], "t", rings[j]) for j in range(1, steps))

    def placed(value, axis):
        return lax.dynamic_slice_in_dim(jnp.concatenate([value, value], axis), steps - t, steps, axis)

    def on_chip(value, near, far):
        return jnp.concatenate([jnp.where(stays, chosen(value, odd, 0), near), far])

    def as_clips(mine, near, far):
        near = jnp.where(stays, mine, near)
        return jnp.stack([jnp.where(odd == 0, near, far), jnp.where(odd == 0, far, near)])

    def scatter_start(sends):
        return swap(sends[0], "x"), swap(sends[1], "y")

    def sums_of(keeps, parts, row, column):
        pick = lambda values, bit: jnp.concatenate([chosen(value, bit, 0) for value in values])
        first = pick(keeps[0], row).astype(F32) + chosen(parts[0], row, 0).astype(F32)
        return first, pick(keeps[1], column).astype(F32) + chosen(parts[1], column, 0).astype(F32)

    def scatter_middle(keeps, parts):
        first, second = sums_of(keeps, parts, 1 - y, 1 - x)
        return swap(first.astype(BF), "y"), swap(second.astype(BF), "x")

    def scatter_end(keeps, parts, ends):
        first, second = sums_of(keeps, parts, y, x)
        return (first + ends[0].astype(F32)).astype(BF), (second + ends[1].astype(F32)).astype(BF)

    dims = w_qkv.shape[1]
    cols = w_out.shape[0] // 2
    lane = bias_qv.shape[1]
    units = w_up.shape[1] // 2
    attn = jnp.concatenate([jnp.swapaxes(w_qkv, 1, 2), w_out[None]]).reshape(4, 2, cols, dims)
    mine, other = chosen(attn, c, 1).reshape(4 * cols, dims), chosen(attn, 1 - c, 1).reshape(4 * cols, dims)
    attn_piece = ordered(c, mine, swap(other, "c"), 1)
    ff = jnp.stack([w_up, w_down.T]).reshape(2, dims, 2, units)
    ff_piece = ordered(c, chosen(ff, c, 2), swap(chosen(ff, 1 - c, 2), "c"), 1)

    pad = lambda value: jnp.pad(value, (0, dims - value.shape[0]))[None]
    tails = jnp.concatenate([pad(bias_qv[0]), pad(bias_qv[1]), pad(up_bias), jnp.zeros((7, dims), BF)])
    vectors = jnp.concatenate([norm_gain, shifts, tails])
    for bit, name in ((c, "c"), (x, "x"), (y, "y")):
        vectors = ordered(bit, vectors, swap(vectors, name), 1)
    gains, shift_all = vectors[0:2].astype(F32), vectors[2:6].astype(F32)
    tails = vectors[6:16]
    tails = jnp.stack([part[:3] for part in (tails, *ring_gather(tails))]).astype(F32)
    tails = lax.dynamic_slice_in_dim(tails, 4 * dims * c, 4 * dims, 2)
    pair = tails[:, :2].reshape(steps, 2, 4, dims)[..., :lane]
    bias_pair = jnp.swapaxes(pair, 0, 1).reshape(2, 2, 2 * cols)
    bias_in = jnp.stack([bias_pair[0], jnp.zeros_like(bias_pair[0]), bias_pair[1]], 1)[..., None]
    up_shift = placed(tails[:, 2:3], 0)

    whole = ("y", "x", "t")
    attn_rows = together(*ring_gather(attn_piece))
    near, far = to_chip(after(clips, attn_rows))
    attn_rows = (attn_piece, *attn_rows)
    qk_rows = jnp.stack([part[: 2 * cols] for part in attn_rows])
    vo_rows = jnp.stack([part[2 * cols :] for part in attn_rows])
    targets = chosen(teacher, odd, 0), chosen(teacher, 1 - odd, 0)
    swapped, near, targets, bias_in, up_shift = together(
        (swap(qk_rows, "y"), swap(vo_rows, "x")), near, targets, bias_in, up_shift
    )
    w_qk, w_vo = ordered(y, qk_rows[None], swapped[0][None], 0), ordered(x, vo_rows[None], swapped[1][None], 0)
    swapped, far = together((swap(w_qk, "x"), swap(w_vo, "y")), far)
    bits = jnp.stack([x, y])
    parts_qk, parts_vo = (w_qk, swapped[0]), (w_vo, swapped[1])
    up_piece, down_piece = ff_piece
    up_piece, down_piece, far = together(up_piece, down_piece, far)
    up_rows = ring_gather(up_piece)
    down_all = lax.all_gather(down_piece, whole, axis=0, tiled=False).reshape(4, steps, 2 * dims, units)
    place = t.reshape(1)

    inputs = on_chip(clips, near, far).astype(F32)
    centred_one, scale_one = moments(inputs)
    first = (centred_one * scale_one * gains[0] + shift_all[0]).astype(BF)
    first_other = swap(first, "c")
    half = first.shape[0] // 2
    qkv, turned = project(bits, first, first_other, parts_qk, parts_vo, bias_in)
    parts_qk, parts_vo, qkv = together(parts_qk, parts_vo, qkv)
    w_qk = ordered(x, parts_qk[0][None], parts_qk[1][None], 0).reshape(4, steps, 2, cols, 2 * dims)
    w_vo = ordered(y, parts_vo[0][None], parts_vo[1][None], 0).reshape(4, steps, 2 * cols, 2 * dims)
    mixed, rows, wide, lse = attend(qkv, 0, 1664)
    up_rows, rows = together(up_rows, rows)
    up_a, up_b = jnp.stack([up_piece, up_rows[0]]), jnp.stack(up_rows[1:])
    swapped = swap(up_a, "y"), swap(up_b, "x")
    mixed, rows, wide, lse = attend(qkv, 1, 1664, (mixed, rows, wide, lse))
    swapped, rows = together(swapped, rows)
    up_a, up_b = ordered(y, up_a[None], swapped[0][None], 0), ordered(x, up_b[None], swapped[1][None], 0)
    swapped = swap(up_a, "x"), swap(up_b, "y")
    attn_other = mix(rows, w_vo, 1, BF)
    attn_mine = mix(after(rows, attn_other), w_vo, 0, F32)
    hidden = inputs + (attn_mine + swap(attn_other, "c").astype(F32)) + shift_all[2]

    centred_two, scale_two = moments(hidden)
    second = (centred_two * scale_two * gains[1] + shift_all[1]).astype(BF)
    second_other = swap(second, "c")
    swapped, second, w_qk = together(swapped, second, w_qk)
    up_a = ordered(x, up_a[None], swapped[0][None], 0).reshape(4, PAIR, 2 * dims, units)
    up_b = ordered(y, up_b[None], swapped[1][None], 0).reshape(4, PAIR, 2 * dims, units)
    up_all = up_a, up_b
    targets, second, down_all = together(targets, second, down_all)
    near, far = sent(targets)
    out_other, act_other, slope_other = ffn_forward(place, second_other, up_all, down_all, up_shift, BF)
    out_other, near = together(out_other, near)
    out_swapped = swap(out_other, "c")
    out_mine, act_mine, slope_mine = ffn_forward(place, after(second, near), up_all, down_all, up_shift, F32)
    out_mine, far, out_swapped = together(out_mine, far, out_swapped)
    output = hidden + (out_mine + out_swapped.astype(F32)) + shift_all[3]
    d_out = output - on_chip(teacher, near, far).astype(F32)
    d_ffn = d_out.astype(BF)
    d_ffn_other = swap(d_ffn, "c")
    d_second, d_pre, sum_mine = ffn_backward(place, d_ffn, up_all, down_all, slope_mine, F32)
    d_ffn_other, d_pre = together(d_ffn_other, d_pre)
    d_second_other, d_pre_other, sum_other = ffn_backward(place, d_ffn_other, up_all, down_all, slope_other, BF)
    d_second_swapped = swap(d_second_other, "c")
    up_sum = (sum_mine + sum_other).reshape(steps, units)

    grad_down, sends = ffn_grad(bits, after(d_ffn, d_pre_other), d_ffn_other, act_mine, act_other, steps)
    down = scatter_start(sends)
    result, grad_down = together(output.astype(BF), grad_down)
    out_near, out_far = from_chip(result)
    d_second_swapped, grad_down = together(d_second_swapped, grad_down)
    d_hidden, d_attn, sums_two = norm_backward(d_second, d_second_swapped, hidden, d_out, gains[1], False)
    d_attn_other = swap(d_attn, "c")
    grad_up, sends = ffn_grad(bits, after(second, d_attn), second_other, d_pre, d_pre_other, steps)
    up = scatter_start(sends)
    d_attn_other, grad_up = together(d_attn_other, grad_up)

    d_heads, delta, grad_o, sends_o = mix_back(bits, d_attn, d_attn_other, w_vo, mixed, wide)
    keeps = (*grad_up, *grad_down)
    back_a, sum_a = attend_backward(qkv, d_heads, lse, delta, 1, 0, 2, 256)
    up, down, out_near, back_a = together(up, down, out_near, back_a)
    ends = add_middle(bits, keeps, (*up, *down))
    ends = [swap(part, name) for part, name in zip(ends, ("y", "x", "y", "x"))]
    back_b, sum_b = attend_backward(qkv, after(d_heads, back_a), lse, delta, 1, 2, 2, 256)
    ends, out_far, back_b = together(ends, out_far, back_b)
    grad_ff = add_end(bits, keeps, (*up, *down), ends).reshape(steps * 4 * dims, units)
    ff_total = lax.psum_scatter(grad_ff, "t", scatter_dimension=0, tiled=True)
    grad_one, sends = project_grads(bits, turned, back_a, back_b)
    one = scatter_start([jnp.concatenate(pair, 1) for pair in zip(sends, sends_o)])
    grad_one = list(zip(grad_one, grad_o))
    delta, grad_ff, grad_one = together(delta, grad_ff, grad_one)
    back_c, sum_c = attend_backward(qkv, after(d_heads, back_b), lse, delta, 0, 0, 4, 256)
    one, back_c = together(one, back_c)
    one_ends = scatter_middle(grad_one, one)
    grad_two, sends = project_grads(bits, turned, back_c)
    two = scatter_start(sends)
    one_ends, grad_two = together(one_ends, grad_two)
    one = [part for part in scatter_end(grad_one, one, one_ends)]
    early = [lax.ppermute(jnp.concatenate([one[p][:3], one[p][4:]]), "t", rings[PAIR + p]) for p in range(PAIR)]
    pieces = (back_c, back_a, back_b)
    d_first_other = project_back(pieces, w_qk, after(w_vo, grad_two), 1)
    d_first_swapped = swap(d_first_other, "c")
    two, d_first_other = together(two, d_first_other)
    two_ends = scatter_middle([[keep] for keep in grad_two], two)
    d_first = project_back(pieces, w_qk, after(w_vo, d_first_other), 0)
    ff_total, d_first = together(ff_total, d_first)
    d_first_swapped, d_first = together(d_first_swapped, d_first)
    *d_inputs, sums_one = norm_backward(d_first, d_first_swapped, inputs, d_hidden, gains[0], True)
    early, sums_one = together(early, sums_one)
    grad_near, grad_far = sent_back(*d_inputs)
    small = (sum_a, sum_b, sum_c, up_sum, sums_one)
    small, d_inputs = together(small, d_inputs)
    two_ends, grad_near, out_near, out_far = together(two_ends, grad_near, out_near, out_far)
    sum_a, sum_b, sum_c, up_sum, sums_one = small
    two = scatter_end([[keep] for keep in grad_two], two, two_ends)
    late = lax.ppermute(jnp.concatenate([two[1], one[1][3:4]]), "t", rings[1])

    grad_ff = ff_total.astype(F32).reshape(2, 2, dims, units)
    grad_ff = ordered(c, chosen(grad_ff, c, 1), swap(chosen(grad_ff, 1 - c, 1), "c"), 2)
    grad_attn = jnp.concatenate([two[0], one[0][3:4]]).astype(F32)
    grad_attn = sum((part.astype(F32) for part in (*early, late)), grad_attn).reshape(4, 2, dims, cols)
    grad_attn = ordered(c, chosen(grad_attn, c, 1), swap(chosen(grad_attn, 1 - c, 1), "c"), 2)

    heads_sum = jnp.concatenate([sum_c, sum_a, sum_b], 2).reshape(3, steps, 4, lane)
    heads_sum = placed(jnp.stack([heads_sum[0], heads_sum[2]]), 1)
    heads_sum = jnp.pad(heads_sum, ((0, 0), (0, 0), (0, 0), (0, dims - lane))).reshape(2 * steps, 4 * dims)
    own = jnp.concatenate([heads_sum, up_sum])
    own = jnp.concatenate([jnp.where(c == 0, own, 0.0), jnp.where(c == 1, own, 0.0)], 1)
    normed = [sums_one[0:1], sums_two[0:1], sums_one[1:2], sums_two[1:4]]
    sums = jnp.concatenate(normed + [jnp.zeros((2, width), F32), own])
    for bit, name in ((y, "y"), (x, "x"), (c, "c")):
        half = sums.shape[1] // 2
        part = lambda which: lax.dynamic_slice_in_dim(sums, which * half, half, 1)
        sums = part(bit) + swap(part(1 - bit), name)
    sums, grad_near = together(sums, grad_near)
    sums = sum((lax.ppermute(sums, "t", rings[away]) for away in range(1, steps)), sums)
    thin = width // 32
    vector_sums = lax.dynamic_slice_in_dim(sums[:6], thin * t, thin, 1)
    place_sums = lax.dynamic_index_in_dim(sums[8:].reshape(3, steps, dims), t, 1, keepdims=False)
    return (
        as_clips(result[: result.shape[0] // 2], out_near, out_far),
        as_clips(d_inputs[0], grad_near, grad_far),
        grad_attn[:3],
        grad_attn[3].T,
        grad_ff[0],
        grad_ff[1].T,
        vector_sums[:2],
        vector_sums[2:],
        place_sums[:2, :lane],
        place_sums[2],
    )


def clip_per_chip(mesh):
    fine = Mesh(mesh.devices.reshape(2, 2, 2, 4), ("y", "x", "c", "t"))
    dp = ("y", "x", "c")
    in_specs = (
        P(dp, "t", None),
        P(None, dp, "t"),
        P("t", dp),
        P(dp, "t"),
        P("t", dp),
        P(None, dp),
        P(None, dp),
        P(None, ("t",) + dp),
        P(("t",) + dp),
        P(dp, "t", None),
    )
    out_specs = in_specs[:1] * 2 + in_specs[1:5] + (
        P(None, dp + ("t",)),
        P(None, dp + ("t",)),
        P(None, ("t",) + dp),
        P(("t",) + dp),
    )
    return jax.shard_map(clip_local, mesh=fine, in_specs=in_specs, out_specs=out_specs, check_vma=False)


def solution(mesh):
    if dict(mesh.shape) == {"dp": 8, "tensor": 4}:
        return clip_per_chip(mesh)
    in_specs = (
        P("dp", "tensor", None),
        P(None, "dp", "tensor"),
        P("tensor", "dp"),
        P("dp", "tensor"),
        P("tensor", "dp"),
        P(None, "dp"),
        P(None, "dp"),
        P(None, ("tensor", "dp")),
        P(("tensor", "dp")),
        P("dp", "tensor", None),
    )
    out_specs = (
        P("dp", "tensor", None),
        P("dp", "tensor", None),
        P(None, "dp", "tensor"),
        P("tensor", "dp"),
        P("dp", "tensor"),
        P("tensor", "dp"),
        P(None, ("dp", "tensor")),
        P(None, ("dp", "tensor")),
        P(None, ("tensor", "dp")),
        P(("tensor", "dp")),
    )
    return jax.shard_map(local, mesh=mesh, in_specs=in_specs, out_specs=out_specs, check_vma=False)
```

```python
import functools

import jax
import jax.numpy as jnp
from jax import lax
from jax.experimental import pallas as pl
from jax.experimental.pallas import tpu as pltpu
from jax.sharding import Mesh, PartitionSpec as P

HEAD_DIM = 64


EPS = 1e-05


def layer_norm(value, gain, shift):
    mean = jnp.mean(value, -1, keepdims=True)
    centred = value - mean
    spread = jnp.mean(centred * centred, -1, keepdims=True)
    return centred * lax.rsqrt(spread + EPS) * gain + shift


def exact_gelu(value):
    return jax.nn.gelu(value, approximate=False)


def attend_clip(query, keys, values, scale):
    scores = jnp.einsum("qhe,khe->hqk", query, keys, preferred_element_type=jnp.float32) * scale
    top = jnp.max(scores, -1, keepdims=True)
    expd = jnp.exp(scores - top)
    total = jnp.sum(expd, -1, keepdims=True)
    prob = (expd / total).astype(jnp.bfloat16)
    mixed = jnp.einsum("hqk,khe->qhe", prob, values, preferred_element_type=jnp.float32)
    return (mixed.astype(jnp.bfloat16), (top + jnp.log(total))[..., 0])


def attend_back(query, keys, values, d_mixed, logsum, scale):
    scores = jnp.einsum("qhe,khe->hqk", query, keys, preferred_element_type=jnp.float32) * scale
    prob = jnp.exp(scores - logsum[:, :, None])
    d_prob = jnp.einsum("qhe,khe->hqk", d_mixed, values, preferred_element_type=jnp.float32)
    delta = jnp.sum(d_prob * prob, -1, keepdims=True)
    d_scores = (prob * (d_prob - delta)).astype(jnp.bfloat16)
    d_values = jnp.einsum(
        "hqk,qhe->khe", prob.astype(jnp.bfloat16), d_mixed, preferred_element_type=jnp.float32
    )
    d_query = jnp.einsum("hqk,khe->qhe", d_scores, keys, preferred_element_type=jnp.float32) * scale
    d_keys = jnp.einsum("hqk,qhe->khe", d_scores, query, preferred_element_type=jnp.float32) * scale
    return jnp.stack([d_query, d_keys, d_values]).astype(jnp.bfloat16)


def local(clips, w_qkv, w_out, w_up, w_down, norm_gain, shifts, bias_qv, up_bias, teacher):
    wq, wo, wu, wd, gains, shift_all, bias_pair, up_shift = (
        lax.all_gather(w_qkv, "dp", axis=1, tiled=True),
        lax.all_gather(w_out, "dp", axis=1, tiled=True),
        lax.all_gather(w_up, "dp", axis=0, tiled=True),
        lax.all_gather(w_down, "dp", axis=1, tiled=True),
        lax.all_gather(norm_gain, "dp", axis=1, tiled=True),
        lax.all_gather(shifts, "dp", axis=1, tiled=True),
        lax.all_gather(bias_qv, "dp", axis=1, tiled=True),
        lax.all_gather(up_bias, "dp", axis=0, tiled=True),
    )
    gains = gains.astype(jnp.float32)
    shift_all = shift_all.astype(jnp.float32)
    bias_pair = bias_pair.astype(jnp.float32)
    up_shift = up_shift.astype(jnp.float32)
    width = wq.shape[2]
    heads_here = width // HEAD_DIM
    scale = HEAD_DIM ** (-0.5)
    inputs = jnp.swapaxes(clips, 0, 1).astype(jnp.float32)
    first = layer_norm(inputs, gains[0], shift_all[0]).astype(jnp.bfloat16)
    whole_first = lax.all_gather(first, "tensor", axis=0, tiled=True)
    seq = whole_first.shape[0]
    count = whole_first.shape[1]
    projected = jnp.einsum("scd,kde->ksce", whole_first, wq, preferred_element_type=jnp.float32)
    qkv_bias = jnp.stack([bias_pair[0], jnp.zeros_like(bias_pair[0]), bias_pair[1]])
    qkv = (projected + qkv_bias[:, None, None, :]).astype(jnp.bfloat16)

    def heads(value):
        return jnp.swapaxes(value, 0, 1).reshape(count, seq, heads_here, HEAD_DIM)

    query_h, keys_h, values_h = (heads(qkv[0]), heads(qkv[1]), heads(qkv[2]))
    attended, logsum = lax.map(
        lambda item: attend_clip(item[0], item[1], item[2], scale), (query_h, keys_h, values_h)
    )
    mixed = jnp.swapaxes(attended.reshape(count, seq, width), 0, 1)
    piece = mixed
    attn = lax.psum_scatter(
        jnp.einsum("scd,de->sce", piece, wo, preferred_element_type=jnp.float32),
        "tensor",
        scatter_dimension=0,
        tiled=True,
    )
    hidden = inputs + attn + shift_all[2]
    second = layer_norm(hidden, gains[1], shift_all[1]).astype(jnp.bfloat16)
    whole_second = lax.all_gather(second, "tensor", axis=0, tiled=True)
    pre = jnp.einsum("scd,df->scf", whole_second, wu, preferred_element_type=jnp.float32) + up_shift
    active = exact_gelu(pre).astype(jnp.bfloat16)
    piece = active
    ffn = lax.psum_scatter(
        jnp.einsum("scf,fe->sce", piece, wd, preferred_element_type=jnp.float32),
        "tensor",
        scatter_dimension=0,
        tiled=True,
    )
    output = hidden + ffn + shift_all[3]
    d_out = output - jnp.swapaxes(teacher, 0, 1).astype(jnp.float32)
    whole_d_ffn = lax.all_gather(d_out.astype(jnp.bfloat16), "tensor", axis=0, tiled=True)
    d_active = jnp.einsum("sce,fe->scf", whole_d_ffn, wd, preferred_element_type=jnp.float32)
    grad_down = jnp.einsum("scf,sce->fe", active, whole_d_ffn, preferred_element_type=jnp.float32)
    gelu_value, gelu_back = jax.vjp(exact_gelu, pre)
    d_pre = gelu_back(d_active)[0].astype(jnp.bfloat16)
    grad_up_shift = jnp.sum(d_pre.astype(jnp.float32), (0, 1))
    grad_up = jnp.einsum("scd,scf->df", whole_second, d_pre, preferred_element_type=jnp.float32)
    piece = d_pre
    d_second = lax.psum_scatter(
        jnp.einsum("scf,df->scd", piece, wu, preferred_element_type=jnp.float32),
        "tensor",
        scatter_dimension=0,
        tiled=True,
    )
    norm_value, second_back = jax.vjp(layer_norm, hidden, gains[1], shift_all[1])
    d_hidden_norm, grad_gain_two, grad_shift_two = second_back(d_second)
    d_hidden = d_out + d_hidden_norm
    whole_d_attn = lax.all_gather(d_hidden.astype(jnp.bfloat16), "tensor", axis=0, tiled=True)
    d_mixed = jnp.einsum(
        "sce,de->scd", whole_d_attn, wo, preferred_element_type=jnp.float32
    ).astype(jnp.bfloat16)
    grad_out = jnp.einsum("scd,sce->de", mixed, whole_d_attn, preferred_element_type=jnp.float32)
    d_heads = jnp.swapaxes(d_mixed, 0, 1).reshape(count, seq, heads_here, HEAD_DIM)
    d_stacked = lax.map(
        lambda item: attend_back(item[0], item[1], item[2], item[3], item[4], scale),
        (query_h, keys_h, values_h, d_heads, logsum),
    )
    d_qkv = jnp.transpose(d_stacked.reshape(count, 3, seq, width), (1, 2, 0, 3))
    bias_sums = jnp.sum(d_qkv.astype(jnp.float32), (1, 2))
    grad_pair = jnp.stack([bias_sums[0], bias_sums[2]])
    grad_qkv = jnp.einsum("scd,ksce->kde", whole_first, d_qkv, preferred_element_type=jnp.float32)
    piece = d_qkv
    d_first = lax.psum_scatter(
        jnp.einsum("ksce,kde->scd", piece, wq, preferred_element_type=jnp.float32),
        "tensor",
        scatter_dimension=0,
        tiled=True,
    )
    first_value, first_back = jax.vjp(layer_norm, inputs, gains[0], shift_all[0])
    d_in_norm, grad_gain_one, grad_shift_one = first_back(d_first)
    d_inputs = d_hidden + d_in_norm
    sums = (
        lax.psum_scatter(grad_qkv, "dp", scatter_dimension=1, tiled=True),
        lax.psum_scatter(grad_out, "dp", scatter_dimension=1, tiled=True),
        lax.psum_scatter(grad_up, "dp", scatter_dimension=0, tiled=True),
        lax.psum_scatter(grad_down, "dp", scatter_dimension=1, tiled=True),
        lax.psum_scatter(grad_pair, "dp", scatter_dimension=1, tiled=True),
        lax.psum_scatter(grad_up_shift, "dp", scatter_dimension=0, tiled=True),
    )
    grad_gain = jnp.stack([grad_gain_one, grad_gain_two])
    grad_shift = jnp.stack(
        [grad_shift_one, grad_shift_two, jnp.sum(d_hidden, (0, 1)), jnp.sum(d_out, (0, 1))]
    )
    norm_sums = (
        lax.psum_scatter(grad_gain, ("dp", "tensor"), scatter_dimension=1, tiled=True),
        lax.psum_scatter(grad_shift, ("dp", "tensor"), scatter_dimension=1, tiled=True),
    )
    result = jnp.swapaxes(output, 0, 1).astype(jnp.bfloat16)
    grad_in = jnp.swapaxes(d_inputs, 0, 1).astype(jnp.bfloat16)
    return (
        result,
        grad_in,
        sums[0],
        sums[1],
        sums[2],
        sums[3],
        norm_sums[0],
        norm_sums[1],
        sums[4],
        sums[5],
    )


BF = jnp.bfloat16
F32 = jnp.float32
LOG2E = 1.4426950408889634
VMEM_LIMIT = 56 * 2**20
ROW_NN = (((1,), (0,)), ((), ()))
ROW_NT = (((1,), (1,)), ((), ()))
PAIR = 2


def dot(left, right, dims=ROW_NN):
    return lax.dot_general(left, right, dims, preferred_element_type=F32)


def call(body, grid, in_specs, out_specs, out_shape, args, scratch=(), name=None, prefetch=0, aliases=None):
    return pl.pallas_call(
        body,
        grid_spec=pltpu.PrefetchScalarGridSpec(
            num_scalar_prefetch=prefetch, grid=grid, in_specs=in_specs, out_specs=out_specs, scratch_shapes=list(scratch)
        ),
        out_shape=out_shape,
        input_output_aliases=aliases or {},
        compiler_params=pltpu.CompilerParams(vmem_limit_bytes=VMEM_LIMIT),
        cost_estimate=pl.CostEstimate(flops=1000, bytes_accessed=1000, transcendentals=0),
        name=name,
    )(*args)


def shaped(shape, dtype=BF):
    return jax.ShapeDtypeStruct(shape, dtype)


def three_parts(value):
    high = value.astype(BF)
    rest = value - high.astype(F32)
    middle = rest.astype(BF)
    return high, middle, (rest - middle.astype(F32)).astype(BF)


def query_blocks(seq, step):
    blocks = []
    start = 0
    while start < seq:
        used = min(step, seq - start)
        blocks.append((start, -(-used // 128) * 128, used))
        start += used
    return blocks


def pad_columns(value, width):
    extra = width - value.shape[1]
    if extra == 0:
        return value
    return jnp.concatenate([value, jnp.zeros((value.shape[0], extra), value.dtype)], 1)


def row_blocks(ref, place, start, stop):
    return jnp.concatenate([ref[owner, place, start:stop] for owner in range(ref.shape[0])], 1)


def turned_owner(owner):
    return owner % 2 * 2 + owner // 2


def owners_of(bits_ref, which, mine_ref, other_ref, pick):
    parts = []
    for owner in range(4):
        row, column = owner // 2, owner % 2
        inner, outer = (row, column) if which == 0 else (column, row)
        parts.append(jnp.where(bits_ref[which] == outer, pick(mine_ref, inner), pick(other_ref, inner)))
    return parts


def project_kernel(bits_ref, xa_ref, xb_ref, qk_ref, qk_other, v_ref, v_other, b_ref, out_ref, t_ref, x_s):
    half = xa_ref.shape[0]
    group = pl.program_id(0)

    @pl.when(group == 0)
    def _():
        x_s[0:half] = xa_ref[...]
        x_s[half:] = xb_ref[...]
        t_ref[...] = x_s[...].T

    cols = v_ref.shape[2]
    for i in range(3):
        rows = slice(i * cols, (i + 1) * cols)
        weights = []
        for p in range(PAIR):
            if i == 2:
                parts = owners_of(bits_ref, 1, v_ref, v_other, lambda ref, inner: ref[inner, p])
            else:
                parts = owners_of(bits_ref, 0, qk_ref, qk_other, lambda ref, inner: ref[inner, p, rows])
            weights.append(jnp.concatenate(parts, 1))
        value = dot(jnp.concatenate(weights, 0), x_s[...], ROW_NT) + b_ref[0, i]
        out_ref[0, i] = value.astype(BF).reshape(out_ref.shape[2:])


def project(bits, xa, xb, w_qk, w_vo, bias):
    half, width = xa.shape
    _, places, rows, part = w_qk[0].shape
    cols = rows // 2
    groups = places // PAIR
    heads = PAIR * cols // HEAD_DIM
    whole = pl.BlockSpec((half, width), lambda g, bits: (0, 0))
    return call(
        project_kernel,
        (groups,),
        [whole, whole]
        + [pl.BlockSpec((2, PAIR, rows, part), lambda g, bits: (0, g, 0, 0))] * 2
        + [pl.BlockSpec((2, PAIR, cols, part), lambda g, bits: (0, g, 0, 0))] * 2
        + [pl.BlockSpec((1, 3, PAIR * cols, 1), lambda g, bits: (g, 0, 0, 0))],
        [
            pl.BlockSpec((1, 3, heads, HEAD_DIM, 2 * half), lambda g, bits: (g, 0, 0, 0, 0)),
            pl.BlockSpec((width, 2 * half), lambda g, bits: (0, 0)),
        ],
        [shaped((groups, 3, heads, HEAD_DIM, 2 * half)), shaped((width, 2 * half))],
        (bits, xa, xb, *w_qk, *w_vo, bias),
        [pltpu.VMEM((2 * half, width), BF)],
        name="project",
        prefetch=1,
    )


def attend_kernel(seq, padded, step, q_ref, k_ref, v_ref, *refs):
    o_ref, row_ref, wide_ref, lse_ref, key_s, query_s, value_s, hold_s = refs[-8:]
    key = k_ref[0, 0, 0]
    key_s[...] = jnp.concatenate([key, key, key, jnp.zeros((HEAD_DIM, seq), BF)], 0).T
    parts = three_parts(pad_columns(q_ref[0, 0, 0].astype(F32) * (LOG2E * HEAD_DIM**-0.5), padded))
    query_s[...] = jnp.concatenate([*parts, jnp.zeros((HEAD_DIM, padded), BF)], 0)
    value_s[0:HEAD_DIM] = v_ref[0, 0, 0]
    value_s[HEAD_DIM : HEAD_DIM + 16] = jnp.ones((16, seq), BF)
    for start, width, used in query_blocks(seq, step):
        scores = dot(key_s[...], query_s[:, start : start + width])
        top = jnp.max(scores, 0, keepdims=True)
        prob = jnp.exp2(scores - top).astype(BF)
        mixed = dot(value_s[...], prob)
        total = mixed[HEAD_DIM : HEAD_DIM + 1]
        result = (mixed[0:HEAD_DIM] * (1.0 / total))[:, :used]
        wide_ref[0, :, start : start + used] = result
        o_ref[0, :, start : start + used] = result.astype(BF)
        lse_ref[0, :, start : start + used] = (top + jnp.log2(total))[:, :used]
    odd = pl.program_id(0) % 2
    hold_s[pl.ds(pl.multiple_of(odd * HEAD_DIM, HEAD_DIM), HEAD_DIM)] = o_ref[0]

    @pl.when(odd == 1)
    def _():
        row_ref[...] = hold_s[...].T


def attend(qkv, group, step, into=()):
    groups, _, heads, _, seq = qkv.shape
    padded = -(-seq // 128) * 128
    part = lambda i: pl.BlockSpec((1, 1, 1, HEAD_DIM, seq), lambda h: (group, i, h, 0, 0))
    spec = lambda rows: pl.BlockSpec((1, rows, seq), lambda h: (group * heads + h, 0, 0))
    total = groups * heads
    return call(
        functools.partial(attend_kernel, seq, padded, step),
        (heads,),
        [part(0), part(1), part(2)] + [pl.BlockSpec(memory_space=pl.ANY)] * len(into),
        [
            spec(HEAD_DIM),
            pl.BlockSpec((seq, 2 * HEAD_DIM), lambda h: (0, group * heads // 2 + h // 2)),
            spec(HEAD_DIM),
            spec(1),
        ],
        [
            shaped((total, HEAD_DIM, seq)),
            shaped((seq, total * HEAD_DIM)),
            shaped((total, HEAD_DIM, seq), F32),
            shaped((total, 1, seq), F32),
        ],
        (qkv, qkv, qkv, *into),
        [
            pltpu.VMEM((seq, 4 * HEAD_DIM), BF),
            pltpu.VMEM((4 * HEAD_DIM, padded), BF),
            pltpu.VMEM((HEAD_DIM + 16, seq), BF),
            pltpu.VMEM((2 * HEAD_DIM, seq), BF),
        ],
        name="attend",
        aliases={3 + i: i for i in range(len(into))},
    )


def attend_back_kernel(
    seq, padded, step, q_ref, k_ref, v_ref, d_ref, lse_ref, delta_ref, out_ref, sum_ref, key_s, query_s, value_s, dmix_s, hold_s
):
    key = k_ref[0, 0, 0]
    ones = jnp.ones((16, seq), BF)
    key_s[...] = jnp.concatenate([key, key, key, ones, jnp.zeros((48, seq), BF)], 0).T
    value_s[...] = jnp.concatenate([v_ref[0, 0, 0], ones, jnp.zeros((48, seq), BF)], 0).T
    query = pad_columns(q_ref[0, 0, 0], padded).astype(F32)
    blank = jnp.zeros((13, padded), BF)
    tail = jnp.zeros((48, padded), BF)
    lse = jnp.concatenate([*three_parts(pad_columns(-lse_ref[0], padded)), blank], 0)
    delta = jnp.concatenate([*three_parts(pad_columns(-delta_ref[0], padded)), blank], 0)
    query_s[...] = jnp.concatenate([*three_parts(query * (LOG2E * HEAD_DIM**-0.5)), lse, tail], 0)
    dmix_s[...] = jnp.concatenate([pad_columns(d_ref[0], padded), delta, tail], 0)
    scaled = (query * HEAD_DIM**-0.5).astype(BF)
    odd = pl.program_id(0) % 2
    here = pl.ds(pl.multiple_of(odd * HEAD_DIM, HEAD_DIM), HEAD_DIM)
    d_keys = jnp.zeros((HEAD_DIM, seq), F32)
    d_values = jnp.zeros((HEAD_DIM, seq), F32)
    for start, width, used in query_blocks(seq, step):
        prob = jnp.exp2(dot(key_s[...], query_s[:, start : start + width]))
        d_scores = (prob * dot(value_s[...], dmix_s[:, start : start + width])).astype(BF)
        d_values = d_values + dot(dmix_s[0:HEAD_DIM, start : start + width], prob.astype(BF), ROW_NT)
        d_keys = d_keys + dot(scaled[:, start : start + width], d_scores, ROW_NT)
        d_query = dot(key, d_scores) * HEAD_DIM**-0.5
        hold_s[0, here, start : start + used] = d_query[:, :used].astype(BF)
    hold_s[1, here] = d_keys.astype(BF)
    hold_s[2, here] = d_values.astype(BF)

    @pl.when(odd == 1)
    def _():
        for i in range(3):
            turned = hold_s[i].T
            out_ref[i] = turned
            sum_ref[i] = jnp.sum(turned.astype(F32), 0, keepdims=True)


def attend_backward(qkv, d_mixed, lse, delta, group, first, count, step):
    _, _, inner, _, seq = qkv.shape
    padded = -(-seq // 128) * 128
    part = lambda i: pl.BlockSpec((1, 1, 1, HEAD_DIM, seq), lambda h: (group, i, first + h, 0, 0))
    spec = lambda rows: pl.BlockSpec((1, rows, seq), lambda h: (group * inner + first + h, 0, 0))
    return call(
        functools.partial(attend_back_kernel, seq, padded, step),
        (count,),
        [part(0), part(1), part(2), spec(HEAD_DIM), spec(1), spec(1)],
        [
            pl.BlockSpec((3, seq, 2 * HEAD_DIM), lambda h: (0, 0, h // 2)),
            pl.BlockSpec((3, 1, 2 * HEAD_DIM), lambda h: (0, 0, h // 2)),
        ],
        [shaped((3, seq, count * HEAD_DIM)), shaped((3, 1, count * HEAD_DIM), F32)],
        (qkv, qkv, qkv, d_mixed, lse, delta),
        [
            pltpu.VMEM((seq, 4 * HEAD_DIM), BF),
            pltpu.VMEM((4 * HEAD_DIM, padded), BF),
            pltpu.VMEM((seq, 2 * HEAD_DIM), BF),
            pltpu.VMEM((2 * HEAD_DIM, padded), BF),
            pltpu.VMEM((3, 2 * HEAD_DIM, seq), BF),
        ],
        name="attend_backward",
    )


def mix_kernel(o_ref, w_ref, out_ref):
    places, cols = w_ref.shape[1:3]
    weights = [row_blocks(w_ref, j, 0, cols) for j in range(places)]
    out_ref[...] = dot(o_ref[...], jnp.concatenate(weights, 0)).astype(out_ref.dtype)


def mix(rows, weights, which, dtype):
    seq, wide = rows.shape
    owners, places, _, part = weights.shape
    cols = wide // places
    half = seq // 2
    return call(
        mix_kernel,
        (2,),
        [
            pl.BlockSpec((half, wide), lambda n: (which, 0)),
            pl.BlockSpec((owners // 2, places, cols, part), lambda n: (n, 0, 1, 0)),
        ],
        pl.BlockSpec((half, owners * part // 2), lambda n: (0, n)),
        shaped((half, owners * part), dtype),
        (rows, weights),
        name="mix",
    )


def mix_back_kernel(bits_ref, da_ref, db_ref, w_ref, o_ref, wide_ref, d_ref, delta_ref, *refs):
    *grad_refs, d_s = refs
    half, width = da_ref.shape
    cols = w_ref.shape[2]
    heads = o_ref.shape[0]

    @pl.when(pl.program_id(0) == 0)
    def _():
        d_s[0:half] = da_ref[...]
        d_s[half:] = db_ref[...]

    weights = jnp.concatenate([row_blocks(w_ref, p, 0, cols) for p in range(PAIR)], 0)
    d_heads = dot(weights, d_s[...], ROW_NT).astype(BF).reshape(o_ref.shape)
    d_ref[...] = d_heads
    delta_ref[...] = jnp.sum(d_heads.astype(F32) * wide_ref[...], 1, keepdims=True)
    grad = dot(o_ref[...].reshape(heads * HEAD_DIM, 2 * half), d_s[...]).astype(BF).T
    for p in range(PAIR):
        part = grad[:, p * cols : (p + 1) * cols]
        put_halves(bits_ref, part, p, grad_refs[2 * p], grad_refs[2 * p + 1], (slice(None), 0))


def mix_back(bits, da, db, weights, mixed, wide):
    half, width = da.shape
    owners, places, _, part = weights.shape
    heads, _, seq = mixed.shape
    groups = places // PAIR
    cols = heads * HEAD_DIM // places
    whole = pl.BlockSpec((half, width), lambda g, bits: (0, 0))
    spec = lambda rows: pl.BlockSpec((heads // groups, rows, seq), lambda g, bits: (g, 0, 0))
    grad = pl.BlockSpec((2, 1, width // 4, cols), lambda g, bits: (0, g, 0, 0))
    d_heads, delta, keep_a, send_a, keep_b, send_b = call(
        mix_back_kernel,
        (groups,),
        [whole, whole, pl.BlockSpec((owners, PAIR, cols, part), lambda g, bits: (0, g, 1, 0)), spec(HEAD_DIM), spec(HEAD_DIM)],
        [spec(HEAD_DIM), spec(1)] + [grad] * 4,
        [shaped((heads, HEAD_DIM, seq)), shaped((heads, 1, seq), F32)] + [shaped((2, groups, width // 4, cols))] * 4,
        (bits, da, db, weights, mixed, wide),
        [pltpu.VMEM((seq, width), BF)],
        name="mix_back",
        prefetch=1,
    )
    return d_heads, delta, (keep_a, keep_b), (send_a, send_b)


def project_grad_kernel(bits_ref, t_ref, *refs):
    *d_refs, _, _, _, _ = refs
    refs = refs[-4:]
    cols = refs[0].shape[3]
    grad = dot(t_ref[...], jnp.concatenate([ref[0] for ref in d_refs], 1)).astype(BF)
    for p in range(PAIR):
        put_halves(bits_ref, grad[:, p * cols : (p + 1) * cols], p, refs[2 * p], refs[2 * p + 1], (slice(None), 0))


def project_grads(bits, turned, *pieces):
    width, seq = turned.shape
    cols = sum(piece.shape[2] for piece in pieces) // PAIR
    specs = [pl.BlockSpec((1, seq, piece.shape[2]), lambda i, bits: (i, 0, 0)) for piece in pieces]
    grad = pl.BlockSpec((2, 1, width // 4, cols), lambda i, bits: (0, i, 0, 0))
    keep_a, send_a, keep_b, send_b = call(
        project_grad_kernel,
        (3,),
        [pl.BlockSpec((width, seq), lambda i, bits: (0, 0))] + specs,
        [grad] * 4,
        [shaped((2, 3, width // 4, cols))] * 4,
        (bits, turned, *pieces),
        name="project_grads",
        prefetch=1,
    )
    return (keep_a, keep_b), (send_a, send_b)


def project_back_kernel(a_ref, c_ref, d_ref, qk_ref, v_ref, out_ref):
    total = None
    for first, refs in ((0, (a_ref,)), (PAIR, (c_ref, d_ref))):
        places = [first + p for p in range(PAIR)]
        left = [ref[i] for i in range(3) for ref in refs]
        right = [qk_ref[0, place, i] for i in range(2) for place in places] + [v_ref[0, place] for place in places]
        part = dot(jnp.concatenate(left, 1), jnp.concatenate(right, 0))
        total = part if total is None else total + part
    out_ref[...] = total


def project_back(pieces, w_qk, w_vo, which):
    seq = pieces[0].shape[1]
    owners, places, _, cols, part = w_qk.shape
    half = seq // 2
    return call(
        project_back_kernel,
        (owners,),
        [pl.BlockSpec((3, half, piece.shape[2]), lambda n: (0, which, 0)) for piece in pieces]
        + [
            pl.BlockSpec((1, places, 2, cols, part), lambda n: (turned_owner(n), 0, 0, 0, 0)),
            pl.BlockSpec((1, places, cols, part), lambda n: (n, 0, 0, 0)),
        ],
        pl.BlockSpec((half, part), lambda n: (0, n)),
        shaped((half, owners * part), F32),
        (*pieces, w_qk, w_vo),
        name="project_back",
    )


def gelu_pair(value):
    cdf = 0.5 * (1.0 + lax.erf(value * 0.7071067811865476))
    return value * cdf, cdf + value * (jnp.exp(-0.5 * value * value) * 0.3989422804014327)


def all_blocks(ref):
    return jnp.concatenate([ref[0, t] for t in range(ref.shape[1])], 1)


def relative_block(block, place, blocks):
    return lax.rem(block + blocks - place, blocks)


def either(first_ref, last_ref, index, pick):
    half = first_ref.shape[1]
    one = pick(first_ref, jnp.minimum(index, half - 1))
    return jnp.where(index < half, one, pick(last_ref, jnp.maximum(index - half, 0)))


def ffn_kernel(place_ref, x_ref, one_ref, two_ref, last_ref, b_ref, out_ref, g_ref, slope_ref, hold_s):
    blocks = hold_s.shape[0]
    step = pl.program_id(0)

    @pl.when(step < blocks)
    def _():
        ones = jnp.concatenate([one_ref[turned_owner(owner), 0] for owner in range(one_ref.shape[0])], 0)
        twos = two_ref[...].reshape(ones.shape)
        weights = jnp.where(relative_block(step, place_ref[0], blocks) < blocks // 2, ones, twos)
        pre = dot(x_ref[...], weights) + b_ref[0]
        active, slope = gelu_pair(pre)
        active = active.astype(BF)
        hold_s[step] = active
        g_ref[...] = active
        slope_ref[...] = slope.astype(BF)

    @pl.when(step >= blocks)
    def _():
        left = jnp.concatenate([hold_s[t] for t in range(blocks)], 1)
        out_ref[...] = dot(left, all_blocks(last_ref), ROW_NT).astype(out_ref.dtype)


def ffn_specs(rows, down):
    owners, blocks, part, units = down.shape
    early = lambda s: jnp.minimum(s, blocks - 1)
    late = lambda s: jnp.maximum(s - blocks, 0)
    return (
        blocks,
        early,
        late,
        pl.BlockSpec((rows, owners * part), lambda s, place: (0, 0)),
        pl.BlockSpec((rows, units), lambda s, place: (0, early(s))),
        pl.BlockSpec((1, 1, units), lambda s, place: (early(s), 0, 0)),
        pl.BlockSpec((rows, part), lambda s, place: (0, late(s))),
    )


def ffn_forward(place, x, up, down, bias, dtype):
    rows, width = x.shape
    owners, blocks, part, units = down.shape
    blocks, early, late, whole, column, thin, out = ffn_specs(rows, down)
    index = lambda s, place: relative_block(early(s), place[0], blocks)
    return call(
        ffn_kernel,
        (blocks + owners,),
        [
            whole,
            pl.BlockSpec((owners, 1, part, units), lambda s, place: (0, jnp.minimum(index(s, place), PAIR - 1), 0, 0)),
            pl.BlockSpec((owners, 1, part, units), lambda s, place: (0, jnp.maximum(index(s, place) - PAIR, 0), 0, 0)),
            pl.BlockSpec((1, blocks, part, units), lambda s, place: (late(s), 0, 0, 0)),
            thin,
        ],
        [out, column, column],
        [shaped((rows, width), dtype), shaped((rows, blocks * units)), shaped((rows, blocks * units))],
        (place, x, *up, down, bias),
        [pltpu.VMEM((blocks, rows, units), BF)],
        name="ffn",
        prefetch=1,
    )


def ffn_back_kernel(place_ref, d_ref, first_ref, one_ref, two_ref, slope_ref, out_ref, dpre_ref, sum_ref, hold_s):
    blocks = hold_s.shape[0]
    step = pl.program_id(0)

    @pl.when(step < blocks)
    def _():
        d_pre = (dot(d_ref[...], first_ref[...].reshape(d_ref.shape[1], -1)) * slope_ref[...].astype(F32)).astype(BF)
        hold_s[step] = d_pre
        dpre_ref[...] = d_pre
        sum_ref[0] = jnp.sum(d_pre.astype(F32), 0, keepdims=True)

    @pl.when(step >= blocks)
    def _():
        left = jnp.concatenate([hold_s[t] for t in range(blocks)], 1)
        order = [relative_block(t, place_ref[0], blocks) for t in range(blocks)]
        weights = [either(one_ref, two_ref, index, lambda ref, i: ref[0, i]) for index in order]
        out_ref[...] = dot(left, jnp.concatenate(weights, 1), ROW_NT).astype(out_ref.dtype)


def ffn_backward(place, d_out, up, down, slope, dtype):
    rows, width = d_out.shape
    owners, blocks, part, units = down.shape
    blocks, early, late, whole, column, thin, out = ffn_specs(rows, down)
    return call(
        ffn_back_kernel,
        (blocks + owners,),
        [
            whole,
            pl.BlockSpec((owners, 1, part, units), lambda s, place: (0, early(s), 0, 0)),
            pl.BlockSpec((1, PAIR, part, units), lambda s, place: (turned_owner(late(s)), 0, 0, 0)),
            pl.BlockSpec((1, PAIR, part, units), lambda s, place: (late(s), 0, 0, 0)),
            column,
        ],
        [out, column, thin],
        [shaped((rows, width), dtype), shaped((rows, blocks * units)), shaped((blocks, 1, units), F32)],
        (place, d_out, down, *up, slope),
        [pltpu.VMEM((blocks, rows, units), BF)],
        name="ffn_backward",
        prefetch=1,
    )


def put_halves(bits_ref, grad, which, keep_ref, send_ref, at):
    grad = grad.reshape((2, 2, grad.shape[0] // 4) + grad.shape[1:])
    pair = (grad[:, 0], grad[:, 1]) if which == 0 else (grad[0], grad[1])
    low = bits_ref[which] == 0
    keep_ref[at] = jnp.where(low, pair[0], pair[1])
    send_ref[at] = jnp.where(low, pair[1], pair[0])


def ffn_grad_kernel(bits_ref, xa_ref, xb_ref, ca_ref, cb_ref, keep_a, send_a, keep_b, send_b, x_s):
    step = pl.program_id(0)

    @pl.when(step == 0)
    def _():
        x_s[...] = jnp.concatenate([xa_ref[...], xb_ref[...]], 0).T

    column = jnp.concatenate([ca_ref[...], cb_ref[...]], 0)
    grad = dot(x_s[...], column).astype(BF)

    @pl.when(step < PAIR)
    def _():
        put_halves(bits_ref, grad, 0, keep_a, send_a, (slice(None), 0))

    @pl.when(step >= PAIR)
    def _():
        put_halves(bits_ref, grad, 1, keep_b, send_b, (slice(None), 0))


def ffn_grad(bits, xa, xb, ca, cb, blocks):
    rows, width = xa.shape
    units = ca.shape[1] // blocks
    whole = pl.BlockSpec((rows, width), lambda t, bits: (0, 0))
    column = pl.BlockSpec((rows, units), lambda t, bits: (0, t))
    first = pl.BlockSpec((2, 1, width // 4, units), lambda t, bits: (0, jnp.minimum(t, PAIR - 1), 0, 0))
    last = pl.BlockSpec((2, 1, width // 4, units), lambda t, bits: (0, jnp.maximum(t - PAIR, 0), 0, 0))
    keep_a, send_a, keep_b, send_b = call(
        ffn_grad_kernel,
        (blocks,),
        [whole, whole, column, column],
        [first, first, last, last],
        [shaped((2, PAIR, width // 4, units))] * 4,
        (bits, xa, xb, ca, cb),
        [pltpu.VMEM((width, 2 * rows), BF)],
        name="ffn_grad",
        prefetch=1,
    )
    return (keep_a, keep_b), (send_a, send_b)


def add_kernel(bits_ref, *refs):
    count = len(refs) // 3
    for i in range(count):
        refs[2 * count + i][...] = (refs[2 * i][0].astype(F32) + refs[2 * i + 1][0].astype(F32)).astype(BF)


def add_middle(bits, keeps, parts):
    _, blocks, rows, units = keeps[0].shape
    args, in_specs = [], []
    for i, pair in enumerate(zip(keeps, parts)):
        args += pair
        in_specs += [pl.BlockSpec((1, 1, rows, units), lambda s, bits, i=i: (1 - bits[1 - i % 2], s, 0, 0))] * 2
    return call(
        add_kernel,
        (blocks,),
        in_specs,
        [pl.BlockSpec((1, rows, units), lambda s, bits: (s, 0, 0))] * len(keeps),
        [shaped((blocks, rows, units))] * len(keeps),
        (bits, *args),
        name="add_middle",
        prefetch=1,
    )


def add_end_kernel(bits_ref, *refs):
    for i in range(len(refs) // 3):
        keep, part, end = refs[3 * i : 3 * i + 3]
        total = keep[0, 0].astype(F32) + part[0, 0].astype(F32) + end[0].astype(F32)
        refs[-1][i % 2, 0, i // 2] = total.astype(BF)


def add_end(bits, keeps, parts, ends):
    _, blocks, rows, units = keeps[0].shape
    args, in_specs = [], []
    for i, triple in enumerate(zip(keeps, parts, ends)):
        args += triple
        in_specs += [pl.BlockSpec((1, 1, rows, units), lambda s, bits, i=i: (bits[1 - i % 2], s, 0, 0))] * 2
        in_specs.append(pl.BlockSpec((1, rows, units), lambda s, bits: (s, 0, 0)))
    count = len(keeps) // 2
    return call(
        add_end_kernel,
        (blocks,),
        in_specs,
        pl.BlockSpec((2, 1, count, rows, units), lambda s, bits: (0, s, 0, 0, 0)),
        shaped((2, blocks, count, rows, units)),
        (bits, *args),
        name="add_end",
        prefetch=1,
    )


def norm_back_block(da_ref, db_ref, x_ref, rest_ref, gain_ref, sum_ref):
    d_value = da_ref[...] + db_ref[...].astype(F32)
    value = x_ref[...].astype(F32)
    centred = value - jnp.mean(value, -1, keepdims=True)
    scale = lax.rsqrt(jnp.mean(centred * centred, -1, keepdims=True) + EPS)
    unit = centred * scale
    d_unit = d_value * gain_ref[...]
    inner = jnp.mean(d_unit * unit, -1, keepdims=True)
    rest = rest_ref[...]
    result = rest + scale * (d_unit - jnp.mean(d_unit, -1, keepdims=True) - unit * inner)
    parts = [d_value * unit, d_value, result, rest]
    sums = jnp.concatenate([jnp.sum(part, 0, keepdims=True) for part in parts] + [jnp.zeros((4, value.shape[1]), F32)], 0)

    @pl.when(pl.program_id(0) == 0)
    def _():
        sum_ref[...] = sums

    @pl.when(pl.program_id(0) > 0)
    def _():
        sum_ref[...] += sums

    return result


def norm_back_kernel(da_ref, db_ref, x_ref, rest_ref, gain_ref, out_ref, low_ref, sum_ref):
    result = norm_back_block(da_ref, db_ref, x_ref, rest_ref, gain_ref, sum_ref)
    out_ref[...] = result
    low_ref[...] = result.astype(BF)


def norm_back_halves_kernel(da_ref, db_ref, x_ref, rest_ref, gain_ref, near_ref, far_ref, sum_ref):
    result = norm_back_block(da_ref, db_ref, x_ref, rest_ref, gain_ref, sum_ref).astype(BF)

    @pl.when(pl.program_id(0) == 0)
    def _():
        near_ref[...] = result

    @pl.when(pl.program_id(0) == 1)
    def _():
        far_ref[...] = result


def norm_backward(da, db, x, rest, gain, halves):
    rows, width = da.shape
    steps = 2 if halves else 1
    row = pl.BlockSpec((rows // steps, width), lambda i: (i, 0))
    whole = lambda count: pl.BlockSpec((count, width), lambda i: (0, 0))
    return call(
        norm_back_halves_kernel if halves else norm_back_kernel,
        (steps,),
        [row] * 4 + [whole(1)],
        [whole(rows // 2)] * 2 + [whole(8)] if halves else [row, row, whole(8)],
        ([shaped((rows // 2, width))] * 2 if halves else [shaped((rows, width), F32), shaped((rows, width))])
        + [shaped((8, width), F32)],
        (da, db, x, rest, gain[None]),
        name="norm_backward",
    )


def swap(value, axis):
    return lax.ppermute(value, axis, [(0, 1), (1, 0)])


def after(value, *others):
    return lax.optimization_barrier((value, *others))[0]


def together(*values):
    return lax.optimization_barrier(values)


def ordered(bit, mine, other, axis):
    return jnp.concatenate([jnp.where(bit == 0, mine, other), jnp.where(bit == 0, other, mine)], axis)


def chosen(value, bit, axis):
    return lax.dynamic_index_in_dim(value, bit, axis, keepdims=False)


def added(mine, other):
    return (mine.astype(F32) + other.astype(F32)).astype(BF)


def moments(value):
    mean = jnp.mean(value, -1, keepdims=True)
    centred = value - mean
    scale = lax.rsqrt(jnp.mean(centred * centred, -1, keepdims=True) + EPS)
    return centred, scale


def clip_local(clips, w_qkv, w_out, w_up, w_down, norm_gain, shifts, bias_qv, up_bias, teacher):
    y, x, c, t = (lax.axis_index(name) for name in ("y", "x", "c", "t"))
    every = ("y", "x", "c", "t")
    steps = 4
    width = clips.shape[2]
    odd = t % 2

    first_way, second_way = [], []
    for column in range(4):
        for core in range(2):
            for place in range(4):
                source = (column * 2 + core) * 4 + place
                to = (column * 2 + place // 2) * 4 + 2 * core
                first_way.append((source, to + place % 2))
                second_way.append((source, to + 1 - place % 2))
    first_way = [(a, b) for a, b in first_way if a != b]
    back = lambda way: [(b, a) for a, b in way]
    stays = t // 2 == c

    def sent(pair):
        return lax.ppermute(pair[0], every, first_way), lax.ppermute(pair[1], every, second_way)

    def to_chip(value):
        return sent((chosen(value, odd, 0), chosen(value, 1 - odd, 0)))

    def sent_back(near, far):
        return lax.ppermute(near, every, back(first_way)), lax.ppermute(far, every, back(second_way))

    def from_chip(value):
        half = value.shape[0] // 2
        return sent_back(value[:half], value[half:])

    rings = [[(i, (i + away) % steps) for i in range(steps)] for away in range(steps)]

    def ring_gather(value):
        return tuple(lax.ppermute(value, "t", rings[-j % steps]) for j in range(1, steps))

    def ring_scatter(blocks):
        return tuple(lax.ppermute(blocks[j], "t", rings[j]) for j in range(1, steps))

    def placed(value, axis):
        return lax.dynamic_slice_in_dim(jnp.concatenate([value, value], axis), steps - t, steps, axis)

    def on_chip(value, near, far):
        return jnp.concatenate([jnp.where(stays, chosen(value, odd, 0), near), far])

    def as_clips(mine, near, far):
        near = jnp.where(stays, mine, near)
        return jnp.stack([jnp.where(odd == 0, near, far), jnp.where(odd == 0, far, near)])

    def scatter_start(sends):
        return swap(sends[0], "x"), swap(sends[1], "y")

    def sums_of(keeps, parts, row, column):
        pick = lambda values, bit: jnp.concatenate([chosen(value, bit, 0) for value in values])
        first = pick(keeps[0], row).astype(F32) + chosen(parts[0], row, 0).astype(F32)
        return first, pick(keeps[1], column).astype(F32) + chosen(parts[1], column, 0).astype(F32)

    def scatter_middle(keeps, parts):
        first, second = sums_of(keeps, parts, 1 - y, 1 - x)
        return swap(first.astype(BF), "y"), swap(second.astype(BF), "x")

    def scatter_end(keeps, parts, ends):
        first, second = sums_of(keeps, parts, y, x)
        return (first + ends[0].astype(F32)).astype(BF), (second + ends[1].astype(F32)).astype(BF)

    dims = w_qkv.shape[1]
    cols = w_out.shape[0] // 2
    lane = bias_qv.shape[1]
    units = w_up.shape[1] // 2
    attn = jnp.concatenate([jnp.swapaxes(w_qkv, 1, 2), w_out[None]]).reshape(4, 2, cols, dims)
    mine, other = chosen(attn, c, 1).reshape(4 * cols, dims), chosen(attn, 1 - c, 1).reshape(4 * cols, dims)
    attn_piece = ordered(c, mine, swap(other, "c"), 1)
    attn_rows = ring_gather(attn_piece)
    attn_rows, w_up, w_down, norm_gain, shifts, bias_qv, up_bias, clips, teacher = together(
        attn_rows, w_up, w_down, norm_gain, shifts, bias_qv, up_bias, clips, teacher
    )
    ff = jnp.stack([w_up, w_down.T]).reshape(2, dims, 2, units)
    ff_piece = ordered(c, chosen(ff, c, 2), swap(chosen(ff, 1 - c, 2), "c"), 1)

    pad = lambda value: jnp.pad(value, (0, dims - value.shape[0]))[None]
    tails = jnp.concatenate([pad(bias_qv[0]), pad(bias_qv[1]), pad(up_bias), jnp.zeros((7, dims), BF)])
    vectors = jnp.concatenate([norm_gain, shifts, tails])
    for bit, name in ((c, "c"), (x, "x"), (y, "y")):
        vectors = ordered(bit, vectors, swap(vectors, name), 1)
    gains, shift_all = vectors[0:2].astype(F32), vectors[2:6].astype(F32)
    tails = vectors[6:16]
    tails = jnp.stack([part[:3] for part in (tails, *ring_gather(tails))]).astype(F32)
    tails = lax.dynamic_slice_in_dim(tails, 4 * dims * c, 4 * dims, 2)
    pair = tails[:, :2].reshape(steps, 2, 4, dims)[..., :lane]
    bias_pair = jnp.swapaxes(pair, 0, 1).reshape(2, 2, 2 * cols)
    bias_in = jnp.stack([bias_pair[0], jnp.zeros_like(bias_pair[0]), bias_pair[1]], 1)[..., None]
    up_shift = placed(tails[:, 2:3], 0)

    whole = ("y", "x", "t")
    near, far = to_chip(clips)
    attn_rows = (attn_piece, *attn_rows)
    qk_rows = jnp.stack([part[: 2 * cols] for part in attn_rows])
    vo_rows = jnp.stack([part[2 * cols :] for part in attn_rows])
    targets = chosen(teacher, odd, 0), chosen(teacher, 1 - odd, 0)
    swapped, near, targets, bias_in, up_shift = together(
        (swap(qk_rows, "y"), swap(vo_rows, "x")), near, targets, bias_in, up_shift
    )
    w_qk, w_vo = ordered(y, qk_rows[None], swapped[0][None], 0), ordered(x, vo_rows[None], swapped[1][None], 0)
    swapped, far = together((swap(w_qk, "x"), swap(w_vo, "y")), far)
    bits = jnp.stack([x, y])
    parts_qk, parts_vo = (w_qk, swapped[0]), (w_vo, swapped[1])
    up_piece, down_piece = ff_piece
    up_piece, down_piece, far = together(up_piece, down_piece, far)
    up_rows = ring_gather(up_piece)
    down_all = lax.all_gather(down_piece, whole, axis=0, tiled=False).reshape(4, steps, 2 * dims, units)
    place = t.reshape(1)

    inputs = on_chip(clips, near, far).astype(F32)
    centred_one, scale_one = moments(inputs)
    first = (centred_one * scale_one * gains[0] + shift_all[0]).astype(BF)
    first_other = swap(first, "c")
    half = first.shape[0] // 2
    qkv, turned = project(bits, first, first_other, parts_qk, parts_vo, bias_in)
    parts_qk, parts_vo, qkv = together(parts_qk, parts_vo, qkv)
    w_qk = ordered(x, parts_qk[0][None], parts_qk[1][None], 0).reshape(4, steps, 2, cols, 2 * dims)
    w_vo = ordered(y, parts_vo[0][None], parts_vo[1][None], 0).reshape(4, steps, 2 * cols, 2 * dims)
    mixed, rows, wide, lse = attend(qkv, 0, 1664)
    up_rows, rows = together(up_rows, rows)
    up_a, up_b = jnp.stack([up_piece, up_rows[0]]), jnp.stack(up_rows[1:])
    swapped = swap(up_a, "y"), swap(up_b, "x")
    mixed, rows, wide, lse = attend(qkv, 1, 1664, (mixed, rows, wide, lse))
    swapped, rows = together(swapped, rows)
    up_a, up_b = ordered(y, up_a[None], swapped[0][None], 0), ordered(x, up_b[None], swapped[1][None], 0)
    swapped = swap(up_a, "x"), swap(up_b, "y")
    attn_other = mix(rows, w_vo, 1, BF)
    attn_mine = mix(after(rows, attn_other), w_vo, 0, F32)
    hidden = inputs + (attn_mine + swap(attn_other, "c").astype(F32)) + shift_all[2]

    centred_two, scale_two = moments(hidden)
    second = (centred_two * scale_two * gains[1] + shift_all[1]).astype(BF)
    second_other = swap(second, "c")
    swapped, second, w_qk = together(swapped, second, w_qk)
    up_a = ordered(x, up_a[None], swapped[0][None], 0).reshape(4, PAIR, 2 * dims, units)
    up_b = ordered(y, up_b[None], swapped[1][None], 0).reshape(4, PAIR, 2 * dims, units)
    up_all = up_a, up_b
    targets, second, down_all = together(targets, second, down_all)
    near, far = sent(targets)
    out_other, act_other, slope_other = ffn_forward(place, second_other, up_all, down_all, up_shift, BF)
    out_other, near = together(out_other, near)
    out_swapped = swap(out_other, "c")
    out_mine, act_mine, slope_mine = ffn_forward(place, after(second, near), up_all, down_all, up_shift, F32)
    out_mine, far, out_swapped = together(out_mine, far, out_swapped)
    output = hidden + (out_mine + out_swapped.astype(F32)) + shift_all[3]
    d_out = output - on_chip(teacher, near, far).astype(F32)
    d_ffn = d_out.astype(BF)
    d_ffn_other = swap(d_ffn, "c")
    d_second, d_pre, sum_mine = ffn_backward(place, d_ffn, up_all, down_all, slope_mine, F32)
    d_ffn_other, d_pre = together(d_ffn_other, d_pre)
    d_second_other, d_pre_other, sum_other = ffn_backward(place, d_ffn_other, up_all, down_all, slope_other, BF)
    d_second_swapped = swap(d_second_other, "c")
    up_sum = (sum_mine + sum_other).reshape(steps, units)

    grad_down, sends = ffn_grad(bits, after(d_ffn, d_pre_other), d_ffn_other, act_mine, act_other, steps)
    down = scatter_start(sends)
    result, grad_down = together(output.astype(BF), grad_down)
    out_near, out_far = from_chip(result)
    d_second_swapped, grad_down = together(d_second_swapped, grad_down)
    d_hidden, d_attn, sums_two = norm_backward(d_second, d_second_swapped, hidden, d_out, gains[1], False)
    d_attn_other = swap(d_attn, "c")
    grad_up, sends = ffn_grad(bits, after(second, d_attn), second_other, d_pre, d_pre_other, steps)
    up = scatter_start(sends)
    d_attn_other, grad_up = together(d_attn_other, grad_up)

    d_heads, delta, grad_o, sends_o = mix_back(bits, d_attn, d_attn_other, w_vo, mixed, wide)
    keeps = (*grad_up, *grad_down)
    back_a, sum_a = attend_backward(qkv, d_heads, lse, delta, 1, 0, 2, 256)
    up, down, out_near, back_a = together(up, down, out_near, back_a)
    ends = add_middle(bits, keeps, (*up, *down))
    ends = [swap(part, name) for part, name in zip(ends, ("y", "x", "y", "x"))]
    back_b, sum_b = attend_backward(qkv, after(d_heads, back_a), lse, delta, 1, 2, 2, 256)
    ends, out_far, back_b = together(ends, out_far, back_b)
    grad_ff = add_end(bits, keeps, (*up, *down), ends).reshape(steps * 4 * dims, units)
    ff_total = lax.psum_scatter(grad_ff, "t", scatter_dimension=0, tiled=True)
    grad_one, sends = project_grads(bits, turned, back_a, back_b)
    one = scatter_start([jnp.concatenate(pair, 1) for pair in zip(sends, sends_o)])
    grad_one = list(zip(grad_one, grad_o))
    delta, grad_ff, grad_one = together(delta, grad_ff, grad_one)
    back_c, sum_c = attend_backward(qkv, after(d_heads, back_b), lse, delta, 0, 0, 4, 256)
    one, back_c = together(one, back_c)
    one_ends = scatter_middle(grad_one, one)
    grad_two, sends = project_grads(bits, turned, back_c)
    two = scatter_start(sends)
    one_ends, grad_two = together(one_ends, grad_two)
    one = [part for part in scatter_end(grad_one, one, one_ends)]
    early = [lax.ppermute(jnp.concatenate([one[p][:3], one[p][4:]]), "t", rings[PAIR + p]) for p in range(PAIR)]
    pieces = (back_c, back_a, back_b)
    d_first_other = project_back(pieces, w_qk, after(w_vo, grad_two), 1)
    d_first_swapped = swap(d_first_other, "c")
    two, d_first_other = together(two, d_first_other)
    two_ends = scatter_middle([[keep] for keep in grad_two], two)
    d_first = project_back(pieces, w_qk, after(w_vo, d_first_other), 0)
    ff_total, d_first = together(ff_total, d_first)
    d_first_swapped, d_first = together(d_first_swapped, d_first)
    *d_inputs, sums_one = norm_backward(d_first, d_first_swapped, inputs, d_hidden, gains[0], True)
    early, sums_one = together(early, sums_one)
    grad_near, grad_far = sent_back(*d_inputs)
    small = (sum_a, sum_b, sum_c, up_sum, sums_one)
    small, d_inputs = together(small, d_inputs)
    two_ends, grad_near, out_near, out_far = together(two_ends, grad_near, out_near, out_far)
    sum_a, sum_b, sum_c, up_sum, sums_one = small
    two = scatter_end([[keep] for keep in grad_two], two, two_ends)
    late = lax.ppermute(jnp.concatenate([two[1], one[1][3:4]]), "t", rings[1])

    grad_ff = ff_total.astype(F32).reshape(2, 2, dims, units)
    grad_ff = ordered(c, chosen(grad_ff, c, 1), swap(chosen(grad_ff, 1 - c, 1), "c"), 2)
    grad_attn = jnp.concatenate([two[0], one[0][3:4]]).astype(F32)
    grad_attn = sum((part.astype(F32) for part in (*early, late)), grad_attn).reshape(4, 2, dims, cols)
    grad_attn = ordered(c, chosen(grad_attn, c, 1), swap(chosen(grad_attn, 1 - c, 1), "c"), 2)

    heads_sum = jnp.concatenate([sum_c, sum_a, sum_b], 2).reshape(3, steps, 4, lane)
    heads_sum = placed(jnp.stack([heads_sum[0], heads_sum[2]]), 1)
    heads_sum = jnp.pad(heads_sum, ((0, 0), (0, 0), (0, 0), (0, dims - lane))).reshape(2 * steps, 4 * dims)
    own = jnp.concatenate([heads_sum, up_sum])
    own = jnp.concatenate([jnp.where(c == 0, own, 0.0), jnp.where(c == 1, own, 0.0)], 1)
    normed = [sums_one[0:1], sums_two[0:1], sums_one[1:2], sums_two[1:4]]
    sums = jnp.concatenate(normed + [jnp.zeros((2, width), F32), own])
    for bit, name in ((y, "y"), (x, "x"), (c, "c")):
        half = sums.shape[1] // 2
        part = lambda which: lax.dynamic_slice_in_dim(sums, which * half, half, 1)
        sums = part(bit) + swap(part(1 - bit), name)
    sums, grad_near = together(sums, grad_near)
    sums = sum((lax.ppermute(sums, "t", rings[away]) for away in range(1, steps)), sums)
    thin = width // 32
    vector_sums = lax.dynamic_slice_in_dim(sums[:6], thin * t, thin, 1)
    place_sums = lax.dynamic_index_in_dim(sums[8:].reshape(3, steps, dims), t, 1, keepdims=False)
    return (
        as_clips(result[: result.shape[0] // 2], out_near, out_far),
        as_clips(d_inputs[0], grad_near, grad_far),
        grad_attn[:3],
        grad_attn[3].T,
        grad_ff[0],
        grad_ff[1].T,
        vector_sums[:2],
        vector_sums[2:],
        place_sums[:2, :lane],
        place_sums[2],
    )


def clip_per_chip(mesh):
    fine = Mesh(mesh.devices.reshape(2, 2, 2, 4), ("y", "x", "c", "t"))
    dp = ("y", "x", "c")
    in_specs = (
        P(dp, "t", None),
        P(None, dp, "t"),
        P("t", dp),
        P(dp, "t"),
        P("t", dp),
        P(None, dp),
        P(None, dp),
        P(None, ("t",) + dp),
        P(("t",) + dp),
        P(dp, "t", None),
    )
    out_specs = in_specs[:1] * 2 + in_specs[1:5] + (
        P(None, dp + ("t",)),
        P(None, dp + ("t",)),
        P(None, ("t",) + dp),
        P(("t",) + dp),
    )
    return jax.shard_map(clip_local, mesh=fine, in_specs=in_specs, out_specs=out_specs, check_vma=False)


def solution(mesh):
    if dict(mesh.shape) == {"dp": 8, "tensor": 4}:
        return clip_per_chip(mesh)
    in_specs = (
        P("dp", "tensor", None),
        P(None, "dp", "tensor"),
        P("tensor", "dp"),
        P("dp", "tensor"),
        P("tensor", "dp"),
        P(None, "dp"),
        P(None, "dp"),
        P(None, ("tensor", "dp")),
        P(("tensor", "dp")),
        P("dp", "tensor", None),
    )
    out_specs = (
        P("dp", "tensor", None),
        P("dp", "tensor", None),
        P(None, "dp", "tensor"),
        P("tensor", "dp"),
        P("dp", "tensor"),
        P("tensor", "dp"),
        P(None, ("dp", "tensor")),
        P(None, ("dp", "tensor")),
        P(None, ("tensor", "dp")),
        P(("tensor", "dp")),
    )
    return jax.shard_map(local, mesh=mesh, in_specs=in_specs, out_specs=out_specs, check_vma=False)
```
